32 devices in a mesh: groups: 2 (over x), expert: 2 (over core), tensor: 8 (over z, y).
Axes of the slice: x: 2, y: 2, z: 4, core: 2. Of those that a mesh axis runs over, the one named last changes fastest.
Arguments:
- tokens: bfloat16 [2048, 6144], P(('groups', 'expert', 'tensor')), parts along dimension 0, may hold values from -6 to 6
- expert_ids: int32 [2048, 2], P(('groups', 'expert', 'tensor')), parts along dimension 0, may hold values from 0 to 7, all different within a row; in each aligned block of 64 rows (0 to 63, 64 to 127, ...) at most 24 rows name the same one
- gate_probs: float32 [2048, 2], P(('groups', 'expert', 'tensor')), parts along dimension 0, may hold values from 0.1 to 1
- w_gate: bfloat16 [2, 6144, 8192], P('expert', None, 'tensor'), may hold values from -0.078125 to 0.078125
- w_up: bfloat16 [2, 6144, 8192], P('expert', None, 'tensor'), may hold values from -0.078125 to 0.078125
- w_down: bfloat16 [2, 8192, 6144], P('expert', 'tensor'), may hold values from -0.0625 to 0.0625
Outputs:
- mixed: bfloat16 [2048, 6144], P(('groups', 'expert', 'tensor')), parts along dimension 0
The draws below stay inside these ranges and needn't reach their ends.
There are 2 independent parts, one for each index of `groups`. The reference program is written for one: setup_inputs(seed, part) draws one part's arguments, and reference() takes and returns one part's arrays. A program takes and returns all parts, laid end to end along the dimension named above; an argument that names none is the same for every part. Nothing has to cross between parts.
Inputs may be any that keep to these rules, and one draw needn't show every extreme that they name: `expert_ids`: in the rows of one device, each expert is named by at most 24 rows; each row names 2 different experts.
All inputs are finite; a program needn't handle non-finite values.
Results may differ from the reference program's by a relative error of at most 0.015.
Values may be sent and summed in bfloat16 or wider, within the bound.
No kernel may reach another device: no remote copies, remote signals or barrier semaphores. Data moves between devices by JAX's collectives and lax.ppermute only.
A program may use at most 128 MiB of HBM per device.

```python
import math
import jax
import jax.numpy as jnp
import numpy as np
from jax import lax

D = 6144
FF = 8192
EXPERTS = 8
TOP = 2
TOK_DEV = 64
CAP = 24
HELD = 2
TOKENS = 1024
N_EXPERT = 2
N_TENSOR = 8


def steps_of(key, extent, split, smallest, high):
    gain = 1.0
    for position, blocks in split:
        draws = jax.random.uniform(jax.random.fold_in(jax.random.fold_in(key, 6), position), (blocks,), jnp.float32, smallest / len(split), high / len(split))
        gain = gain * jnp.repeat(jnp.exp(draws), extent[position] // blocks).reshape((-1,) + (1,) * (len(extent) - 1 - position))
    return gain


def routed_block(rng, own, number, rows, count, top, limit, slope):
    sequence = jax.random.permutation(rng, count)
    crowded, ordinary = portions_of(count, rows * top, limit, slope, True), portions_of(count, rows * top, limit, slope, False)
    places = jnp.arange(count)

    def named(lengths, rotation):
        used = int((lengths > 0).sum())
        fixed = max(1, used // 4)
        moved = fixed + (places - fixed + rotation * (used - fixed)) % max(1, count - fixed)
        return jnp.zeros((count,), jnp.int32).at[sequence[jnp.where(places < fixed, places, moved)]].set(jnp.asarray(lengths, jnp.int32))

    lengths = jnp.where(number % 4 == 0, named(crowded, number // 4), named(ordinary, number - number // 4 - 1))
    mixed = jax.random.permutation(jax.random.fold_in(own, 3), count)
    donor, taker = mixed[0:count // 2 * 2:2], mixed[1:count // 2 * 2:2]
    slack = jnp.minimum(lengths[donor] - 1, limit - lengths[taker]) // 2
    slack = jnp.where((donor == sequence[0]) | (taker == sequence[0]) | (lengths[taker] == 0), 0, jnp.maximum(slack, 0))
    moved = jax.random.randint(jax.random.fold_in(own, 4), (count // 2,), 0, 1 << 20) % (slack + 1)
    lengths = lengths.at[donor].add(-moved).at[taker].add(moved)
    labels = jnp.searchsorted(jnp.cumsum(lengths), jnp.arange(rows * top), side="right").astype(jnp.int32)
    grid = labels.reshape(top, rows).T
    grid = grid[jax.random.permutation(jax.random.fold_in(own, 1), rows)]
    rotation = jax.random.randint(jax.random.fold_in(own, 2), (rows, 1), 0, top)
    return jnp.take_along_axis(grid, (jnp.arange(top)[None, :] + rotation) % top, axis=1)


def portions_of(amount, total, most, skew, full):
    weights = [(1 << 20) // math.isqrt(standing ** skew) + 1 for standing in range(1, amount + 1)]
    largest = most if full else min(most, max(-(-total // amount), total * weights[0] // sum(weights)))
    least = 1 if total - largest >= amount - 1 else 0
    given, spare = [largest] + [least] * (amount - 1), total - largest - least * (amount - 1)
    while spare > 0:
        free = [i for i in range(1, amount) if given[i] < largest] or [i for i in range(1, amount) if given[i] < most]
        pool, remaining = sum([weights[i] for i in free]), spare
        for i in free:
            addition = min(most - given[i], max(1, remaining * weights[i] // pool), spare)
            given[i] = given[i] + addition
            spare = spare - addition
    return np.array(given)


def centred(key, shape, width, most, split=(), held_as=jnp.bfloat16):
    entries = width * jax.random.normal(key, shape, jnp.float32)
    if split:
        entries = entries * steps_of(key, shape, split, -0.22, 0.18)
    return jnp.clip(entries, -most, most).astype(held_as)


def setup_inputs(seed: int = 0, part: int = 0) -> dict:
    streams_of = jax.random.split(jax.random.key(seed), 7)
    own_keys = jax.random.split(jax.random.fold_in(streams_of[6], part), 7)
    tokens = centred(own_keys[0], (TOKENS, D), 1.0, 6.0, ((0, 16),))
    expert_ids_keys = jax.random.split(jax.random.fold_in(own_keys[1], 1), TOKENS // TOK_DEV)
    expert_ids_turns = jax.random.permutation(jax.random.fold_in(own_keys[1], 3), TOKENS // TOK_DEV)
    expert_ids = jax.vmap(lambda own, number: routed_block(jax.random.fold_in(own_keys[1], 2), own, number, TOK_DEV, EXPERTS, TOP, CAP, 2))(expert_ids_keys, expert_ids_turns).reshape((TOKENS, TOP))
    gate_probs = jnp.clip(0.1 + 0.9 * jax.random.uniform(own_keys[2], (TOKENS, TOP), jnp.float32) ** steps_of(own_keys[2], (TOKENS, TOP), ((0, 16),), -0.2, 0.2), 0.1, 1.0)
    w_gate = centred(streams_of[3], (HELD, D, FF), D ** -0.5, 0.078125, ((0, 2), (2, 8)))
    w_up = centred(streams_of[4], (HELD, D, FF), D ** -0.5, 0.078125, ((0, 2), (2, 8)))
    w_down = centred(streams_of[5], (HELD, FF, D), FF ** -0.5, 0.0625, ((0, 2), (1, 8)))
    return {"tokens": tokens, "expert_ids": expert_ids, "gate_probs": gate_probs, "w_gate": w_gate, "w_up": w_up, "w_down": w_down}


def routing(expert_ids, gate_probs, held_count, slots):
    experts = jnp.arange(held_count).astype(jnp.int32)
    matches = expert_ids[:, :, None] == experts[None, None, :]
    member = jnp.any(matches, axis=1).astype(jnp.int32)
    weight = jnp.sum(jnp.where(matches, gate_probs[:, :, None], jnp.float32(0.0)), axis=1)
    slot_index = jnp.cumsum(member, axis=0) - member
    column = jnp.arange(slots).astype(jnp.int32)
    dispatch_map = (member[None, :, :] == 1) & (slot_index[None, :, :] == column[:, None, None])
    return jnp.transpose(dispatch_map, (2, 0, 1)), weight


def reference(tokens, expert_ids, gate_probs, w_gate, w_up, w_down):
    sources = N_EXPERT * N_TENSOR
    blocks = tokens.reshape(sources, TOK_DEV, D)
    chosen = expert_ids.reshape(sources, TOK_DEV, TOP)
    chances = gate_probs.reshape(sources, TOK_DEV, TOP)
    dispatch_map, weight = jax.vmap(lambda ids_block, prob_block: routing(ids_block, prob_block, N_EXPERT, CAP))(chosen, chances)
    buffer = jnp.einsum("swcr,srd->swcd", dispatch_map.astype(jnp.float32), blocks.astype(jnp.float32)).astype(jnp.bfloat16)
    combine = dispatch_map.astype(jnp.float32) * jnp.transpose(weight, (0, 2, 1))[:, :, None, :]
    slice_width = FF // N_TENSOR
    mixed = jnp.zeros((sources, TOK_DEV, D), jnp.float32)
    for expert in range(N_EXPERT):
        row_block = buffer[:, expert].reshape(sources * CAP, D)
        gate_part = jnp.dot(row_block, w_gate[expert], preferred_element_type=jnp.float32)
        up_part = jnp.dot(row_block, w_up[expert], preferred_element_type=jnp.float32)
        hidden = (jax.nn.silu(gate_part) * up_part).astype(jnp.bfloat16)
        down_full = w_down[expert]

        def add_slice(running, slice_index):
            start = (slice_index * slice_width).astype(jnp.int32)
            hidden_cols = lax.dynamic_slice_in_dim(hidden, start, slice_width, 1)
            down_rows = lax.dynamic_slice_in_dim(down_full, start, slice_width, 0)
            partial_value = jnp.dot(hidden_cols, down_rows, preferred_element_type=jnp.float32).astype(jnp.bfloat16)
            partial_value = lax.optimization_barrier(partial_value)
            return running + partial_value.astype(jnp.float32), None

        running, _ = lax.scan(add_slice, jnp.zeros((sources * CAP, D), jnp.float32), jnp.arange(N_TENSOR).astype(jnp.int32))
        expert_out = running.astype(jnp.bfloat16).reshape(sources, CAP, D)
        mixed = mixed + jnp.einsum("scr,scd->srd", combine[:, expert], expert_out.astype(jnp.float32))
    return mixed.reshape(TOKENS, D).astype(jnp.bfloat16)
```

```python
import jax
import jax.numpy as jnp
from jax import lax
from jax.sharding import PartitionSpec as P

CAP = 24
COLUMN_CHUNKS = 2


def ring_of(count):
    return list(range(0, count, 2)) + list(range(count - 1, 0, -2))


def routing(expert_ids, gate_probs, experts, slots):
    matches = expert_ids[:, :, None] == experts[None, None, :]
    member = jnp.any(matches, axis=1).astype(jnp.int32)
    weight = jnp.sum(jnp.where(matches, gate_probs[:, :, None], jnp.float32(0.0)), axis=1)
    slot_index = jnp.cumsum(member, axis=0) - member
    column = jnp.arange(slots)
    dispatch_map = (member[None, :, :] == 1) & (slot_index[None, :, :] == column[:, None, None])
    return (jnp.transpose(dispatch_map, (2, 0, 1)), weight)


def per_device(tokens, expert_ids, gate_probs, w_gate, w_up, w_down):
    n_tensor = lax.axis_size("tensor")
    model_width = tokens.shape[1]
    half = n_tensor // 2
    ring = ring_of(n_tensor)
    right = [(ring[i], ring[(i + 1) % n_tensor]) for i in range(n_tensor)]
    left = [(b, a) for a, b in right]
    swap = [(0, 1), (1, 0)]

    me = lax.axis_index("expert")
    experts = jnp.stack([me, 1 - me])
    dispatch_map, weight = routing(expert_ids, gate_probs, experts, CAP)
    outgoing = jnp.dot(
        dispatch_map.astype(jnp.bfloat16).reshape(2 * CAP, tokens.shape[0]),
        tokens,
        preferred_element_type=jnp.float32,
    ).astype(jnp.bfloat16)
    arrived = lax.ppermute(outgoing[CAP:], "expert", swap)
    own = jnp.concatenate([outgoing[:CAP], arrived], axis=0)

    width = model_width // COLUMN_CHUNKS
    gate_part = 0.0
    up_part = 0.0
    for c in range(COLUMN_CHUNKS):
        cols = slice(c * width, (c + 1) * width)
        block = own[:, cols]
        from_left = [block]
        from_right = [block]
        for _ in range(half - 1):
            from_left.append(lax.ppermute(from_left[-1], "tensor", right))
            from_right.append(lax.ppermute(from_right[-1], "tensor", left))
        far_a = lax.ppermute(from_left[-1][:CAP], "tensor", right)
        far_b = lax.ppermute(from_right[-1][CAP:], "tensor", left)
        rows = jnp.concatenate(from_left + from_right[1:] + [far_a, far_b], axis=0)
        gate_part += jnp.dot(rows, w_gate[0, cols], preferred_element_type=jnp.float32)
        up_part += jnp.dot(rows, w_up[0, cols], preferred_element_type=jnp.float32)
    hidden = (jax.nn.silu(gate_part) * up_part).astype(jnp.bfloat16)

    sums = []
    for c in range(COLUMN_CHUNKS):
        cols = slice(c * width, (c + 1) * width)
        part = jnp.dot(hidden, w_down[0][:, cols], preferred_element_type=jnp.float32).astype(jnp.bfloat16)
        part = part.reshape(n_tensor, 2 * CAP, width)
        to_left = [part[k] for k in range(half)]
        to_right = [part[0]] + [part[half + k] for k in range(half - 1)]
        far = part[n_tensor - 1]
        got_a = lax.ppermute(far[:CAP], "tensor", right)
        got_b = lax.ppermute(far[CAP:], "tensor", left)
        for k in range(half - 1, 0, -1):
            send_a = to_right[k].astype(jnp.float32)
            send_b = to_left[k].astype(jnp.float32)
            if k == half - 1:
                send_a = jnp.concatenate([send_a[:CAP] + got_a.astype(jnp.float32), send_a[CAP:]], axis=0)
                send_b = jnp.concatenate([send_b[:CAP], send_b[CAP:] + got_b.astype(jnp.float32)], axis=0)
            else:
                send_a = send_a + got_a.astype(jnp.float32)
                send_b = send_b + got_b.astype(jnp.float32)
            got_a = lax.ppermute(send_a.astype(jnp.bfloat16), "tensor", right)
            got_b = lax.ppermute(send_b.astype(jnp.bfloat16), "tensor", left)
        sums.append((part[0].astype(jnp.float32) + got_a.astype(jnp.float32) + got_b.astype(jnp.float32)).astype(jnp.bfloat16))
    expert_out = jnp.concatenate(sums, axis=1)
    returned = lax.ppermute(expert_out[CAP:], "expert", swap)
    returned = jnp.stack([expert_out[:CAP], returned])
    combine = dispatch_map.astype(jnp.float32) * jnp.transpose(weight)[:, None, :]
    mixed = jnp.einsum("wcr,wcd->rd", combine, returned.astype(jnp.float32))
    return mixed.astype(jnp.bfloat16)


def solution(mesh):
    in_specs = (
        P(("groups", "expert", "tensor"), None),
        P(("groups", "expert", "tensor"), None),
        P(("groups", "expert", "tensor"), None),
        P("expert", None, "tensor"),
        P("expert", None, "tensor"),
        P("expert", "tensor", None),
    )
    out_specs = P(("groups", "expert", "tensor"), None)
    return jax.shard_map(
        per_device, mesh=mesh, in_specs=in_specs, out_specs=out_specs, check_vma=False
    )
```

```python
import jax
import jax.numpy as jnp
from jax import lax
from jax.sharding import PartitionSpec as P

CAP = 24
GATHER_CHUNKS = 4
SUM_CHUNKS = 2
STREAMS = 2


def ring_of(count):
    return list(range(0, count, 2)) + list(range(count - 1, 0, -2))


def routing(expert_ids, gate_probs, experts, slots):
    matches = expert_ids[:, :, None] == experts[None, None, :]
    member = jnp.any(matches, axis=1).astype(jnp.int32)
    weight = jnp.sum(jnp.where(matches, gate_probs[:, :, None], jnp.float32(0.0)), axis=1)
    slot_index = jnp.cumsum(member, axis=0) - member
    column = jnp.arange(slots)
    dispatch_map = (member[None, :, :] == 1) & (slot_index[None, :, :] == column[:, None, None])
    return (jnp.transpose(dispatch_map, (2, 0, 1)), weight)


def per_device(tokens, expert_ids, gate_probs, w_gate, w_up, w_down):
    n_tensor = lax.axis_size("tensor")
    model_width = tokens.shape[1]
    half = n_tensor // 2
    ring = ring_of(n_tensor)
    right = [(ring[i], ring[(i + 1) % n_tensor]) for i in range(n_tensor)]
    left = [(b, a) for a, b in right]
    swap = [(0, 1), (1, 0)]

    me = lax.axis_index("expert")
    experts = jnp.stack([me, 1 - me])
    dispatch_map, weight = routing(expert_ids, gate_probs, experts, CAP)
    outgoing = jnp.dot(
        dispatch_map.astype(jnp.bfloat16).reshape(2 * CAP, tokens.shape[0]),
        tokens,
        preferred_element_type=jnp.float32,
    ).astype(jnp.bfloat16)
    arrived = lax.ppermute(outgoing[CAP:], "expert", swap)
    own = jnp.concatenate([outgoing[:CAP], arrived], axis=0)

    width = model_width // GATHER_CHUNKS
    gate_part = 0.0
    up_part = 0.0
    last = [None] * STREAMS
    for c in range(GATHER_CHUNKS):
        cols = slice(c * width, (c + 1) * width)
        block = own[:, cols]
        if last[c % STREAMS] is not None:
            block, _ = lax.optimization_barrier((block, last[c % STREAMS]))
        from_left = [block]
        from_right = [block]
        for _ in range(half - 1):
            pair = (
                lax.ppermute(from_left[-1], "tensor", right),
                lax.ppermute(from_right[-1], "tensor", left),
            )
            pair = lax.optimization_barrier(pair)
            from_left.append(pair[0])
            from_right.append(pair[1])
        far = (
            lax.ppermute(from_left[-1][:CAP], "tensor", right),
            lax.ppermute(from_right[-1][CAP:], "tensor", left),
        )
        far = lax.optimization_barrier(far)
        last[c % STREAMS] = far[0]
        rows = jnp.concatenate(from_left + from_right[1:] + list(far), axis=0)
        gate_part += jnp.dot(rows, w_gate[0, cols], preferred_element_type=jnp.float32)
        up_part += jnp.dot(rows, w_up[0, cols], preferred_element_type=jnp.float32)
    hidden = (jax.nn.silu(gate_part) * up_part).astype(jnp.bfloat16)

    width = model_width // SUM_CHUNKS
    sums = []
    for c in range(SUM_CHUNKS):
        cols = slice(c * width, (c + 1) * width)
        part = jnp.dot(hidden, w_down[0][:, cols], preferred_element_type=jnp.float32).astype(jnp.bfloat16)
        part = part.reshape(n_tensor, 2 * CAP, width)
        to_left = [part[k] for k in range(half)]
        to_right = [part[0]] + [part[half + k] for k in range(half - 1)]
        far = part[n_tensor - 1]
        got = (lax.ppermute(far[:CAP], "tensor", right), lax.ppermute(far[CAP:], "tensor", left))
        got_a, got_b = lax.optimization_barrier(got)
        for k in range(half - 1, 0, -1):
            send_a = to_right[k].astype(jnp.float32)
            send_b = to_left[k].astype(jnp.float32)
            if k == half - 1:
                send_a = jnp.concatenate([send_a[:CAP] + got_a.astype(jnp.float32), send_a[CAP:]], axis=0)
                send_b = jnp.concatenate([send_b[:CAP], send_b[CAP:] + got_b.astype(jnp.float32)], axis=0)
            else:
                send_a = send_a + got_a.astype(jnp.float32)
                send_b = send_b + got_b.astype(jnp.float32)
            got = (
                lax.ppermute(send_a.astype(jnp.bfloat16), "tensor", right),
                lax.ppermute(send_b.astype(jnp.bfloat16), "tensor", left),
            )
            got_a, got_b = lax.optimization_barrier(got)
        sums.append((part[0].astype(jnp.float32) + got_a.astype(jnp.float32) + got_b.astype(jnp.float32)).astype(jnp.bfloat16))
    expert_out = jnp.concatenate(sums, axis=1)
    returned = lax.ppermute(expert_out[CAP:], "expert", swap)
    returned = jnp.stack([expert_out[:CAP], returned])
    combine = dispatch_map.astype(jnp.float32) * jnp.transpose(weight)[:, None, :]
    mixed = jnp.einsum("wcr,wcd->rd", combine, returned.astype(jnp.float32))
    return mixed.astype(jnp.bfloat16)


def solution(mesh):
    in_specs = (
        P(("groups", "expert", "tensor"), None),
        P(("groups", "expert", "tensor"), None),
        P(("groups", "expert", "tensor"), None),
        P("expert", None, "tensor"),
        P("expert", None, "tensor"),
        P("expert", "tensor", None),
    )
    out_specs = P(("groups", "expert", "tensor"), None)
    return jax.shard_map(
        per_device, mesh=mesh, in_specs=in_specs, out_specs=out_specs, check_vma=False
    )
```

```python
import jax
import jax.numpy as jnp
from jax import lax
from jax.sharding import PartitionSpec as P

CAP = 24


def ring_of(count):
    return list(range(0, count, 2)) + list(range(count - 1, 0, -2))


def routing(expert_ids, gate_probs, experts, slots):
    matches = expert_ids[:, :, None] == experts[None, None, :]
    member = jnp.any(matches, axis=1).astype(jnp.int32)
    weight = jnp.sum(jnp.where(matches, gate_probs[:, :, None], jnp.float32(0.0)), axis=1)
    slot_index = jnp.cumsum(member, axis=0) - member
    column = jnp.arange(slots)
    dispatch_map = (member[None, :, :] == 1) & (slot_index[None, :, :] == column[:, None, None])
    return (jnp.transpose(dispatch_map, (2, 0, 1)), weight)


def per_device(tokens, expert_ids, gate_probs, w_gate, w_up, w_down):
    n_tensor = lax.axis_size("tensor")
    model_width = tokens.shape[1]
    mid_col = model_width // 2
    half = n_tensor // 2
    ring = ring_of(n_tensor)
    right = [(ring[i], ring[(i + 1) % n_tensor]) for i in range(n_tensor)]
    left = [(b, a) for a, b in right]
    swap = [(0, 1), (1, 0)]

    def step(to_right, to_left):
        pair = (lax.ppermute(to_right, "tensor", right), lax.ppermute(to_left, "tensor", left))
        return lax.optimization_barrier(pair)

    me = lax.axis_index("expert")
    experts = jnp.stack([me, 1 - me])
    dispatch_map, weight = routing(expert_ids, gate_probs, experts, CAP)
    outgoing = jnp.dot(
        dispatch_map.astype(jnp.bfloat16).reshape(2 * CAP, tokens.shape[0]),
        tokens,
        preferred_element_type=jnp.float32,
    ).astype(jnp.bfloat16)
    same, away = outgoing[:CAP], outgoing[CAP:]
    other = lax.ppermute(away, "expert", swap)

    def first(perm):
        across = [(e * n_tensor + a, (1 - e) * n_tensor + b) for e in range(2) for a, b in perm]
        return lax.ppermute(away, ("expert", "tensor"), across)

    blocks = [[same, other]]
    carried = [step(same, same), lax.optimization_barrier((first(right), first(left)))]
    blocks.append([pair[side] for side in range(2) for pair in carried])
    for _ in range(half - 2):
        carried = [step(*pair) for pair in carried]
        blocks.append([pair[side] for side in range(2) for pair in carried])
    far = []
    for from_left, from_right in carried:
        pair = step(from_left[:, :mid_col], from_right[:, mid_col:])
        far.append(jnp.concatenate(pair, axis=1))
    blocks.append(far)

    def hidden_of(rows):
        gate_part = jnp.dot(rows, w_gate[0], preferred_element_type=jnp.float32)
        up_part = jnp.dot(rows, w_up[0], preferred_element_type=jnp.float32)
        return lax.optimization_barrier((jax.nn.silu(gate_part) * up_part).astype(jnp.bfloat16))

    near_hidden = hidden_of(jnp.concatenate(sum(blocks[:half - 1], []), axis=0))
    mid_hidden = hidden_of(jnp.concatenate(blocks[half - 1], axis=0))
    far_hidden = hidden_of(jnp.concatenate(far, axis=0))

    sums = []
    for cols in (slice(0, mid_col), slice(mid_col, model_width)):

        def down_of(hidden):
            part = jnp.dot(hidden, w_down[0, :, cols], preferred_element_type=jnp.float32).astype(jnp.bfloat16)
            return [part[i * 2 * CAP:(i + 1) * 2 * CAP].astype(jnp.float32) for i in range(part.shape[0] // (2 * CAP))]

        far_part = down_of(far_hidden)[0].astype(jnp.bfloat16)
        mid_parts = down_of(mid_hidden)
        own, *near_parts = down_of(near_hidden)
        to_left = near_parts[0::2] + [mid_parts[0]]
        to_right = near_parts[1::2] + [mid_parts[1]]
        got_a, got_b = step(far_part[:CAP], far_part[CAP:])
        for k in range(half - 2, -1, -1):
            got_a, got_b = got_a.astype(jnp.float32), got_b.astype(jnp.float32)
            send_a, send_b = to_right[k], to_left[k]
            if k == half - 2:
                send_a = jnp.concatenate([send_a[:CAP] + got_a, send_a[CAP:]], axis=0)
                send_b = jnp.concatenate([send_b[:CAP], send_b[CAP:] + got_b], axis=0)
            else:
                send_a = send_a + got_a
                send_b = send_b + got_b
            got_a, got_b = step(send_a.astype(jnp.bfloat16), send_b.astype(jnp.bfloat16))
        total = (own + got_a.astype(jnp.float32) + got_b.astype(jnp.float32)).astype(jnp.bfloat16)
        sums.append(jnp.stack([total[:CAP], lax.ppermute(total[CAP:], "expert", swap)]))
    returned = jnp.concatenate(sums, axis=2)
    combine = dispatch_map.astype(jnp.float32) * jnp.transpose(weight)[:, None, :]
    mixed = jnp.einsum("wcr,wcd->rd", combine, returned.astype(jnp.float32))
    return mixed.astype(jnp.bfloat16)


def solution(mesh):
    in_specs = (
        P(("groups", "expert", "tensor"), None),
        P(("groups", "expert", "tensor"), None),
        P(("groups", "expert", "tensor"), None),
        P("expert", None, "tensor"),
        P("expert", None, "tensor"),
        P("expert", "tensor", None),
    )
    out_specs = P(("groups", "expert", "tensor"), None)
    return jax.shard_map(
        per_device, mesh=mesh, in_specs=in_specs, out_specs=out_specs, check_vma=False
    )
```

```python
import jax
import jax.numpy as jnp
from jax import lax
from jax.experimental import pallas as pl
from jax.experimental.pallas import tpu as pltpu
from jax.sharding import PartitionSpec as P

CAP = 24


def ring_of(count):
    return list(range(0, count, 2)) + list(range(count - 1, 0, -2))


def routing(expert_ids, gate_probs, experts, slots):
    matches = expert_ids[:, :, None] == experts[None, None, :]
    member = jnp.any(matches, axis=1).astype(jnp.int32)
    weight = jnp.sum(jnp.where(matches, gate_probs[:, :, None], jnp.float32(0.0)), axis=1)
    slot_index = jnp.cumsum(member, axis=0) - member
    column = jnp.arange(slots)
    dispatch_map = (member[None, :, :] == 1) & (slot_index[None, :, :] == column[:, None, None])
    return (jnp.transpose(dispatch_map, (2, 0, 1)), weight)


CHEAP = pl.CostEstimate(flops=1024, bytes_accessed=1024, transcendentals=0)
PARAMS = pltpu.CompilerParams(dimension_semantics=("arbitrary",), vmem_limit_bytes=12 * 2**20)


def gate_kernel(rows, weights, out):
    part = jnp.dot(rows[...], weights[0], preferred_element_type=jnp.float32)

    @pl.when(pl.program_id(0) == 0)
    def _():
        out[...] = part

    @pl.when(pl.program_id(0) > 0)
    def _():
        out[...] += part


def up_kernel(rows, weights, gate, out, total):
    part = jnp.dot(rows[...], weights[0], preferred_element_type=jnp.float32)

    @pl.when(pl.program_id(0) == 0)
    def _():
        total[...] = part

    @pl.when(pl.program_id(0) > 0)
    def _():
        total[...] += part

    @pl.when(pl.program_id(0) == pl.num_programs(0) - 1)
    def _():
        value = gate[...]
        out[...] = (value / (1.0 + jnp.exp(-value)) * total[...]).astype(out.dtype)


def down_kernel(hidden, weights, out):
    out[...] = jnp.dot(hidden[...], weights[0], preferred_element_type=jnp.float32).astype(out.dtype)


def gate_product(rows, w_gate):
    count, depth = rows.shape
    units = w_gate.shape[2]
    return pl.pallas_call(
        gate_kernel,
        grid=(depth // 512,),
        in_specs=[
            pl.BlockSpec((count, 512), lambda k: (0, k)),
            pl.BlockSpec((1, 512, units), lambda k: (0, k, 0)),
        ],
        out_specs=pl.BlockSpec((count, units), lambda k: (0, 0)),
        out_shape=jax.ShapeDtypeStruct((count, units), jnp.float32),
        cost_estimate=CHEAP,
        compiler_params=PARAMS,
        name="gate_product",
    )(rows, pltpu.with_memory_space_constraint(w_gate, pltpu.HBM))


def up_product(rows, w_up, gate):
    count, depth = rows.shape
    units = w_up.shape[2]
    return pl.pallas_call(
        up_kernel,
        grid=(depth // 512,),
        in_specs=[
            pl.BlockSpec((count, 512), lambda k: (0, k)),
            pl.BlockSpec((1, 512, units), lambda k: (0, k, 0)),
            pl.BlockSpec((count, units), lambda k: (0, 0)),
        ],
        out_specs=pl.BlockSpec((count, units), lambda k: (0, 0)),
        out_shape=jax.ShapeDtypeStruct((count, units), jnp.bfloat16),
        scratch_shapes=[pltpu.VMEM((count, units), jnp.float32)],
        cost_estimate=CHEAP,
        compiler_params=PARAMS,
        name="up_product",
    )(rows, pltpu.with_memory_space_constraint(w_up, pltpu.HBM), gate)


def down_product(hidden, w_down, start, width):
    count, units = hidden.shape
    return pl.pallas_call(
        down_kernel,
        grid=(width // 512,),
        in_specs=[
            pl.BlockSpec((count, units), lambda j: (0, 0)),
            pl.BlockSpec((1, units, 512), lambda j: (0, 0, j + start // 512)),
        ],
        out_specs=pl.BlockSpec((count, 512), lambda j: (0, j)),
        out_shape=jax.ShapeDtypeStruct((count, width), jnp.bfloat16),
        cost_estimate=CHEAP,
        compiler_params=PARAMS,
        name="down_product",
    )(hidden, pltpu.with_memory_space_constraint(w_down, pltpu.HBM))


def per_device(tokens, expert_ids, gate_probs, w_gate, w_up, w_down):
    n_tensor = lax.axis_size("tensor")
    model_width = tokens.shape[1]
    mid_col = model_width // 2
    half = n_tensor // 2
    ring = ring_of(n_tensor)
    right = [(ring[i], ring[(i + 1) % n_tensor]) for i in range(n_tensor)]
    left = [(b, a) for a, b in right]
    swap = [(0, 1), (1, 0)]

    def step(to_right, to_left):
        pair = (lax.ppermute(to_right, "tensor", right), lax.ppermute(to_left, "tensor", left))
        return lax.optimization_barrier(pair)

    me = lax.axis_index("expert")
    experts = jnp.stack([me, 1 - me])
    dispatch_map, weight = routing(expert_ids, gate_probs, experts, CAP)
    outgoing = jnp.dot(
        dispatch_map.astype(jnp.bfloat16).reshape(2 * CAP, tokens.shape[0]),
        tokens,
        preferred_element_type=jnp.float32,
    ).astype(jnp.bfloat16)
    same, away = outgoing[:CAP], outgoing[CAP:]
    other = lax.ppermute(away, "expert", swap)

    def first(perm):
        across = [(e * n_tensor + a, (1 - e) * n_tensor + b) for e in range(2) for a, b in perm]
        return lax.ppermute(away, ("expert", "tensor"), across)

    blocks = [[same, other]]
    carried = [step(same, same), lax.optimization_barrier((first(right), first(left)))]
    blocks.append([pair[side] for side in range(2) for pair in carried])
    for _ in range(half - 3):
        carried = [step(*pair) for pair in carried]
        blocks.append([pair[side] for side in range(2) for pair in carried])

    near = jnp.concatenate(sum(blocks, []), axis=0)
    near_gate = gate_product(near, w_gate)
    held, near_gate = lax.optimization_barrier((carried[1], near_gate))
    carried = [step(*carried[0]), step(*held)]
    blocks.append([pair[side] for side in range(2) for pair in carried])
    near, held = lax.optimization_barrier((near, carried[1]))
    near_hidden = up_product(near, w_up, near_gate)
    far = []
    for from_left, from_right in (carried[0], held):
        pair = step(from_left[:, :mid_col], from_right[:, mid_col:])
        far.append(jnp.concatenate(pair, axis=1))

    rest = jnp.concatenate(blocks[half - 1] + far, axis=0)
    rest, near_hidden = lax.optimization_barrier((rest, near_hidden))
    rest_gate = jnp.dot(rest, w_gate[0], preferred_element_type=jnp.float32)
    rest_up = jnp.dot(rest, w_up[0], preferred_element_type=jnp.float32)
    rest_hidden = lax.optimization_barrier((jax.nn.silu(rest_gate) * rest_up).astype(jnp.bfloat16))

    def block_of(part, index):
        return part[index * 2 * CAP:(index + 1) * 2 * CAP]

    rest_part, near_part, got = [], [], []
    for start in (0, mid_col):
        part = down_product(rest_hidden, w_down, start, mid_col)
        rest_part.append(part)
        far_part = block_of(part, 2)
        got.append(step(far_part[:CAP], far_part[CAP:]))

    def sending(chunk, distance):
        got_a, got_b = (part.astype(jnp.float32) for part in got[chunk])
        if distance == half - 1:
            send_b, send_a = (block_of(rest_part[chunk], side).astype(jnp.float32) for side in range(2))
            send_a = jnp.concatenate([send_a[:CAP] + got_a, send_a[CAP:]], axis=0)
            send_b = jnp.concatenate([send_b[:CAP], send_b[CAP:] + got_b], axis=0)
        else:
            send_b, send_a = (block_of(near_part[chunk], 2 * distance - 1 + side).astype(jnp.float32) for side in range(2))
            send_a = send_a + got_a
            send_b = send_b + got_b
        return send_a.astype(jnp.bfloat16), send_b.astype(jnp.bfloat16)

    def near_down(chunk, after):
        hidden, after = lax.optimization_barrier((near_hidden, after))
        near_part.append(down_product(hidden, w_down, chunk * mid_col, mid_col))
        return after

    got[0] = step(*sending(0, half - 1))
    got[1] = near_down(0, got[1])
    second = sending(1, half - 1)
    second, near_part[0] = lax.optimization_barrier((second, near_part[0]))
    got[1] = step(*second)
    got[0] = near_down(1, got[0])
    for distance in range(half - 2, 0, -1):
        first_pair = sending(0, distance)
        if distance == half - 2:
            first_pair, near_part[1] = lax.optimization_barrier((first_pair, near_part[1]))
        got[0] = step(*first_pair)
        got[1] = step(*sending(1, distance))
    sums = []
    for chunk in range(2):
        got_a, got_b = (part.astype(jnp.float32) for part in got[chunk])
        total = (block_of(near_part[chunk], 0).astype(jnp.float32) + got_a + got_b).astype(jnp.bfloat16)
        sums.append(jnp.stack([total[:CAP], lax.ppermute(total[CAP:], "expert", swap)]))
    returned = jnp.concatenate(sums, axis=2)
    combine = dispatch_map.astype(jnp.float32) * jnp.transpose(weight)[:, None, :]
    mixed = jnp.einsum("wcr,wcd->rd", combine, returned.astype(jnp.float32))
    return mixed.astype(jnp.bfloat16)


def solution(mesh):
    in_specs = (
        P(("groups", "expert", "tensor"), None),
        P(("groups", "expert", "tensor"), None),
        P(("groups", "expert", "tensor"), None),
        P("expert", None, "tensor"),
        P("expert", None, "tensor"),
        P("expert", "tensor", None),
    )
    out_specs = P(("groups", "expert", "tensor"), None)
    return jax.shard_map(
        per_device, mesh=mesh, in_specs=in_specs, out_specs=out_specs, check_vma=False
    )
```

```python
import jax
import jax.numpy as jnp
from jax import lax
from jax.sharding import PartitionSpec as P

CAP = 24


def ring_of(count):
    return list(range(0, count, 2)) + list(range(count - 1, 0, -2))


def routing(expert_ids, gate_probs, experts, slots):
    matches = expert_ids[:, :, None] == experts[None, None, :]
    member = jnp.any(matches, axis=1).astype(jnp.int32)
    weight = jnp.sum(jnp.where(matches, gate_probs[:, :, None], jnp.float32(0.0)), axis=1)
    slot_index = jnp.cumsum(member, axis=0) - member
    column = jnp.arange(slots)
    dispatch_map = (member[None, :, :] == 1) & (slot_index[None, :, :] == column[:, None, None])
    return (jnp.transpose(dispatch_map, (2, 0, 1)), weight)


def product(rows, weights):
    return jnp.dot(rows, weights, preferred_element_type=jnp.float32)


def activated(gate, up):
    return (jax.nn.silu(gate) * up).astype(jnp.bfloat16)


def per_device(tokens, expert_ids, gate_probs, w_gate, w_up, w_down):
    n_tensor = lax.axis_size("tensor")
    model_width = tokens.shape[1]
    mid_col = model_width // 2
    half = n_tensor // 2
    ring = ring_of(n_tensor)
    right = [(ring[i], ring[(i + 1) % n_tensor]) for i in range(n_tensor)]
    left = [(b, a) for a, b in right]
    swap = [(0, 1), (1, 0)]

    def step(to_right, to_left):
        pair = (lax.ppermute(to_right, "tensor", right), lax.ppermute(to_left, "tensor", left))
        return lax.optimization_barrier(pair)

    me = lax.axis_index("expert")
    experts = jnp.stack([me, 1 - me])
    dispatch_map, weight = routing(expert_ids, gate_probs, experts, CAP)
    outgoing = jnp.dot(
        dispatch_map.astype(jnp.bfloat16).reshape(2 * CAP, tokens.shape[0]),
        tokens,
        preferred_element_type=jnp.float32,
    ).astype(jnp.bfloat16)
    same, away = outgoing[:CAP], outgoing[CAP:]
    other = lax.ppermute(away, "expert", swap)

    def first(perm):
        across = [(e * n_tensor + a, (1 - e) * n_tensor + b) for e in range(2) for a, b in perm]
        return lax.ppermute(away, ("expert", "tensor"), across)

    blocks = [[same, other]]
    carried = [step(same, same), lax.optimization_barrier((first(right), first(left)))]
    blocks.append([pair[side] for side in range(2) for pair in carried])
    for _ in range(half - 2):
        carried = [step(*pair) for pair in carried]
        blocks.append([pair[side] for side in range(2) for pair in carried])
    far = []
    for from_left, from_right in carried:
        pair = step(from_left[:, :mid_col], from_right[:, mid_col:])
        far.append(jnp.concatenate(pair, axis=1))

    rows = jnp.concatenate(sum(blocks, []) + far, axis=0)
    hidden = lax.optimization_barrier(activated(product(rows, w_gate[0]), product(rows, w_up[0])))

    def block_of(part, index):
        return part[index * 2 * CAP:(index + 1) * 2 * CAP]

    down, got = [], []
    for start in (0, mid_col):
        part = product(hidden, w_down[0, :, start:start + mid_col]).astype(jnp.bfloat16)
        down.append(part)
        far_part = block_of(part, n_tensor - 1)
        got.append(step(far_part[:CAP], far_part[CAP:]))

    def sending(chunk, distance):
        got_a, got_b = (part.astype(jnp.float32) for part in got[chunk])
        send_b, send_a = (block_of(down[chunk], 2 * distance - 1 + side).astype(jnp.float32) for side in range(2))
        if distance == half - 1:
            send_a = jnp.concatenate([send_a[:CAP] + got_a, send_a[CAP:]], axis=0)
            send_b = jnp.concatenate([send_b[:CAP], send_b[CAP:] + got_b], axis=0)
        else:
            send_a = send_a + got_a
            send_b = send_b + got_b
        return send_a.astype(jnp.bfloat16), send_b.astype(jnp.bfloat16)

    for distance in range(half - 1, 0, -1):
        for chunk in range(2):
            got[chunk] = step(*sending(chunk, distance))
    sums = []
    for chunk in range(2):
        got_a, got_b = (part.astype(jnp.float32) for part in got[chunk])
        total = (block_of(down[chunk], 0).astype(jnp.float32) + got_a + got_b).astype(jnp.bfloat16)
        sums.append(jnp.stack([total[:CAP], lax.ppermute(total[CAP:], "expert", swap)]))
    returned = jnp.concatenate(sums, axis=2)
    combine = dispatch_map.astype(jnp.float32) * jnp.transpose(weight)[:, None, :]
    mixed = jnp.einsum("wcr,wcd->rd", combine, returned.astype(jnp.float32))
    return mixed.astype(jnp.bfloat16)


def solution(mesh):
    in_specs = (
        P(("groups", "expert", "tensor"), None),
        P(("groups", "expert", "tensor"), None),
        P(("groups", "expert", "tensor"), None),
        P("expert", None, "tensor"),
        P("expert", None, "tensor"),
        P("expert", "tensor", None),
    )
    out_specs = P(("groups", "expert", "tensor"), None)
    return jax.shard_map(
        per_device, mesh=mesh, in_specs=in_specs, out_specs=out_specs, check_vma=False
    )
```

```python
import jax
import jax.numpy as jnp
from jax import lax
from jax.experimental import pallas as pl
from jax.experimental.pallas import tpu as pltpu
from jax.sharding import PartitionSpec as P

CAP = 24
COPIES = 16


def ring_of(count):
    return list(range(0, count, 2)) + list(range(count - 1, 0, -2))


def fill_kernel(source, target, done):
    rows = source.shape[1] // COPIES
    copies = [
        pltpu.make_async_copy(
            source.at[:, pl.ds(i * rows, rows)], target.at[:, pl.ds(i * rows, rows)], done.at[i]
        )
        for i in range(COPIES)
    ]
    for copy in copies:
        copy.start()
    for copy in copies:
        copy.wait()


def fetched(weights):
    return pl.pallas_call(
        fill_kernel,
        in_specs=[pl.BlockSpec(memory_space=pltpu.HBM)],
        out_specs=pl.BlockSpec(memory_space=pltpu.VMEM),
        out_shape=pltpu.VMEM(weights.shape, weights.dtype),
        scratch_shapes=[pltpu.SemaphoreType.DMA((COPIES,))],
        cost_estimate=pl.CostEstimate(flops=1024, bytes_accessed=1024, transcendentals=0),
        compiler_params=pltpu.CompilerParams(vmem_limit_bytes=2**20),
        name="fetched",
    )(pltpu.with_memory_space_constraint(weights, pltpu.HBM))


def routing(expert_ids, gate_probs, experts, slots):
    matches = expert_ids[:, :, None] == experts[None, None, :]
    member = jnp.any(matches, axis=1).astype(jnp.int32)
    weight = jnp.sum(jnp.where(matches, gate_probs[:, :, None], jnp.float32(0.0)), axis=1)
    slot_index = jnp.cumsum(member, axis=0) - member
    column = jnp.arange(slots)
    dispatch_map = (member[None, :, :] == 1) & (slot_index[None, :, :] == column[:, None, None])
    return (jnp.transpose(dispatch_map, (2, 0, 1)), weight)


def product(rows, weights):
    return jnp.dot(rows, weights, preferred_element_type=jnp.float32)


def activated(gate, up):
    return (jax.nn.silu(gate) * up).astype(jnp.bfloat16)


def per_device(tokens, expert_ids, gate_probs, w_gate, w_up, w_down):
    n_tensor = lax.axis_size("tensor")
    half = n_tensor // 2
    block_rows = 2 * CAP
    ring = ring_of(n_tensor)
    right = [(ring[i], ring[(i + 1) % n_tensor]) for i in range(n_tensor)]
    left = [(b, a) for a, b in right]
    swap = [(0, 1), (1, 0)]

    def step(to_right, to_left):
        pair = (lax.ppermute(to_right, "tensor", right), lax.ppermute(to_left, "tensor", left))
        return lax.optimization_barrier(pair)

    def before(pair, *others):
        return lax.optimization_barrier((pair, *others))

    me = lax.axis_index("expert")
    experts = jnp.stack([me, 1 - me])
    dispatch_map, weight = routing(expert_ids, gate_probs, experts, CAP)
    outgoing = jnp.dot(
        dispatch_map.astype(jnp.bfloat16).reshape(block_rows, tokens.shape[0]),
        tokens,
        preferred_element_type=jnp.float32,
    ).astype(jnp.bfloat16)
    own = jnp.concatenate([outgoing[:CAP], lax.ppermute(outgoing[CAP:], "expert", swap)], axis=0)

    blocks = [[own]]
    own, w_gate, w_up = before(own, w_gate, w_up)
    pair = step(own, own)
    gate_here, up_here = fetched(w_gate), fetched(w_up)
    pair, gate_here, up_here = before(pair, gate_here, up_here)
    blocks.append(list(pair))
    for distance in range(2, half - 1):
        pair = step(*pair)
        blocks.append(list(pair))
    near = jnp.concatenate(sum(blocks, []), axis=0)
    pair = step(*pair)
    near_hidden = activated(product(near, gate_here[0]), product(near, up_here[0]))
    pair, near_hidden = before(pair, near_hidden)
    far = jnp.concatenate(step(pair[0][:CAP], pair[1][CAP:]), axis=0)
    rest = jnp.concatenate([*pair, far], axis=0)
    rest_hidden = lax.optimization_barrier(activated(product(rest, gate_here[0]), product(rest, up_here[0])))

    def block_of(part, index):
        return part[index * block_rows:(index + 1) * block_rows].astype(jnp.float32)

    rest_part = product(rest_hidden, w_down[0]).astype(jnp.bfloat16)
    far_part = rest_part[2 * block_rows:]
    pair = step(far_part[:CAP], far_part[CAP:])
    got_a, got_b = (part.astype(jnp.float32) for part in pair)
    send_b, send_a = block_of(rest_part, 0), block_of(rest_part, 1)
    send_a = jnp.concatenate([send_a[:CAP] + got_a, send_a[CAP:]], axis=0)
    send_b = jnp.concatenate([send_b[:CAP], send_b[CAP:] + got_b], axis=0)
    near_hidden, send_a, send_b = before(near_hidden, send_a.astype(jnp.bfloat16), send_b.astype(jnp.bfloat16))
    pair = step(send_a, send_b)
    near_part = product(near_hidden, w_down[0]).astype(jnp.bfloat16)
    for distance in range(half - 2, 0, -1):
        got_a, got_b = (part.astype(jnp.float32) for part in pair)
        send_b, send_a = (block_of(near_part, 2 * distance - 1 + side) for side in range(2))
        pair = step((send_a + got_a).astype(jnp.bfloat16), (send_b + got_b).astype(jnp.bfloat16))
    got_a, got_b = (part.astype(jnp.float32) for part in pair)
    total = (block_of(near_part, 0) + got_a + got_b).astype(jnp.bfloat16)

    returned = jnp.stack([total[:CAP], lax.ppermute(total[CAP:], "expert", swap)])
    combine = dispatch_map.astype(jnp.float32) * jnp.transpose(weight)[:, None, :]
    mixed = jnp.einsum("wcr,wcd->rd", combine, returned.astype(jnp.float32))
    return mixed.astype(jnp.bfloat16)


def solution(mesh):
    in_specs = (
        P(("groups", "expert", "tensor"), None),
        P(("groups", "expert", "tensor"), None),
        P(("groups", "expert", "tensor"), None),
        P("expert", None, "tensor"),
        P("expert", None, "tensor"),
        P("expert", "tensor", None),
    )
    out_specs = P(("groups", "expert", "tensor"), None)
    return jax.shard_map(
        per_device, mesh=mesh, in_specs=in_specs, out_specs=out_specs, check_vma=False
    )
```

```python
import jax
import jax.numpy as jnp
from jax import lax
from jax.experimental import pallas as pl
from jax.experimental.pallas import tpu as pltpu
from jax.sharding import PartitionSpec as P

CAP = 24
COPIES = 16


def ring_of(count):
    return list(range(0, count, 2)) + list(range(count - 1, 0, -2))


def fill_kernel(source, target, done):
    rows = source.shape[1] // COPIES
    copies = [
        pltpu.make_async_copy(
            source.at[:, pl.ds(i * rows, rows)], target.at[:, pl.ds(i * rows, rows)], done.at[i]
        )
        for i in range(COPIES)
    ]
    for copy in copies:
        copy.start()
    for copy in copies:
        copy.wait()


def fetched(weights):
    return pl.pallas_call(
        fill_kernel,
        in_specs=[pl.BlockSpec(memory_space=pltpu.HBM)],
        out_specs=pl.BlockSpec(memory_space=pltpu.VMEM),
        out_shape=pltpu.VMEM(weights.shape, weights.dtype),
        scratch_shapes=[pltpu.SemaphoreType.DMA((COPIES,))],
        cost_estimate=pl.CostEstimate(flops=1024, bytes_accessed=1024, transcendentals=0),
        compiler_params=pltpu.CompilerParams(vmem_limit_bytes=2**20),
        name="fetched",
    )(pltpu.with_memory_space_constraint(weights, pltpu.HBM))


def routing(expert_ids, gate_probs, experts, slots):
    matches = expert_ids[:, :, None] == experts[None, None, :]
    member = jnp.any(matches, axis=1).astype(jnp.int32)
    weight = jnp.sum(jnp.where(matches, gate_probs[:, :, None], jnp.float32(0.0)), axis=1)
    slot_index = jnp.cumsum(member, axis=0) - member
    column = jnp.arange(slots)
    dispatch_map = (member[None, :, :] == 1) & (slot_index[None, :, :] == column[:, None, None])
    return (jnp.transpose(dispatch_map, (2, 0, 1)), weight)


def product(rows, weights):
    return jnp.dot(rows, weights, preferred_element_type=jnp.float32)


def activated(gate, up):
    return (jax.nn.silu(gate) * up).astype(jnp.bfloat16)


def per_device(tokens, expert_ids, gate_probs, w_gate, w_up, w_down):
    n_tensor = lax.axis_size("tensor")
    half = n_tensor // 2
    block_rows = 2 * CAP
    mid_col = tokens.shape[1] // 2
    ring = ring_of(n_tensor)
    right = [(ring[i], ring[(i + 1) % n_tensor]) for i in range(n_tensor)]
    left = [(b, a) for a, b in right]
    swap = [(0, 1), (1, 0)]

    def step(to_right, to_left):
        pair = (lax.ppermute(to_right, "tensor", right), lax.ppermute(to_left, "tensor", left))
        return lax.optimization_barrier(pair)

    def before(pair, *others):
        return lax.optimization_barrier((pair, *others))

    me = lax.axis_index("expert")
    experts = jnp.stack([me, 1 - me])
    dispatch_map, weight = routing(expert_ids, gate_probs, experts, CAP)
    outgoing = jnp.dot(
        dispatch_map.astype(jnp.bfloat16).reshape(block_rows, tokens.shape[0]),
        tokens,
        preferred_element_type=jnp.float32,
    ).astype(jnp.bfloat16)
    own = jnp.concatenate([outgoing[:CAP], lax.ppermute(outgoing[CAP:], "expert", swap)], axis=0)

    halves = [own[:, :mid_col], own[:, mid_col:]]
    reached = [[[part] for part in halves]]
    halves, w_gate, w_up = before(halves, w_gate, w_up)
    ends = [[part, part] for part in halves]

    def advance(chunk):
        to_right, to_left = ends[chunk]
        ends[chunk] = [lax.ppermute(to_right, "tensor", right), lax.ppermute(to_left, "tensor", left)]

    def joined(distances):
        return jnp.concatenate(
            [jnp.concatenate([reached[d][chunk][side] for chunk in range(2)], axis=1)
             for d in distances for side in range(len(reached[d][0]))], axis=0)

    advance(0)
    advance(1)
    gate_here, up_here = fetched(w_gate), fetched(w_up)
    ends[1], gate_here, up_here = before(ends[1], gate_here, up_here)
    for _ in range(half - 2):
        reached.append([list(ends[0]), list(ends[1])])
        advance(0)
        advance(1)
    near = joined(range(half - 1))
    near_gate = product(near, gate_here[0])
    ends[0], near_gate = before(ends[0], near_gate)
    near, after = before(near, ends[0])
    near_hidden = activated(near_gate, product(near, up_here[0]))
    ends[0] = list(after)
    ends[1], near_hidden = before(ends[1], near_hidden)
    reached.append([list(ends[0]), list(ends[1])])
    far = []
    for to_right, to_left in ends:
        far.append([lax.ppermute(to_right[:CAP], "tensor", right), lax.ppermute(to_left[CAP:], "tensor", left)])
    far = jnp.concatenate([jnp.concatenate([far[0][side], far[1][side]], axis=1) for side in range(2)], axis=0)
    rest = jnp.concatenate([joined([half - 1]), far], axis=0)
    near_hidden, w_down = before(near_hidden, w_down)
    down_here = fetched(w_down)
    rest, down_here = before(rest, down_here)
    rest_hidden = lax.optimization_barrier(activated(product(rest, gate_here[0]), product(rest, up_here[0])))

    def block_of(part, index):
        return part[index * block_rows:(index + 1) * block_rows]

    def down_of(hidden, chunk):
        return product(hidden, down_here[0, :, chunk * mid_col:(chunk + 1) * mid_col]).astype(jnp.bfloat16)

    rest_part, got = [], []
    for chunk in range(2):
        rest_part.append(down_of(rest_hidden, chunk))
        far_part = block_of(rest_part[chunk], 2)
        got.append(step(far_part[:CAP], far_part[CAP:]))

    def sending(chunk, distance):
        got_a, got_b = (part.astype(jnp.float32) for part in got[chunk])
        if distance == half - 1:
            send_b, send_a = (block_of(rest_part[chunk], side).astype(jnp.float32) for side in range(2))
            send_a = jnp.concatenate([send_a[:CAP] + got_a, send_a[CAP:]], axis=0)
            send_b = jnp.concatenate([send_b[:CAP], send_b[CAP:] + got_b], axis=0)
        else:
            send_b, send_a = (block_of(near_part[chunk], 2 * distance - 1 + side).astype(jnp.float32) for side in range(2))
            send_a = send_a + got_a
            send_b = send_b + got_b
        return send_a.astype(jnp.bfloat16), send_b.astype(jnp.bfloat16)

    near_part = [down_of(near_hidden, chunk) for chunk in range(2)]
    for chunk in range(2):
        got[chunk] = step(*sending(chunk, half - 1))
    for distance in range(half - 2, 0, -1):
        for chunk in range(2):
            got[chunk] = step(*sending(chunk, distance))
    sums = []
    for chunk in range(2):
        got_a, got_b = (part.astype(jnp.float32) for part in got[chunk])
        total = (block_of(near_part[chunk], 0).astype(jnp.float32) + got_a + got_b).astype(jnp.bfloat16)
        sums.append(jnp.stack([total[:CAP], lax.ppermute(total[CAP:], "expert", swap)]))
    returned = jnp.concatenate(sums, axis=2)
    combine = dispatch_map.astype(jnp.float32) * jnp.transpose(weight)[:, None, :]
    mixed = jnp.einsum("wcr,wcd->rd", combine, returned.astype(jnp.float32))
    return mixed.astype(jnp.bfloat16)


def solution(mesh):
    in_specs = (
        P(("groups", "expert", "tensor"), None),
        P(("groups", "expert", "tensor"), None),
        P(("groups", "expert", "tensor"), None),
        P("expert", None, "tensor"),
        P("expert", None, "tensor"),
        P("expert", "tensor", None),
    )
    out_specs = P(("groups", "expert", "tensor"), None)
    return jax.shard_map(
        per_device, mesh=mesh, in_specs=in_specs, out_specs=out_specs, check_vma=False
    )
```

```python
import functools
import jax
import jax.numpy as jnp
from jax import lax
from jax.experimental import pallas as pl
from jax.experimental.pallas import tpu as pltpu
from jax.sharding import PartitionSpec as P

CAP = 24
COPIES = 16
TILE = 512
MARGIN = 3 * 2**20
CHEAP = pl.CostEstimate(flops=1024, bytes_accessed=1024, transcendentals=0)


def ring_of(count):
    return list(range(0, count, 2)) + list(range(count - 1, 0, -2))


def in_vmem(array):
    return pltpu.with_memory_space_constraint(array, pltpu.VMEM)


def in_hbm(array):
    return pltpu.with_memory_space_constraint(array, pltpu.HBM)


def call(kernel, name, operands, outs, scratch, room):
    return pl.pallas_call(
        kernel,
        in_specs=[pl.BlockSpec(memory_space=memory) for _, memory in operands],
        out_specs=[pl.BlockSpec(memory_space=pltpu.VMEM)] * len(outs),
        out_shape=[pltpu.VMEM(*out) for out in outs],
        scratch_shapes=scratch,
        cost_estimate=CHEAP,
        compiler_params=pltpu.CompilerParams(vmem_limit_bytes=room + MARGIN),
        name=name,
    )(*[in_vmem(array) if memory == pltpu.VMEM else in_hbm(array) for array, memory in operands])


def fill_kernel(source, target, done):
    rows = source.shape[1] // COPIES
    copies = [
        pltpu.make_async_copy(
            source.at[:, pl.ds(i * rows, rows)], target.at[:, pl.ds(i * rows, rows)], done.at[i]
        )
        for i in range(COPIES)
    ]
    for copy in copies:
        copy.start()
    for copy in copies:
        copy.wait()


def fetched(weights):
    operands = [(weights, pltpu.HBM)]
    outs = [(weights.shape, weights.dtype)]
    return call(fill_kernel, "fetched", operands, outs, [pltpu.SemaphoreType.DMA((COPIES,))], 0)[0]


def accumulate(chunks, products):
    for _, total in products:
        total[...] = jnp.zeros_like(total)
    for c, blocks in enumerate(chunks):
        width = blocks[0].shape[1]

        @pl.loop(0, width // TILE)
        def _(i):
            at = pl.multiple_of(i * TILE, TILE)
            rows = jnp.concatenate([block[:, pl.ds(at, TILE)] for block in blocks], axis=0)
            for weights, total in products:
                below = weights[0, pl.ds(pl.multiple_of(c * width + at, TILE), TILE), :]
                total[...] += jnp.dot(rows, below, preferred_element_type=jnp.float32)


def activated(gate, up):
    return (gate / (1.0 + jnp.exp(-gate)) * up).astype(jnp.bfloat16)


def gate_kernel(count, *refs):
    chunks, (weights, out) = (refs[:count], refs[count:2 * count]), refs[2 * count:]
    accumulate(chunks, [(weights, out)])


def up_kernel(count, *refs):
    chunks, (weights, gate, out, total) = (refs[:count], refs[count:2 * count]), refs[2 * count:]
    accumulate(chunks, [(weights, total)])
    out[...] = activated(gate[...], total[...])


def down_copies(source, target, done):
    return [
        pltpu.make_async_copy(
            source.at[:, :, pl.ds(i * TILE, TILE)], target.at[:, :, pl.ds(i * TILE, TILE)], done.at[i]
        )
        for i in range(source.shape[2] // TILE)
    ]


def rest_kernel(*refs):
    chunks, (w_gate, w_up, w_down), outs = (refs[:3], refs[3:6]), refs[6:9], refs[9:15]
    gate, up, hidden, down, done = refs[15:]
    copies = down_copies(w_down, down, done)
    for copy in copies:
        copy.start()
    accumulate(chunks, [(w_gate, gate), (w_up, up)])
    hidden[...] = activated(gate[...], up[...])
    size = outs[0].shape[0]
    for i, copy in enumerate(copies):
        copy.wait()
        part = jnp.dot(hidden[...], down[0, :, i * TILE:(i + 1) * TILE], preferred_element_type=jnp.float32)
        chunk, at = divmod(i * TILE, outs[0].shape[1])
        for b in range(3):
            outs[3 * chunk + b][:, at:at + TILE] = part[b * size:(b + 1) * size].astype(jnp.bfloat16)


def near_down_kernel(hidden, w_down, *refs):
    outs, (down, done) = refs[:-2], refs[-2:]
    size, width = outs[0].shape
    count = len(outs) // 2
    copies = down_copies(w_down, down, done)
    for copy in copies:
        copy.start()
    for i, copy in enumerate(copies):
        copy.wait()
        part = jnp.dot(hidden[...], down[0, :, i * TILE:(i + 1) * TILE], preferred_element_type=jnp.float32)
        chunk, at = divmod(i * TILE, width)
        for b in range(count):
            outs[count * chunk + b][:, at:at + TILE] = part[b * size:(b + 1) * size].astype(jnp.bfloat16)


def routing(expert_ids, gate_probs, experts, slots):
    matches = expert_ids[:, :, None] == experts[None, None, :]
    member = jnp.any(matches, axis=1).astype(jnp.int32)
    weight = jnp.sum(jnp.where(matches, gate_probs[:, :, None], jnp.float32(0.0)), axis=1)
    slot_index = jnp.cumsum(member, axis=0) - member
    column = jnp.arange(slots)
    dispatch_map = (member[None, :, :] == 1) & (slot_index[None, :, :] == column[:, None, None])
    return (jnp.transpose(dispatch_map, (2, 0, 1)), weight)


def per_device(tokens, expert_ids, gate_probs, w_gate, w_up, w_down):
    n_tensor = lax.axis_size("tensor")
    half = n_tensor // 2
    size = 2 * CAP
    width = tokens.shape[1]
    mid_col = width // 2
    units = w_gate.shape[2]
    ring = ring_of(n_tensor)
    right = [(ring[i], ring[(i + 1) % n_tensor]) for i in range(n_tensor)]
    left = [(b, a) for a, b in right]
    swap = [(0, 1), (1, 0)]

    def step(to_right, to_left):
        pair = (lax.ppermute(to_right, "tensor", right), lax.ppermute(to_left, "tensor", left))
        return lax.optimization_barrier(pair)

    def tied(*values):
        return lax.optimization_barrier(values)

    me = lax.axis_index("expert")
    experts = jnp.stack([me, 1 - me])
    dispatch_map, weight = routing(expert_ids, gate_probs, experts, CAP)
    outgoing = jnp.dot(
        dispatch_map.astype(jnp.bfloat16).reshape(size, tokens.shape[0]),
        tokens,
        preferred_element_type=jnp.float32,
    ).astype(jnp.bfloat16)
    own = jnp.concatenate([outgoing[:CAP], lax.ppermute(outgoing[CAP:], "expert", swap)], axis=0)

    own, w_gate = tied(own, w_gate)
    halves = [own[:, :mid_col], own[:, mid_col:]]
    blocks = [[halves[0]], [halves[1]]]

    def arrived(a, b):
        blocks[0].extend([a[0], b[1]])
        blocks[1].extend([b[0], a[1]])

    a = step(halves[0], halves[1])
    b = step(halves[1], halves[0])
    gate_here = fetched(w_gate)
    a, gate_here = tied(a, gate_here)
    b, w_up = tied(b, w_up)
    up_here = fetched(w_up)
    b, up_here = tied(b, up_here)
    arrived(a, b)
    for _ in range(half - 3):
        a = step(*a)
        b = step(*b)
        arrived(a, b)
    near = [(block, pltpu.VMEM) for chunk in blocks for block in chunk]
    count = len(blocks[0])
    rows = count * size
    product = ((rows, units), jnp.float32)
    near_gate, = call(
        functools.partial(gate_kernel, count), "near_gate", near + [(gate_here, pltpu.VMEM)], [product], [],
        rows * units * 8,
    )
    b, near_gate = tied(b, near_gate)
    a = step(*a)
    b = step(*b)
    rest = [[a[0], b[1]], [b[0], a[1]]]
    a, near_gate = tied(a, near_gate)
    far = step(*a)
    near_hidden, = call(
        functools.partial(up_kernel, count), "near_up",
        near + [(up_here, pltpu.VMEM), (near_gate, pltpu.VMEM)], [((rows, units), jnp.bfloat16)],
        [pltpu.VMEM((rows, units), jnp.float32)], rows * units * 16,
    )
    rest = [rest[chunk] + [far[chunk]] for chunk in range(2)]
    rest, near_hidden = tied(rest, near_hidden)
    down_scratch = [pltpu.VMEM(w_down.shape, jnp.bfloat16), pltpu.SemaphoreType.DMA((width // TILE,))]
    down_room = units * width * 2
    rest_parts = call(
        rest_kernel, "rest",
        [(block, pltpu.VMEM) for chunk in rest for block in chunk]
        + [(gate_here, pltpu.VMEM), (up_here, pltpu.VMEM), (w_down, pltpu.HBM)],
        [((size, mid_col), jnp.bfloat16)] * 6,
        [pltpu.VMEM((3 * size, units), jnp.float32)] * 2 + [pltpu.VMEM((3 * size, units), jnp.bfloat16)] + down_scratch,
        down_room + 3 * size * units * 24,
    )
    near_parts = call(
        near_down_kernel, "near_down", [(near_hidden, pltpu.VMEM), (w_down, pltpu.HBM)],
        [((size, mid_col), jnp.bfloat16)] * (2 * count), down_scratch, down_room + rows * TILE * 8,
    )

    def part_of(chunk, distance, side):
        if distance == half - 1:
            return rest_parts[3 * chunk + side].astype(jnp.float32)
        index = 2 * distance - 1 + side if distance else 0
        return near_parts[count * chunk + index].astype(jnp.float32)

    def sent(stream, distance, got):
        to_right = part_of(stream, distance, 1) + got[0].astype(jnp.float32)
        to_left = part_of(1 - stream, distance, 0) + got[1].astype(jnp.float32)
        return step(to_right.astype(jnp.bfloat16), to_left.astype(jnp.bfloat16))

    a = step(rest_parts[2], rest_parts[5])
    b = step(rest_parts[4], rest_parts[0])
    a = sent(0, half - 1, a)
    for distance in range(half - 2, 0, -1):
        b = sent(1, distance, b)
        a = sent(0, distance, a)
    totals = [
        part_of(0, 0, 0) + a[0].astype(jnp.float32) + b[1].astype(jnp.float32),
        part_of(1, 0, 0) + b[0].astype(jnp.float32) + a[1].astype(jnp.float32),
    ]
    total = jnp.concatenate(totals, axis=1).astype(jnp.bfloat16)
    returned = jnp.stack([total[:CAP], lax.ppermute(total[CAP:], "expert", swap)])
    combine = dispatch_map.astype(jnp.float32) * jnp.transpose(weight)[:, None, :]
    mixed = jnp.einsum("wcr,wcd->rd", combine, returned.astype(jnp.float32))
    return mixed.astype(jnp.bfloat16)


def solution(mesh):
    in_specs = (
        P(("groups", "expert", "tensor"), None),
        P(("groups", "expert", "tensor"), None),
        P(("groups", "expert", "tensor"), None),
        P("expert", None, "tensor"),
        P("expert", None, "tensor"),
        P("expert", "tensor", None),
    )
    out_specs = P(("groups", "expert", "tensor"), None)
    return jax.shard_map(
        per_device, mesh=mesh, in_specs=in_specs, out_specs=out_specs, check_vma=False
    )
```

```python
import functools
import jax
import jax.numpy as jnp
from jax import lax
from jax.experimental import pallas as pl
from jax.experimental.pallas import tpu as pltpu
from jax.sharding import PartitionSpec as P

CAP = 24
COPIES = 16
TILE = 512
MARGIN = 3 * 2**20
CHEAP = pl.CostEstimate(flops=1024, bytes_accessed=1024, transcendentals=0)


def ring_of(count):
    return list(range(0, count, 2)) + list(range(count - 1, 0, -2))


def in_vmem(array):
    return pltpu.with_memory_space_constraint(array, pltpu.VMEM)


def in_hbm(array):
    return pltpu.with_memory_space_constraint(array, pltpu.HBM)


def call(kernel, name, operands, outs, scratch, room):
    return pl.pallas_call(
        kernel,
        in_specs=[pl.BlockSpec(memory_space=memory) for _, memory in operands],
        out_specs=[pl.BlockSpec(memory_space=pltpu.VMEM)] * len(outs),
        out_shape=[pltpu.VMEM(*out) for out in outs],
        scratch_shapes=scratch,
        cost_estimate=CHEAP,
        compiler_params=pltpu.CompilerParams(vmem_limit_bytes=room + MARGIN),
        name=name,
    )(*[in_vmem(array) if memory == pltpu.VMEM else in_hbm(array) for array, memory in operands])


def fill_kernel(source, target, done):
    rows = source.shape[1] // COPIES
    copies = [
        pltpu.make_async_copy(
            source.at[:, pl.ds(i * rows, rows)], target.at[:, pl.ds(i * rows, rows)], done.at[i]
        )
        for i in range(COPIES)
    ]
    for copy in copies:
        copy.start()
    for copy in copies:
        copy.wait()


def fetched(weights):
    operands = [(weights, pltpu.HBM)]
    outs = [(weights.shape, weights.dtype)]
    return call(fill_kernel, "fetched", operands, outs, [pltpu.SemaphoreType.DMA((COPIES,))], 0)[0]


def accumulate(chunks, products):
    size, width = chunks[0][0].shape
    depth = width if size * len(chunks[0]) <= 512 else TILE
    for c, blocks in enumerate(chunks):
        for at in range(0, width, depth):
            rows = jnp.concatenate([block[:, at:at + depth] for block in blocks], axis=0)
            above = c * width + at
            for weights, total in products:
                part = jnp.dot(rows, weights[0, above:above + depth, :], preferred_element_type=jnp.float32)
                total[...] = total[...] + part if above else part


def activated(gate, up):
    return (gate / (1.0 + jnp.exp(-gate)) * up).astype(jnp.bfloat16)


def gate_kernel(count, *refs):
    chunks, (weights, out) = (refs[:count], refs[count:2 * count]), refs[2 * count:]
    accumulate(chunks, [(weights, out)])


def up_kernel(count, *refs):
    chunks, (weights, gate, out, total) = (refs[:count], refs[count:2 * count]), refs[2 * count:]
    accumulate(chunks, [(weights, total)])
    out[...] = activated(gate[...], total[...])


def down_copies(source, target, done):
    return [
        pltpu.make_async_copy(
            source.at[:, :, pl.ds(i * TILE, TILE)], target.at[:, :, pl.ds(i * TILE, TILE)], done.at[i]
        )
        for i in range(source.shape[2] // TILE)
    ]


def rest_kernel(*refs):
    chunks, (w_gate, w_up, w_down), outs = (refs[:3], refs[3:6]), refs[6:9], refs[9:15]
    gate, up, hidden, down, done = refs[15:]
    copies = down_copies(w_down, down, done)
    for copy in copies:
        copy.start()
    accumulate(chunks, [(w_gate, gate), (w_up, up)])
    hidden[...] = activated(gate[...], up[...])
    size = outs[0].shape[0]
    for i, copy in enumerate(copies):
        copy.wait()
        part = jnp.dot(hidden[...], down[0, :, i * TILE:(i + 1) * TILE], preferred_element_type=jnp.float32)
        chunk, at = divmod(i * TILE, outs[0].shape[1])
        for b in range(3):
            outs[3 * chunk + b][:, at:at + TILE] = part[b * size:(b + 1) * size].astype(jnp.bfloat16)


def near_down_kernel(hidden, w_down, *refs):
    outs, (down, done) = refs[:-2], refs[-2:]
    size, width = outs[0].shape
    count = len(outs) // 2
    copies = down_copies(w_down, down, done)
    for copy in copies:
        copy.start()
    for i, copy in enumerate(copies):
        copy.wait()
        part = jnp.dot(hidden[...], down[0, :, i * TILE:(i + 1) * TILE], preferred_element_type=jnp.float32)
        chunk, at = divmod(i * TILE, width)
        for b in range(count):
            outs[count * chunk + b][:, at:at + TILE] = part[b * size:(b + 1) * size].astype(jnp.bfloat16)


def routing(expert_ids, gate_probs, experts, slots):
    matches = expert_ids[:, :, None] == experts[None, None, :]
    member = jnp.any(matches, axis=1).astype(jnp.int32)
    weight = jnp.sum(jnp.where(matches, gate_probs[:, :, None], jnp.float32(0.0)), axis=1)
    slot_index = jnp.cumsum(member, axis=0) - member
    column = jnp.arange(slots)
    dispatch_map = (member[None, :, :] == 1) & (slot_index[None, :, :] == column[:, None, None])
    return (jnp.transpose(dispatch_map, (2, 0, 1)), weight)


def per_device(tokens, expert_ids, gate_probs, w_gate, w_up, w_down):
    n_tensor = lax.axis_size("tensor")
    half = n_tensor // 2
    size = 2 * CAP
    width = tokens.shape[1]
    mid_col = width // 2
    units = w_gate.shape[2]
    ring = ring_of(n_tensor)
    right = [(ring[i], ring[(i + 1) % n_tensor]) for i in range(n_tensor)]
    left = [(b, a) for a, b in right]
    swap = [(0, 1), (1, 0)]

    def step(to_right, to_left):
        pair = (lax.ppermute(to_right, "tensor", right), lax.ppermute(to_left, "tensor", left))
        return lax.optimization_barrier(pair)

    def tied(*values):
        return lax.optimization_barrier(values)

    me = lax.axis_index("expert")
    experts = jnp.stack([me, 1 - me])
    dispatch_map, weight = routing(expert_ids, gate_probs, experts, CAP)
    outgoing = jnp.dot(
        dispatch_map.astype(jnp.bfloat16).reshape(size, tokens.shape[0]),
        tokens,
        preferred_element_type=jnp.float32,
    ).astype(jnp.bfloat16)
    own = jnp.concatenate([outgoing[:CAP], lax.ppermute(outgoing[CAP:], "expert", swap)], axis=0)

    own, w_gate = tied(own, w_gate)
    halves = [own[:, :mid_col], own[:, mid_col:]]
    blocks = [[halves[0]], [halves[1]]]

    def arrived(a, b):
        blocks[0].extend([a[0], b[1]])
        blocks[1].extend([b[0], a[1]])

    a = step(halves[0], halves[1])
    b = step(halves[1], halves[0])
    gate_here = fetched(w_gate)
    a, gate_here = tied(a, gate_here)
    a, w_up = tied(a, w_up)
    up_here = fetched(w_up)
    b, up_here = tied(b, up_here)
    arrived(a, b)
    for _ in range(half - 3):
        a = step(*a)
        b = step(*b)
        arrived(a, b)
    near = [(block, pltpu.VMEM) for chunk in blocks for block in chunk]
    count = len(blocks[0])
    rows = count * size
    product = ((rows, units), jnp.float32)
    near_gate, = call(
        functools.partial(gate_kernel, count), "near_gate", near + [(gate_here, pltpu.VMEM)], [product], [],
        rows * units * 8,
    )
    b, near_gate = tied(b, near_gate)
    a = step(*a)
    b = step(*b)
    rest = [[a[0], b[1]], [b[0], a[1]]]
    a, near_gate = tied(a, near_gate)
    far = step(*a)
    near_hidden, = call(
        functools.partial(up_kernel, count), "near_up",
        near + [(up_here, pltpu.VMEM), (near_gate, pltpu.VMEM)], [((rows, units), jnp.bfloat16)],
        [pltpu.VMEM((rows, units), jnp.float32)], rows * units * 16,
    )
    rest = [rest[chunk] + [far[chunk]] for chunk in range(2)]
    rest, near_hidden = tied(rest, near_hidden)
    down_scratch = [pltpu.VMEM(w_down.shape, jnp.bfloat16), pltpu.SemaphoreType.DMA((width // TILE,))]
    down_room = units * width * 2
    rest_parts = call(
        rest_kernel, "rest",
        [(block, pltpu.VMEM) for chunk in rest for block in chunk]
        + [(gate_here, pltpu.VMEM), (up_here, pltpu.VMEM), (w_down, pltpu.HBM)],
        [((size, mid_col), jnp.bfloat16)] * 6,
        [pltpu.VMEM((3 * size, units), jnp.float32)] * 2 + [pltpu.VMEM((3 * size, units), jnp.bfloat16)] + down_scratch,
        down_room + 3 * size * units * 24,
    )
    near_parts = call(
        near_down_kernel, "near_down", [(near_hidden, pltpu.VMEM), (w_down, pltpu.HBM)],
        [((size, mid_col), jnp.bfloat16)] * (2 * count), down_scratch, down_room + rows * TILE * 8,
    )

    def part_of(chunk, distance, side):
        if distance == half - 1:
            return rest_parts[3 * chunk + side].astype(jnp.float32)
        index = 2 * distance - 1 + side if distance else 0
        return near_parts[count * chunk + index].astype(jnp.float32)

    def sent(stream, distance, got):
        to_right = part_of(stream, distance, 1) + got[0].astype(jnp.float32)
        to_left = part_of(1 - stream, distance, 0) + got[1].astype(jnp.float32)
        return step(to_right.astype(jnp.bfloat16), to_left.astype(jnp.bfloat16))

    a = step(rest_parts[2], rest_parts[5])
    b = step(rest_parts[4], rest_parts[0])
    a = sent(0, half - 1, a)
    for distance in range(half - 2, 0, -1):
        b = sent(1, distance, b)
        a = sent(0, distance, a)
    totals = [
        part_of(0, 0, 0) + a[0].astype(jnp.float32) + b[1].astype(jnp.float32),
        part_of(1, 0, 0) + b[0].astype(jnp.float32) + a[1].astype(jnp.float32),
    ]
    total = jnp.concatenate(totals, axis=1).astype(jnp.bfloat16)
    returned = jnp.stack([total[:CAP], lax.ppermute(total[CAP:], "expert", swap)])
    combine = dispatch_map.astype(jnp.float32) * jnp.transpose(weight)[:, None, :]
    mixed = jnp.einsum("wcr,wcd->rd", combine, returned.astype(jnp.float32))
    return mixed.astype(jnp.bfloat16)


def solution(mesh):
    in_specs = (
        P(("groups", "expert", "tensor"), None),
        P(("groups", "expert", "tensor"), None),
        P(("groups", "expert", "tensor"), None),
        P("expert", None, "tensor"),
        P("expert", None, "tensor"),
        P("expert", "tensor", None),
    )
    out_specs = P(("groups", "expert", "tensor"), None)
    return jax.shard_map(
        per_device, mesh=mesh, in_specs=in_specs, out_specs=out_specs, check_vma=False
    )
```

```python
import functools
import jax
import jax.numpy as jnp
from jax import lax
from jax.experimental import pallas as pl
from jax.experimental.pallas import tpu as pltpu
from jax.sharding import PartitionSpec as P

CAP = 24
COPIES = 16
TILE = 512
MARGIN = 3 * 2**20
CHEAP = pl.CostEstimate(flops=1024, bytes_accessed=1024, transcendentals=0)


def ring_of(count):
    return list(range(0, count, 2)) + list(range(count - 1, 0, -2))


def in_vmem(array):
    return pltpu.with_memory_space_constraint(array, pltpu.VMEM)


def in_hbm(array):
    return pltpu.with_memory_space_constraint(array, pltpu.HBM)


def call(kernel, name, operands, outs, scratch, room):
    return pl.pallas_call(
        kernel,
        in_specs=[pl.BlockSpec(memory_space=memory) for _, memory in operands],
        out_specs=[pl.BlockSpec(memory_space=pltpu.VMEM)] * len(outs),
        out_shape=[pltpu.VMEM(*out) for out in outs],
        scratch_shapes=scratch,
        cost_estimate=CHEAP,
        compiler_params=pltpu.CompilerParams(vmem_limit_bytes=room + MARGIN),
        name=name,
    )(*[in_vmem(array) if memory == pltpu.VMEM else in_hbm(array) for array, memory in operands])


def row_copies(source, target, done):
    rows = source.shape[1] // COPIES
    return [
        pltpu.make_async_copy(
            source.at[:, pl.ds(i * rows, rows)], target.at[:, pl.ds(i * rows, rows)], done.at[i]
        )
        for i in range(COPIES)
    ]


def fill_kernel(source, target, done):
    copies = row_copies(source, target, done)
    for copy in copies:
        copy.start()
    for copy in copies:
        copy.wait()


def fetched(weights):
    operands = [(weights, pltpu.HBM)]
    outs = [(weights.shape, weights.dtype)]
    return call(fill_kernel, "fetched", operands, outs, [pltpu.SemaphoreType.DMA((COPIES,))], 0)[0]


def accumulate(chunks, products):
    size, width = chunks[0][0].shape
    depth = width if size * len(chunks[0]) <= 512 else TILE
    for c, blocks in enumerate(chunks):
        for at in range(0, width, depth):
            rows = jnp.concatenate([block[:, at:at + depth] for block in blocks], axis=0)
            above = c * width + at
            for weights, total in products:
                part = jnp.dot(rows, weights[0, above:above + depth, :], preferred_element_type=jnp.float32)
                total[...] = total[...] + part if above else part


def activated(gate, up):
    return (gate / (1.0 + jnp.exp(-gate)) * up).astype(jnp.bfloat16)


def gate_kernel(count, *refs):
    chunks, (weights, out) = (refs[:count], refs[count:2 * count]), refs[2 * count:]
    accumulate(chunks, [(weights, out)])


def add_down(hidden, down, outs):
    size, width = outs[0].shape
    count = len(outs) // 2
    for at in range(0, down.shape[2], TILE):
        part = jnp.dot(hidden, down[0, :, at:at + TILE], preferred_element_type=jnp.float32).astype(jnp.bfloat16)
        chunk, column = divmod(at, width)
        for b in range(count):
            outs[count * chunk + b][:, column:column + TILE] = part[b * size:(b + 1) * size]


def near_kernel(count, *refs):
    chunks, (w_up, gate, w_down) = (refs[:count], refs[count:2 * count]), refs[2 * count:2 * count + 3]
    outs, (up, down, done) = refs[2 * count + 3:4 * count + 3], refs[4 * count + 3:]
    copies = row_copies(w_down, down, done)
    for copy in copies:
        copy.start()
    accumulate(chunks, [(w_up, up)])
    hidden = activated(gate[...], up[...])
    for copy in copies:
        copy.wait()
    add_down(hidden, down, outs)


def rest_kernel(*refs):
    chunks, (w_gate, w_up, w_down), outs = (refs[:3], refs[3:6]), refs[6:9], refs[9:15]
    gate, up, down, done = refs[15:]
    copies = row_copies(w_down, down, done)
    for copy in copies:
        copy.start()
    accumulate(chunks, [(w_gate, gate), (w_up, up)])
    hidden = activated(gate[...], up[...])
    for copy in copies:
        copy.wait()
    add_down(hidden, down, outs)


def routing(expert_ids, gate_probs, experts, slots):
    matches = expert_ids[:, :, None] == experts[None, None, :]
    member = jnp.any(matches, axis=1).astype(jnp.int32)
    weight = jnp.sum(jnp.where(matches, gate_probs[:, :, None], jnp.float32(0.0)), axis=1)
    slot_index = jnp.cumsum(member, axis=0) - member
    column = jnp.arange(slots)
    dispatch_map = (member[None, :, :] == 1) & (slot_index[None, :, :] == column[:, None, None])
    return (jnp.transpose(dispatch_map, (2, 0, 1)), weight)


def per_device(tokens, expert_ids, gate_probs, w_gate, w_up, w_down):
    n_tensor = lax.axis_size("tensor")
    half = n_tensor // 2
    size = 2 * CAP
    width = tokens.shape[1]
    mid_col = width // 2
    units = w_gate.shape[2]
    ring = ring_of(n_tensor)
    right = [(ring[i], ring[(i + 1) % n_tensor]) for i in range(n_tensor)]
    left = [(b, a) for a, b in right]
    swap = [(0, 1), (1, 0)]

    def step(to_right, to_left):
        pair = (lax.ppermute(to_right, "tensor", right), lax.ppermute(to_left, "tensor", left))
        return lax.optimization_barrier(pair)

    def tied(*values):
        return lax.optimization_barrier(values)

    me = lax.axis_index("expert")
    experts = jnp.stack([me, 1 - me])
    dispatch_map, weight = routing(expert_ids, gate_probs, experts, CAP)
    outgoing = jnp.dot(
        dispatch_map.astype(jnp.bfloat16).reshape(size, tokens.shape[0]),
        tokens,
        preferred_element_type=jnp.float32,
    ).astype(jnp.bfloat16)
    own = jnp.concatenate([outgoing[:CAP], lax.ppermute(outgoing[CAP:], "expert", swap)], axis=0)

    own, w_gate = tied(own, w_gate)
    halves = [own[:, :mid_col], own[:, mid_col:]]
    blocks = [[halves[0]], [halves[1]]]

    def arrived(a, b):
        blocks[0].extend([a[0], b[1]])
        blocks[1].extend([b[0], a[1]])

    a = step(halves[0], halves[1])
    b = step(halves[1], halves[0])
    gate_here = fetched(w_gate)
    a, gate_here = tied(a, gate_here)
    a, w_up = tied(a, w_up)
    up_here = fetched(w_up)
    b, up_here = tied(b, up_here)
    arrived(a, b)
    for _ in range(half - 3):
        a = step(*a)
        b = step(*b)
        arrived(a, b)
    near = [(block, pltpu.VMEM) for chunk in blocks for block in chunk]
    count = len(blocks[0])
    rows = count * size
    product = ((rows, units), jnp.float32)
    near_gate, = call(
        functools.partial(gate_kernel, count), "near_gate", near + [(gate_here, pltpu.VMEM)], [product], [],
        rows * units * 8,
    )
    b, near_gate = tied(b, near_gate)
    a = step(*a)
    b = step(*b)
    rest = [[a[0], b[1]], [b[0], a[1]]]
    a, near_gate = tied(a, near_gate)
    far = step(*a)
    down_scratch = [pltpu.VMEM(w_down.shape, jnp.bfloat16), pltpu.SemaphoreType.DMA((COPIES,))]
    down_room = units * width * 2
    near_parts = call(
        functools.partial(near_kernel, count), "near_parts",
        near + [(up_here, pltpu.VMEM), (near_gate, pltpu.VMEM), (w_down, pltpu.HBM)],
        [((size, mid_col), jnp.bfloat16)] * (2 * count), [pltpu.VMEM((rows, units), jnp.float32)] + down_scratch,
        down_room + rows * units * 16,
    )
    rest = [rest[chunk] + [far[chunk]] for chunk in range(2)]
    rest, near_parts = tied(rest, near_parts)
    rest_parts = call(
        rest_kernel, "rest",
        [(block, pltpu.VMEM) for chunk in rest for block in chunk]
        + [(gate_here, pltpu.VMEM), (up_here, pltpu.VMEM), (w_down, pltpu.HBM)],
        [((size, mid_col), jnp.bfloat16)] * 6,
        [pltpu.VMEM((3 * size, units), jnp.float32)] * 2 + down_scratch,
        down_room + 3 * size * units * 16,
    )

    def part_of(chunk, distance, side):
        if distance == half - 1:
            return rest_parts[3 * chunk + side].astype(jnp.float32)
        index = 2 * distance - 1 + side if distance else 0
        return near_parts[count * chunk + index].astype(jnp.float32)

    def sent(stream, distance, got):
        to_right = part_of(stream, distance, 1) + got[0].astype(jnp.float32)
        to_left = part_of(1 - stream, distance, 0) + got[1].astype(jnp.float32)
        return step(to_right.astype(jnp.bfloat16), to_left.astype(jnp.bfloat16))

    a = step(rest_parts[2], rest_parts[5])
    b = step(rest_parts[4], rest_parts[0])
    a = sent(0, half - 1, a)
    for distance in range(half - 2, 0, -1):
        b = sent(1, distance, b)
        a = sent(0, distance, a)
    totals = [
        part_of(0, 0, 0) + a[0].astype(jnp.float32) + b[1].astype(jnp.float32),
        part_of(1, 0, 0) + b[0].astype(jnp.float32) + a[1].astype(jnp.float32),
    ]
    total = jnp.concatenate(totals, axis=1).astype(jnp.bfloat16)
    returned = jnp.stack([total[:CAP], lax.ppermute(total[CAP:], "expert", swap)])
    combine = dispatch_map.astype(jnp.float32) * jnp.transpose(weight)[:, None, :]
    mixed = jnp.einsum("wcr,wcd->rd", combine, returned.astype(jnp.float32))
    return mixed.astype(jnp.bfloat16)


def solution(mesh):
    in_specs = (
        P(("groups", "expert", "tensor"), None),
        P(("groups", "expert", "tensor"), None),
        P(("groups", "expert", "tensor"), None),
        P("expert", None, "tensor"),
        P("expert", None, "tensor"),
        P("expert", "tensor", None),
    )
    out_specs = P(("groups", "expert", "tensor"), None)
    return jax.shard_map(
        per_device, mesh=mesh, in_specs=in_specs, out_specs=out_specs, check_vma=False
    )
```

```python
import functools
import jax
import jax.numpy as jnp
from jax import lax
from jax.experimental import pallas as pl
from jax.experimental.pallas import tpu as pltpu
from jax.sharding import PartitionSpec as P

CAP = 24
COPIES = 16
TILE = 512
MARGIN = 3 * 2**20
CHEAP = pl.CostEstimate(flops=1024, bytes_accessed=1024, transcendentals=0)


def ring_of(count):
    return list(range(0, count, 2)) + list(range(count - 1, 0, -2))


def in_vmem(array):
    return pltpu.with_memory_space_constraint(array, pltpu.VMEM)


def in_hbm(array):
    return pltpu.with_memory_space_constraint(array, pltpu.HBM)


def call(kernel, name, operands, outs, scratch, room):
    return pl.pallas_call(
        kernel,
        in_specs=[pl.BlockSpec(memory_space=memory) for _, memory in operands],
        out_specs=[pl.BlockSpec(memory_space=pltpu.VMEM)] * len(outs),
        out_shape=[pltpu.VMEM(*out) for out in outs],
        scratch_shapes=scratch,
        cost_estimate=CHEAP,
        compiler_params=pltpu.CompilerParams(vmem_limit_bytes=room + MARGIN),
        name=name,
    )(*[in_vmem(array) if memory == pltpu.VMEM else in_hbm(array) for array, memory in operands])


def row_copies(source, target, done):
    rows = source.shape[1] // COPIES
    return [
        pltpu.make_async_copy(
            source.at[:, pl.ds(i * rows, rows)], target.at[:, pl.ds(i * rows, rows)], done.at[i]
        )
        for i in range(COPIES)
    ]


def fill_kernel(source, target, done):
    copies = row_copies(source, target, done)
    for copy in copies:
        copy.start()
    for copy in copies:
        copy.wait()


def fetched(weights):
    operands = [(weights, pltpu.HBM)]
    outs = [(weights.shape, weights.dtype)]
    return call(fill_kernel, "fetched", operands, outs, [pltpu.SemaphoreType.DMA((COPIES,))], 0)[0]


def accumulate(chunks, products):
    size, width = chunks[0][0].shape
    depth = width if size * len(chunks[0]) <= 512 else TILE
    for c, blocks in enumerate(chunks):
        for at in range(0, width, depth):
            rows = jnp.concatenate([block[:, at:at + depth] for block in blocks], axis=0)
            above = c * width + at
            for weights, total in products:
                part = jnp.dot(rows, weights[0, above:above + depth, :], preferred_element_type=jnp.float32)
                total[...] = total[...] + part if above else part


def activated(gate, up):
    return (gate / (1.0 + jnp.exp(-gate)) * up).astype(jnp.bfloat16)


def gate_kernel(count, *refs):
    chunks, (weights, out) = (refs[:count], refs[count:2 * count]), refs[2 * count:]
    accumulate(chunks, [(weights, out)])


def add_down(hidden, down, outs):
    size, width = outs[0].shape
    count = len(outs) // 2
    depth = width if size * count <= 512 else TILE
    for at in range(0, down.shape[2], depth):
        part = jnp.dot(hidden, down[0, :, at:at + depth], preferred_element_type=jnp.float32).astype(jnp.bfloat16)
        chunk, column = divmod(at, width)
        for b in range(count):
            outs[count * chunk + b][:, column:column + depth] = part[b * size:(b + 1) * size]


def near_kernel(count, *refs):
    chunks, (w_up, gate, w_down) = (refs[:count], refs[count:2 * count]), refs[2 * count:2 * count + 3]
    outs, (up, down, done) = refs[2 * count + 3:4 * count + 3], refs[4 * count + 3:]
    copies = row_copies(w_down, down, done)
    for copy in copies:
        copy.start()
    accumulate(chunks, [(w_up, up)])
    hidden = activated(gate[...], up[...])
    for copy in copies:
        copy.wait()
    add_down(hidden, down, outs)


def rest_kernel(*refs):
    chunks, (w_gate, w_up, w_down), outs = (refs[:3], refs[3:6]), refs[6:9], refs[9:15]
    gate, up, down, done = refs[15:]
    copies = row_copies(w_down, down, done)
    for copy in copies:
        copy.start()
    accumulate(chunks, [(w_gate, gate), (w_up, up)])
    hidden = activated(gate[...], up[...])
    for copy in copies:
        copy.wait()
    add_down(hidden, down, outs)


def routing(expert_ids, gate_probs, experts, slots):
    matches = expert_ids[:, :, None] == experts[None, None, :]
    member = jnp.any(matches, axis=1).astype(jnp.int32)
    weight = jnp.sum(jnp.where(matches, gate_probs[:, :, None], jnp.float32(0.0)), axis=1)
    slot_index = jnp.cumsum(member, axis=0) - member
    column = jnp.arange(slots)
    dispatch_map = (member[None, :, :] == 1) & (slot_index[None, :, :] == column[:, None, None])
    return (jnp.transpose(dispatch_map, (2, 0, 1)), weight)


def per_device(tokens, expert_ids, gate_probs, w_gate, w_up, w_down):
    n_tensor = lax.axis_size("tensor")
    half = n_tensor // 2
    size = 2 * CAP
    width = tokens.shape[1]
    mid_col = width // 2
    units = w_gate.shape[2]
    ring = ring_of(n_tensor)
    right = [(ring[i], ring[(i + 1) % n_tensor]) for i in range(n_tensor)]
    left = [(b, a) for a, b in right]
    swap = [(0, 1), (1, 0)]

    def step(to_right, to_left):
        pair = (lax.ppermute(to_right, "tensor", right), lax.ppermute(to_left, "tensor", left))
        return lax.optimization_barrier(pair)

    def tied(*values):
        return lax.optimization_barrier(values)

    me = lax.axis_index("expert")
    experts = jnp.stack([me, 1 - me])
    dispatch_map, weight = routing(expert_ids, gate_probs, experts, CAP)
    outgoing = jnp.dot(
        dispatch_map.astype(jnp.bfloat16).reshape(size, tokens.shape[0]),
        tokens,
        preferred_element_type=jnp.float32,
    ).astype(jnp.bfloat16)
    own = jnp.concatenate([outgoing[:CAP], lax.ppermute(outgoing[CAP:], "expert", swap)], axis=0)

    own, w_gate = tied(own, w_gate)
    halves = [own[:, :mid_col], own[:, mid_col:]]
    blocks = [[halves[0]], [halves[1]]]

    def arrived(a, b):
        blocks[0].extend([a[0], b[1]])
        blocks[1].extend([b[0], a[1]])

    a = step(halves[0], halves[1])
    b = step(halves[1], halves[0])
    gate_here = fetched(w_gate)
    a, gate_here = tied(a, gate_here)
    a, w_up = tied(a, w_up)
    up_here = fetched(w_up)
    b, up_here = tied(b, up_here)
    arrived(a, b)
    for _ in range(half - 3):
        a = step(*a)
        b = step(*b)
        arrived(a, b)
    near = [(block, pltpu.VMEM) for chunk in blocks for block in chunk]
    count = len(blocks[0])
    rows = count * size
    product = ((rows, units), jnp.float32)
    near_gate, = call(
        functools.partial(gate_kernel, count), "near_gate", near + [(gate_here, pltpu.VMEM)], [product], [],
        rows * units * 8,
    )
    b, near_gate = tied(b, near_gate)
    a = step(*a)
    b = step(*b)
    rest = [[a[0], b[1]], [b[0], a[1]]]
    a, near_gate = tied(a, near_gate)
    far = step(*a)
    down_scratch = [pltpu.VMEM(w_down.shape, jnp.bfloat16), pltpu.SemaphoreType.DMA((COPIES,))]
    down_room = units * width * 2
    near_parts = call(
        functools.partial(near_kernel, count), "near_parts",
        near + [(up_here, pltpu.VMEM), (near_gate, pltpu.VMEM), (w_down, pltpu.HBM)],
        [((size, mid_col), jnp.bfloat16)] * (2 * count), [pltpu.VMEM((rows, units), jnp.float32)] + down_scratch,
        down_room + rows * units * 16,
    )
    rest = [rest[chunk] + [far[chunk]] for chunk in range(2)]
    rest, near_parts = tied(rest, near_parts)
    rest_parts = call(
        rest_kernel, "rest",
        [(block, pltpu.VMEM) for chunk in rest for block in chunk]
        + [(gate_here, pltpu.VMEM), (up_here, pltpu.VMEM), (w_down, pltpu.HBM)],
        [((size, mid_col), jnp.bfloat16)] * 6,
        [pltpu.VMEM((3 * size, units), jnp.float32)] * 2 + down_scratch,
        down_room + 3 * size * units * 16,
    )

    def part_of(chunk, distance, side):
        if distance == half - 1:
            return rest_parts[3 * chunk + side].astype(jnp.float32)
        index = 2 * distance - 1 + side if distance else 0
        return near_parts[count * chunk + index].astype(jnp.float32)

    def sent(stream, distance, got):
        to_right = part_of(stream, distance, 1) + got[0].astype(jnp.float32)
        to_left = part_of(1 - stream, distance, 0) + got[1].astype(jnp.float32)
        return step(to_right.astype(jnp.bfloat16), to_left.astype(jnp.bfloat16))

    a = step(rest_parts[2], rest_parts[5])
    b = step(rest_parts[4], rest_parts[0])
    a = sent(0, half - 1, a)
    for distance in range(half - 2, 0, -1):
        b = sent(1, distance, b)
        a = sent(0, distance, a)
    totals = [
        part_of(0, 0, 0) + a[0].astype(jnp.float32) + b[1].astype(jnp.float32),
        part_of(1, 0, 0) + b[0].astype(jnp.float32) + a[1].astype(jnp.float32),
    ]
    total = jnp.concatenate(totals, axis=1).astype(jnp.bfloat16)
    returned = jnp.stack([total[:CAP], lax.ppermute(total[CAP:], "expert", swap)])
    combine = dispatch_map.astype(jnp.float32) * jnp.transpose(weight)[:, None, :]
    mixed = jnp.einsum("wcr,wcd->rd", combine, returned.astype(jnp.float32))
    return mixed.astype(jnp.bfloat16)


def solution(mesh):
    in_specs = (
        P(("groups", "expert", "tensor"), None),
        P(("groups", "expert", "tensor"), None),
        P(("groups", "expert", "tensor"), None),
        P("expert", None, "tensor"),
        P("expert", None, "tensor"),
        P("expert", "tensor", None),
    )
    out_specs = P(("groups", "expert", "tensor"), None)
    return jax.shard_map(
        per_device, mesh=mesh, in_specs=in_specs, out_specs=out_specs, check_vma=False
    )
```

```python
import functools
import jax
import jax.numpy as jnp
from jax import lax
from jax.experimental import pallas as pl
from jax.experimental.pallas import tpu as pltpu
from jax.sharding import PartitionSpec as P

CAP = 24
COPIES = 16
TILE = 512
MARGIN = 3 * 2**20
CHEAP = pl.CostEstimate(flops=1024, bytes_accessed=1024, transcendentals=0)


def ring_of(count):
    return list(range(0, count, 2)) + list(range(count - 1, 0, -2))


def in_vmem(array):
    return pltpu.with_memory_space_constraint(array, pltpu.VMEM)


def in_hbm(array):
    return pltpu.with_memory_space_constraint(array, pltpu.HBM)


def call(kernel, name, operands, outs, scratch, room):
    return pl.pallas_call(
        kernel,
        in_specs=[pl.BlockSpec(memory_space=memory) for _, memory in operands],
        out_specs=[pl.BlockSpec(memory_space=pltpu.VMEM)] * len(outs),
        out_shape=[pltpu.VMEM(*out) for out in outs],
        scratch_shapes=scratch,
        cost_estimate=CHEAP,
        compiler_params=pltpu.CompilerParams(vmem_limit_bytes=room + MARGIN),
        name=name,
    )(*[in_vmem(array) if memory == pltpu.VMEM else in_hbm(array) for array, memory in operands])


def row_copies(source, target, done, column=0):
    rows, width = source.shape[1] // COPIES, target.shape[2]
    return [
        pltpu.make_async_copy(
            source.at[:, pl.ds(i * rows, rows), pl.ds(column, width)], target.at[:, pl.ds(i * rows, rows)], done.at[i]
        )
        for i in range(COPIES)
    ]


def fill_kernel(source, target, done):
    copies = row_copies(source, target, done)
    for copy in copies:
        copy.start()
    for copy in copies:
        copy.wait()


def fetched(weights, width):
    operands = [(weights, pltpu.HBM)]
    outs = [((*weights.shape[:2], width), weights.dtype)]
    return call(fill_kernel, "fetched", operands, outs, [pltpu.SemaphoreType.DMA((COPIES,))], 0)[0]


def accumulate(chunks, products):
    size, width = chunks[0][0].shape
    depth = width if size * len(chunks[0]) <= 512 else TILE
    for c, blocks in enumerate(chunks):
        for at in range(0, width, depth):
            rows = jnp.concatenate([block[:, at:at + depth] for block in blocks], axis=0)
            above = c * width + at
            for weights, total in products:
                part = jnp.dot(rows, weights[0, above:above + depth, :], preferred_element_type=jnp.float32)
                total[...] = total[...] + part if above else part


def activated(gate, up):
    return (gate / (1.0 + jnp.exp(-gate)) * up).astype(jnp.bfloat16)


def gate_kernel(count, *refs):
    chunks, (weights, out) = (refs[:count], refs[count:2 * count]), refs[2 * count:]
    accumulate(chunks, [(weights, out)])


def add_down(hidden, down, outs):
    size, width = outs[0].shape
    depth = width if size * len(outs) <= 512 else TILE
    for at in range(0, width, depth):
        part = jnp.dot(hidden, down[0, :, at:at + depth], preferred_element_type=jnp.float32).astype(jnp.bfloat16)
        for b, out in enumerate(outs):
            out[:, at:at + depth] = part[b * size:(b + 1) * size]


def up_kernel(count, *refs):
    chunks, (weights, gate, out, total) = (refs[:count], refs[count:2 * count]), refs[2 * count:]
    accumulate(chunks, [(weights, total)])
    out[...] = activated(gate[...], total[...])


def rest_kernel(*refs):
    chunks, (w_gate, w_up, down_0, w_down), outs = (refs[:3], refs[3:6]), refs[6:10], refs[10:16]
    gate, up, down_1, done = refs[16:]
    copies = row_copies(w_down, down_1, done, down_1.shape[2])
    for copy in copies:
        copy.start()
    accumulate(chunks, [(w_gate, gate), (w_up, up)])
    hidden = activated(gate[...], up[...])
    add_down(hidden, down_0, outs[:3])
    for copy in copies:
        copy.wait()
    add_down(hidden, down_1, outs[3:])


def near_down_kernel(hidden, down_0, w_down, *refs):
    outs, (down_1, done) = refs[:-2], refs[-2:]
    count = len(outs) // 2
    copies = row_copies(w_down, down_1, done, down_1.shape[2])
    for copy in copies:
        copy.start()
    add_down(hidden[...], down_0, outs[:count])
    for copy in copies:
        copy.wait()
    add_down(hidden[...], down_1, outs[count:])


def routing(expert_ids, gate_probs, experts, slots):
    matches = expert_ids[:, :, None] == experts[None, None, :]
    member = jnp.any(matches, axis=1).astype(jnp.int32)
    weight = jnp.sum(jnp.where(matches, gate_probs[:, :, None], jnp.float32(0.0)), axis=1)
    slot_index = jnp.cumsum(member, axis=0) - member
    column = jnp.arange(slots)
    dispatch_map = (member[None, :, :] == 1) & (slot_index[None, :, :] == column[:, None, None])
    return (jnp.transpose(dispatch_map, (2, 0, 1)), weight)


def per_device(tokens, expert_ids, gate_probs, w_gate, w_up, w_down):
    n_tensor = lax.axis_size("tensor")
    half = n_tensor // 2
    size = 2 * CAP
    width = tokens.shape[1]
    mid_col = width // 2
    units = w_gate.shape[2]
    ring = ring_of(n_tensor)
    right = [(ring[i], ring[(i + 1) % n_tensor]) for i in range(n_tensor)]
    left = [(b, a) for a, b in right]
    swap = [(0, 1), (1, 0)]

    def step(to_right, to_left):
        pair = (lax.ppermute(to_right, "tensor", right), lax.ppermute(to_left, "tensor", left))
        return lax.optimization_barrier(pair)

    def tied(*values):
        return lax.optimization_barrier(values)

    me = lax.axis_index("expert")
    experts = jnp.stack([me, 1 - me])
    dispatch_map, weight = routing(expert_ids, gate_probs, experts, CAP)
    outgoing = jnp.dot(
        dispatch_map.astype(jnp.bfloat16).reshape(size, tokens.shape[0]),
        tokens,
        preferred_element_type=jnp.float32,
    ).astype(jnp.bfloat16)
    own = jnp.concatenate([outgoing[:CAP], lax.ppermute(outgoing[CAP:], "expert", swap)], axis=0)

    own, w_gate = tied(own, w_gate)
    halves = [own[:, :mid_col], own[:, mid_col:]]
    blocks = [[halves[0]], [halves[1]]]

    def arrived(a, b):
        blocks[0].extend([a[0], b[1]])
        blocks[1].extend([b[0], a[1]])

    a = step(halves[0], halves[1])
    b = step(halves[1], halves[0])
    gate_here = fetched(w_gate, units)
    a, gate_here = tied(a, gate_here)
    a, w_up = tied(a, w_up)
    up_here = fetched(w_up, units)
    b, up_here = tied(b, up_here)
    arrived(a, b)
    for _ in range(half - 3):
        a = step(*a)
        b = step(*b)
        arrived(a, b)
    near = [(block, pltpu.VMEM) for chunk in blocks for block in chunk]
    count = len(blocks[0])
    rows = count * size
    product = ((rows, units), jnp.float32)
    near_gate, = call(
        functools.partial(gate_kernel, count), "near_gate", near + [(gate_here, pltpu.VMEM)], [product], [],
        rows * units * 8,
    )
    b, near_gate = tied(b, near_gate)
    a = step(*a)
    b = step(*b)
    rest = [[a[0], b[1]], [b[0], a[1]]]
    a, near_gate = tied(a, near_gate)
    far = step(*a)
    near_hidden, = call(
        functools.partial(up_kernel, count), "near_up",
        near + [(up_here, pltpu.VMEM), (near_gate, pltpu.VMEM)], [((rows, units), jnp.bfloat16)],
        [pltpu.VMEM((rows, units), jnp.float32)], rows * units * 16,
    )
    near_hidden, w_down = tied(near_hidden, w_down)
    down_here = fetched(w_down, mid_col)
    rest = [rest[chunk] + [far[chunk]] for chunk in range(2)]
    rest, down_here = tied(rest, down_here)
    down_scratch = [pltpu.VMEM(down_here.shape, jnp.bfloat16), pltpu.SemaphoreType.DMA((COPIES,))]
    down_room = units * width
    rest_parts = call(
        rest_kernel, "rest",
        [(block, pltpu.VMEM) for chunk in rest for block in chunk]
        + [(gate_here, pltpu.VMEM), (up_here, pltpu.VMEM), (down_here, pltpu.VMEM), (w_down, pltpu.HBM)],
        [((size, mid_col), jnp.bfloat16)] * 6,
        [pltpu.VMEM((3 * size, units), jnp.float32)] * 2 + down_scratch,
        down_room + 3 * size * units * 16,
    )
    near_parts = call(
        near_down_kernel, "near_down", [(near_hidden, pltpu.VMEM), (down_here, pltpu.VMEM), (w_down, pltpu.HBM)],
        [((size, mid_col), jnp.bfloat16)] * (2 * count), down_scratch, down_room + rows * TILE * 12,
    )

    def part_of(chunk, distance, side):
        if distance == half - 1:
            return rest_parts[3 * chunk + side].astype(jnp.float32)
        index = 2 * distance - 1 + side if distance else 0
        return near_parts[count * chunk + index].astype(jnp.float32)

    def sent(stream, distance, got):
        to_right = part_of(stream, distance, 1) + got[0].astype(jnp.float32)
        to_left = part_of(1 - stream, distance, 0) + got[1].astype(jnp.float32)
        return step(to_right.astype(jnp.bfloat16), to_left.astype(jnp.bfloat16))

    a = step(rest_parts[2], rest_parts[5])
    b = step(rest_parts[4], rest_parts[0])
    a = sent(0, half - 1, a)
    for distance in range(half - 2, 0, -1):
        b = sent(1, distance, b)
        a = sent(0, distance, a)
    totals = [
        part_of(0, 0, 0) + a[0].astype(jnp.float32) + b[1].astype(jnp.float32),
        part_of(1, 0, 0) + b[0].astype(jnp.float32) + a[1].astype(jnp.float32),
    ]
    total = jnp.concatenate(totals, axis=1).astype(jnp.bfloat16)
    returned = jnp.stack([total[:CAP], lax.ppermute(total[CAP:], "expert", swap)])
    combine = dispatch_map.astype(jnp.float32) * jnp.transpose(weight)[:, None, :]
    mixed = jnp.einsum("wcr,wcd->rd", combine, returned.astype(jnp.float32))
    return mixed.astype(jnp.bfloat16)


def solution(mesh):
    in_specs = (
        P(("groups", "expert", "tensor"), None),
        P(("groups", "expert", "tensor"), None),
        P(("groups", "expert", "tensor"), None),
        P("expert", None, "tensor"),
        P("expert", None, "tensor"),
        P("expert", "tensor", None),
    )
    out_specs = P(("groups", "expert", "tensor"), None)
    return jax.shard_map(
        per_device, mesh=mesh, in_specs=in_specs, out_specs=out_specs, check_vma=False
    )
```

```python
import functools
import jax
import jax.numpy as jnp
from jax import lax
from jax.experimental import pallas as pl
from jax.experimental.pallas import tpu as pltpu
from jax.sharding import PartitionSpec as P

CAP = 24
COPIES = 16
TILE = 512
MARGIN = 3 * 2**20
CHEAP = pl.CostEstimate(flops=1024, bytes_accessed=1024, transcendentals=0)


def ring_of(count):
    return list(range(0, count, 2)) + list(range(count - 1, 0, -2))


def placed(array, memory):
    return array if memory == pltpu.SMEM else pltpu.with_memory_space_constraint(array, memory)


def call(kernel, name, operands, outs, scratch, room, aliases=None):
    return pl.pallas_call(
        kernel,
        in_specs=[pl.BlockSpec(memory_space=memory) for _, memory in operands],
        out_specs=[pl.BlockSpec(memory_space=pltpu.VMEM)] * len(outs),
        out_shape=[pltpu.VMEM(*out) for out in outs],
        scratch_shapes=scratch,
        input_output_aliases=aliases or {},
        cost_estimate=CHEAP,
        compiler_params=pltpu.CompilerParams(vmem_limit_bytes=room + MARGIN),
        name=name,
    )(*[placed(array, memory) for array, memory in operands])


def row_copies(source, target, done, column=0):
    rows, width = source.shape[1] // COPIES, target.shape[2]
    return [
        pltpu.make_async_copy(
            source.at[:, pl.ds(i * rows, rows), pl.ds(column, width)], target.at[:, pl.ds(i * rows, rows)], done.at[i]
        )
        for i in range(COPIES)
    ]


def fill_kernel(source, target, done):
    copies = row_copies(source, target, done)
    for copy in copies:
        copy.start()
    for copy in copies:
        copy.wait()


def fill_some_kernel(which, core, source, *refs):
    target, done = refs[-2:]

    @pl.when(core[0] == which)
    def _():
        fill_kernel(source, target, done)


def fetched(weights, width):
    operands = [(weights, pltpu.HBM)]
    outs = [((*weights.shape[:2], width), weights.dtype)]
    return call(fill_kernel, "fetched", operands, outs, [pltpu.SemaphoreType.DMA((COPIES,))], 0)[0]


def fetched_by(which, core, weights, target=None):
    operands = [(core, pltpu.SMEM), (weights, pltpu.HBM)] + ([] if target is None else [(target, pltpu.VMEM)])
    outs = [(weights.shape, weights.dtype)]
    scratch = [pltpu.SemaphoreType.DMA((COPIES,))]
    kernel = functools.partial(fill_some_kernel, which)
    return call(kernel, "fetched_by", operands, outs, scratch, 0, {} if target is None else {2: 0})[0]


def accumulate(chunks, products):
    size, width = chunks[0][0].shape
    depth = width if size * len(chunks[0]) <= 512 else TILE
    for c, blocks in enumerate(chunks):
        for at in range(0, width, depth):
            rows = jnp.concatenate([block[:, at:at + depth] for block in blocks], axis=0)
            above = c * width + at
            for weights, total in products:
                part = jnp.dot(rows, weights[0, above:above + depth, :], preferred_element_type=jnp.float32)
                total[...] = total[...] + part if above else part


def activated(gate, up):
    return (gate / (1.0 + jnp.exp(-gate)) * up).astype(jnp.bfloat16)


def gate_kernel(count, *refs):
    chunks, (weights, out) = (refs[:count], refs[count:2 * count]), refs[2 * count:]
    accumulate(chunks, [(weights, out)])


def add_down(hidden, down, outs):
    size, width = outs[0].shape
    depth = width if size * len(outs) <= 512 else TILE
    for at in range(0, width, depth):
        part = jnp.dot(hidden, down[0, :, at:at + depth], preferred_element_type=jnp.float32).astype(jnp.bfloat16)
        for b, out in enumerate(outs):
            out[:, at:at + depth] = part[b * size:(b + 1) * size]


def up_kernel(count, *refs):
    chunks, (weights, gate, out, total) = (refs[:count], refs[count:2 * count]), refs[2 * count:]
    accumulate(chunks, [(weights, total)])
    out[...] = activated(gate[...], total[...])


def rest_kernel(*refs):
    chunks, (w_gate, w_up, down_0, w_down), outs = (refs[:3], refs[3:6]), refs[6:10], refs[10:16]
    gate, up, down_1, done = refs[16:]
    copies = row_copies(w_down, down_1, done, down_1.shape[2])
    for copy in copies:
        copy.start()
    accumulate(chunks, [(w_gate, gate), (w_up, up)])
    hidden = activated(gate[...], up[...])
    add_down(hidden, down_0, outs[:3])
    for copy in copies:
        copy.wait()
    add_down(hidden, down_1, outs[3:])


def near_down_kernel(hidden, down_0, w_down, *refs):
    outs, (down_1, done) = refs[:-2], refs[-2:]
    count = len(outs) // 2
    copies = row_copies(w_down, down_1, done, down_1.shape[2])
    for copy in copies:
        copy.start()
    add_down(hidden[...], down_0, outs[:count])
    for copy in copies:
        copy.wait()
    add_down(hidden[...], down_1, outs[count:])


def routing(expert_ids, gate_probs, experts, slots):
    matches = expert_ids[:, :, None] == experts[None, None, :]
    member = jnp.any(matches, axis=1).astype(jnp.int32)
    weight = jnp.sum(jnp.where(matches, gate_probs[:, :, None], jnp.float32(0.0)), axis=1)
    slot_index = jnp.cumsum(member, axis=0) - member
    column = jnp.arange(slots)
    dispatch_map = (member[None, :, :] == 1) & (slot_index[None, :, :] == column[:, None, None])
    return (jnp.transpose(dispatch_map, (2, 0, 1)), weight)


def per_device(tokens, expert_ids, gate_probs, w_gate, w_up, w_down):
    n_tensor = lax.axis_size("tensor")
    half = n_tensor // 2
    size = 2 * CAP
    width = tokens.shape[1]
    mid_col = width // 2
    units = w_gate.shape[2]
    ring = ring_of(n_tensor)
    right = [(ring[i], ring[(i + 1) % n_tensor]) for i in range(n_tensor)]
    left = [(b, a) for a, b in right]
    swap = [(0, 1), (1, 0)]

    def step(to_right, to_left):
        pair = (lax.ppermute(to_right, "tensor", right), lax.ppermute(to_left, "tensor", left))
        return lax.optimization_barrier(pair)

    def tied(*values):
        return lax.optimization_barrier(values)

    me = lax.axis_index("expert")
    experts = jnp.stack([me, 1 - me])
    dispatch_map, weight = routing(expert_ids, gate_probs, experts, CAP)
    outgoing = jnp.dot(
        dispatch_map.astype(jnp.bfloat16).reshape(size, tokens.shape[0]),
        tokens,
        preferred_element_type=jnp.float32,
    ).astype(jnp.bfloat16)
    core = jnp.reshape(me, (1,)).astype(jnp.int32)
    outgoing, w_gate = tied(outgoing, w_gate)
    gate_here = fetched_by(0, core, w_gate)
    gate_here, w_up = tied(gate_here, w_up)
    up_here = fetched_by(0, core, w_up)
    swapped = lax.ppermute(outgoing[CAP:], "expert", swap)
    own = jnp.concatenate([outgoing[:CAP], swapped], axis=0)

    own, gate_here, up_here = tied(own, gate_here, up_here)
    halves = [own[:, :mid_col], own[:, mid_col:]]
    blocks = [[halves[0]], [halves[1]]]

    def arrived(a, b):
        blocks[0].extend([a[0], b[1]])
        blocks[1].extend([b[0], a[1]])

    a = step(halves[0], halves[1])
    b = step(halves[1], halves[0])
    gate_here = fetched_by(1, core, w_gate, gate_here)
    a, gate_here = tied(a, gate_here)
    a, up_here = tied(a, up_here)
    up_here = fetched_by(1, core, w_up, up_here)
    b, up_here = tied(b, up_here)
    arrived(a, b)
    for _ in range(half - 3):
        a = step(*a)
        b = step(*b)
        arrived(a, b)
    near = [(block, pltpu.VMEM) for chunk in blocks for block in chunk]
    count = len(blocks[0])
    rows = count * size
    product = ((rows, units), jnp.float32)
    near_gate, = call(
        functools.partial(gate_kernel, count), "near_gate", near + [(gate_here, pltpu.VMEM)], [product], [],
        rows * units * 8,
    )
    b, near_gate = tied(b, near_gate)
    a = step(*a)
    b = step(*b)
    rest = [[a[0], b[1]], [b[0], a[1]]]
    a, near_gate = tied(a, near_gate)
    far = step(*a)
    near_hidden, = call(
        functools.partial(up_kernel, count), "near_up",
        near + [(up_here, pltpu.VMEM), (near_gate, pltpu.VMEM)], [((rows, units), jnp.bfloat16)],
        [pltpu.VMEM((rows, units), jnp.float32)], rows * units * 16,
    )
    near_hidden, w_down = tied(near_hidden, w_down)
    down_here = fetched(w_down, mid_col)
    rest = [rest[chunk] + [far[chunk]] for chunk in range(2)]
    rest, down_here = tied(rest, down_here)
    down_scratch = [pltpu.VMEM(down_here.shape, jnp.bfloat16), pltpu.SemaphoreType.DMA((COPIES,))]
    down_room = units * width
    rest_parts = call(
        rest_kernel, "rest",
        [(block, pltpu.VMEM) for chunk in rest for block in chunk]
        + [(gate_here, pltpu.VMEM), (up_here, pltpu.VMEM), (down_here, pltpu.VMEM), (w_down, pltpu.HBM)],
        [((size, mid_col), jnp.bfloat16)] * 6,
        [pltpu.VMEM((3 * size, units), jnp.float32)] * 2 + down_scratch,
        down_room + 3 * size * units * 16,
    )
    near_hidden, _ = tied(near_hidden, rest_parts)
    near_parts = call(
        near_down_kernel, "near_down", [(near_hidden, pltpu.VMEM), (down_here, pltpu.VMEM), (w_down, pltpu.HBM)],
        [((size, mid_col), jnp.bfloat16)] * (2 * count), down_scratch, down_room + rows * TILE * 12,
    )

    def part_of(chunk, distance, side):
        if distance == half - 1:
            return rest_parts[3 * chunk + side].astype(jnp.float32)
        index = 2 * distance - 1 + side if distance else 0
        return near_parts[count * chunk + index].astype(jnp.float32)

    def sent(stream, distance, got):
        to_right = part_of(stream, distance, 1) + got[0].astype(jnp.float32)
        to_left = part_of(1 - stream, distance, 0) + got[1].astype(jnp.float32)
        return step(to_right.astype(jnp.bfloat16), to_left.astype(jnp.bfloat16))

    a = step(rest_parts[2], rest_parts[5])
    b = step(rest_parts[4], rest_parts[0])
    a = sent(0, half - 1, a)
    for distance in range(half - 2, 0, -1):
        b = sent(1, distance, b)
        a = sent(0, distance, a)
    totals = [
        part_of(0, 0, 0) + a[0].astype(jnp.float32) + b[1].astype(jnp.float32),
        part_of(1, 0, 0) + b[0].astype(jnp.float32) + a[1].astype(jnp.float32),
    ]
    total = jnp.concatenate(totals, axis=1).astype(jnp.bfloat16)
    returned = jnp.stack([total[:CAP], lax.ppermute(total[CAP:], "expert", swap)])
    combine = dispatch_map.astype(jnp.float32) * jnp.transpose(weight)[:, None, :]
    mixed = jnp.einsum("wcr,wcd->rd", combine, returned.astype(jnp.float32))
    return mixed.astype(jnp.bfloat16)


def solution(mesh):
    in_specs = (
        P(("groups", "expert", "tensor"), None),
        P(("groups", "expert", "tensor"), None),
        P(("groups", "expert", "tensor"), None),
        P("expert", None, "tensor"),
        P("expert", None, "tensor"),
        P("expert", "tensor", None),
    )
    out_specs = P(("groups", "expert", "tensor"), None)
    return jax.shard_map(
        per_device, mesh=mesh, in_specs=in_specs, out_specs=out_specs, check_vma=False
    )
```

```python
import functools
import jax
import jax.numpy as jnp
from jax import lax
from jax.experimental import pallas as pl
from jax.experimental.pallas import tpu as pltpu
from jax.sharding import PartitionSpec as P

CAP = 24
COPIES = 16
TILE = 512
MARGIN = 3 * 2**20
CHEAP = pl.CostEstimate(flops=1024, bytes_accessed=1024, transcendentals=0)


def ring_of(count):
    return list(range(0, count, 2)) + list(range(count - 1, 0, -2))


def in_vmem(array):
    return pltpu.with_memory_space_constraint(array, pltpu.VMEM)


def in_hbm(array):
    return pltpu.with_memory_space_constraint(array, pltpu.HBM)


def call(kernel, name, operands, outs, scratch, room):
    return pl.pallas_call(
        kernel,
        in_specs=[pl.BlockSpec(memory_space=memory) for _, memory in operands],
        out_specs=[pl.BlockSpec(memory_space=pltpu.VMEM)] * len(outs),
        out_shape=[pltpu.VMEM(*out) for out in outs],
        scratch_shapes=scratch,
        cost_estimate=CHEAP,
        compiler_params=pltpu.CompilerParams(vmem_limit_bytes=room + MARGIN),
        name=name,
    )(*[in_vmem(array) if memory == pltpu.VMEM else in_hbm(array) for array, memory in operands])


def row_copies(source, target, done, column=0):
    rows, width = source.shape[1] // COPIES, target.shape[2]
    return [
        pltpu.make_async_copy(
            source.at[:, pl.ds(i * rows, rows), pl.ds(column, width)], target.at[:, pl.ds(i * rows, rows)], done.at[i]
        )
        for i in range(COPIES)
    ]


def fill_kernel(source, target, done):
    copies = row_copies(source, target, done)
    for copy in copies:
        copy.start()
    for copy in copies:
        copy.wait()


def fetched(weights, width):
    operands = [(weights, pltpu.HBM)]
    outs = [((*weights.shape[:2], width), weights.dtype)]
    return call(fill_kernel, "fetched", operands, outs, [pltpu.SemaphoreType.DMA((COPIES,))], 0)[0]


def accumulate(chunks, products):
    size, width = chunks[0][0].shape
    depth = width if size * len(chunks[0]) <= 512 else TILE
    for c, blocks in enumerate(chunks):
        for at in range(0, width, depth):
            rows = jnp.concatenate([block[:, at:at + depth] for block in blocks], axis=0)
            above = c * width + at
            for weights, total in products:
                part = jnp.dot(rows, weights[0, above:above + depth, :], preferred_element_type=jnp.float32)
                total[...] = total[...] + part if above else part


def activated(gate, up):
    return (gate / (1.0 + jnp.exp(-gate)) * up).astype(jnp.bfloat16)


def gate_kernel(count, *refs):
    chunks, (weights, out) = (refs[:count], refs[count:2 * count]), refs[2 * count:]
    accumulate(chunks, [(weights, out)])


def add_down(hidden, down, outs):
    size, width = outs[0].shape
    depth = width if size * len(outs) <= 512 else TILE
    for at in range(0, width, depth):
        part = jnp.dot(hidden, down[0, :, at:at + depth], preferred_element_type=jnp.float32).astype(jnp.bfloat16)
        for b, out in enumerate(outs):
            out[:, at:at + depth] = part[b * size:(b + 1) * size]


def up_kernel(count, *refs):
    chunks, (weights, gate, out, total) = (refs[:count], refs[count:2 * count]), refs[2 * count:]
    accumulate(chunks, [(weights, total)])
    out[...] = activated(gate[...], total[...])


def rest_kernel(*refs):
    chunks, (w_gate, w_up, down_0, w_down), outs = (refs[:3], refs[3:6]), refs[6:10], refs[10:16]
    gate, up, down_1, done = refs[16:]
    copies = row_copies(w_down, down_1, done, down_1.shape[2])
    for copy in copies:
        copy.start()
    accumulate(chunks, [(w_gate, gate), (w_up, up)])
    hidden = activated(gate[...], up[...])
    add_down(hidden, down_0, outs[:3])
    for copy in copies:
        copy.wait()
    add_down(hidden, down_1, outs[3:])


def near_down_kernel(hidden, down_0, w_down, *refs):
    outs, (down_1, done) = refs[:-2], refs[-2:]
    count = len(outs) // 2
    copies = row_copies(w_down, down_1, done, down_1.shape[2])
    for copy in copies:
        copy.start()
    add_down(hidden[...], down_0, outs[:count])
    for copy in copies:
        copy.wait()
    add_down(hidden[...], down_1, outs[count:])


def routing(expert_ids, gate_probs, experts, slots):
    matches = expert_ids[:, :, None] == experts[None, None, :]
    member = jnp.any(matches, axis=1).astype(jnp.int32)
    weight = jnp.sum(jnp.where(matches, gate_probs[:, :, None], jnp.float32(0.0)), axis=1)
    slot_index = jnp.cumsum(member, axis=0) - member
    column = jnp.arange(slots)
    dispatch_map = (member[None, :, :] == 1) & (slot_index[None, :, :] == column[:, None, None])
    return (jnp.transpose(dispatch_map, (2, 0, 1)), weight)


def per_device(tokens, expert_ids, gate_probs, w_gate, w_up, w_down):
    n_tensor = lax.axis_size("tensor")
    half = n_tensor // 2
    size = 2 * CAP
    width = tokens.shape[1]
    mid_col = width // 2
    units = w_gate.shape[2]
    ring = ring_of(n_tensor)
    right = [(ring[i], ring[(i + 1) % n_tensor]) for i in range(n_tensor)]
    left = [(b, a) for a, b in right]
    swap = [(0, 1), (1, 0)]

    def step(to_right, to_left):
        pair = (lax.ppermute(to_right, "tensor", right), lax.ppermute(to_left, "tensor", left))
        return lax.optimization_barrier(pair)

    def tied(*values):
        return lax.optimization_barrier(values)

    me = lax.axis_index("expert")
    experts = jnp.stack([me, 1 - me])
    dispatch_map, weight = routing(expert_ids, gate_probs, experts, CAP)
    outgoing = jnp.dot(
        dispatch_map.astype(jnp.bfloat16).reshape(size, tokens.shape[0]),
        tokens,
        preferred_element_type=jnp.float32,
    ).astype(jnp.bfloat16)
    own = jnp.concatenate([outgoing[:CAP], lax.ppermute(outgoing[CAP:], "expert", swap)], axis=0)

    own, w_gate = tied(own, w_gate)
    halves = [own[:, :mid_col], own[:, mid_col:]]
    blocks = [[halves[0]], [halves[1]]]

    def arrived(a, b):
        blocks[0].extend([a[0], b[1]])
        blocks[1].extend([b[0], a[1]])

    a = step(halves[0], halves[1])
    b = step(halves[1], halves[0])
    gate_here = fetched(w_gate, units)
    a, gate_here = tied(a, gate_here)
    a, w_up = tied(a, w_up)
    up_here = fetched(w_up, units)
    b, up_here = tied(b, up_here)
    arrived(a, b)
    for _ in range(half - 3):
        a = step(*a)
        b = step(*b)
        arrived(a, b)
    near = [(block, pltpu.VMEM) for chunk in blocks for block in chunk]
    count = len(blocks[0])
    rows = count * size
    product = ((rows, units), jnp.float32)
    near_gate, = call(
        functools.partial(gate_kernel, count), "near_gate", near + [(gate_here, pltpu.VMEM)], [product], [],
        rows * units * 8,
    )
    b, near_gate = tied(b, near_gate)
    a = step(*a)
    b = step(*b)
    rest = [[a[0], b[1]], [b[0], a[1]]]
    a, near_gate = tied(a, near_gate)
    far = step(*a)
    near_hidden, = call(
        functools.partial(up_kernel, count), "near_up",
        near + [(up_here, pltpu.VMEM), (near_gate, pltpu.VMEM)], [((rows, units), jnp.bfloat16)],
        [pltpu.VMEM((rows, units), jnp.float32)], rows * units * 16,
    )
    near_hidden, w_down = tied(near_hidden, w_down)
    down_here = fetched(w_down, mid_col)
    rest = [rest[chunk] + [far[chunk]] for chunk in range(2)]
    rest, down_here = tied(rest, down_here)
    down_scratch = [pltpu.VMEM(down_here.shape, jnp.bfloat16), pltpu.SemaphoreType.DMA((COPIES,))]
    down_room = units * width
    rest_parts = call(
        rest_kernel, "rest",
        [(block, pltpu.VMEM) for chunk in rest for block in chunk]
        + [(gate_here, pltpu.VMEM), (up_here, pltpu.VMEM), (down_here, pltpu.VMEM), (w_down, pltpu.HBM)],
        [((size, mid_col), jnp.bfloat16)] * 6,
        [pltpu.VMEM((3 * size, units), jnp.float32)] * 2 + down_scratch,
        down_room + 3 * size * units * 16,
    )
    near_hidden, _, _ = tied(near_hidden, rest_parts[4], rest_parts[0])
    near_parts = call(
        near_down_kernel, "near_down", [(near_hidden, pltpu.VMEM), (down_here, pltpu.VMEM), (w_down, pltpu.HBM)],
        [((size, mid_col), jnp.bfloat16)] * (2 * count), down_scratch, down_room + rows * TILE * 12,
    )

    def part_of(chunk, distance, side):
        if distance == half - 1:
            return rest_parts[3 * chunk + side].astype(jnp.float32)
        index = 2 * distance - 1 + side if distance else 0
        return near_parts[count * chunk + index].astype(jnp.float32)

    def sent(stream, distance, got):
        to_right = part_of(stream, distance, 1) + got[0].astype(jnp.float32)
        to_left = part_of(1 - stream, distance, 0) + got[1].astype(jnp.float32)
        return step(to_right.astype(jnp.bfloat16), to_left.astype(jnp.bfloat16))

    a = step(rest_parts[2], rest_parts[5])
    b = step(rest_parts[4], rest_parts[0])
    a = sent(0, half - 1, a)
    for distance in range(half - 2, 0, -1):
        b = sent(1, distance, b)
        a = sent(0, distance, a)
    totals = [
        part_of(0, 0, 0) + a[0].astype(jnp.float32) + b[1].astype(jnp.float32),
        part_of(1, 0, 0) + b[0].astype(jnp.float32) + a[1].astype(jnp.float32),
    ]
    total = jnp.concatenate(totals, axis=1).astype(jnp.bfloat16)
    returned = jnp.stack([total[:CAP], lax.ppermute(total[CAP:], "expert", swap)])
    combine = dispatch_map.astype(jnp.float32) * jnp.transpose(weight)[:, None, :]
    mixed = jnp.einsum("wcr,wcd->rd", combine, returned.astype(jnp.float32))
    return mixed.astype(jnp.bfloat16)


def solution(mesh):
    in_specs = (
        P(("groups", "expert", "tensor"), None),
        P(("groups", "expert", "tensor"), None),
        P(("groups", "expert", "tensor"), None),
        P("expert", None, "tensor"),
        P("expert", None, "tensor"),
        P("expert", "tensor", None),
    )
    out_specs = P(("groups", "expert", "tensor"), None)
    return jax.shard_map(
        per_device, mesh=mesh, in_specs=in_specs, out_specs=out_specs, check_vma=False
    )
```

```python
import functools
import jax
import jax.numpy as jnp
from jax import lax
from jax.experimental import pallas as pl
from jax.experimental.pallas import tpu as pltpu
from jax.sharding import PartitionSpec as P

CAP = 24
COPIES = 16
TILE = 512
MARGIN = 3 * 2**20
CHEAP = pl.CostEstimate(flops=1024, bytes_accessed=1024, transcendentals=0)


def ring_of(count):
    return list(range(0, count, 2)) + list(range(count - 1, 0, -2))


def in_vmem(array):
    return pltpu.with_memory_space_constraint(array, pltpu.VMEM)


def in_hbm(array):
    return pltpu.with_memory_space_constraint(array, pltpu.HBM)


def call(kernel, name, operands, outs, scratch, room):
    return pl.pallas_call(
        kernel,
        in_specs=[pl.BlockSpec(memory_space=memory) for _, memory in operands],
        out_specs=[pl.BlockSpec(memory_space=pltpu.VMEM)] * len(outs),
        out_shape=[pltpu.VMEM(*out) for out in outs],
        scratch_shapes=scratch,
        cost_estimate=CHEAP,
        compiler_params=pltpu.CompilerParams(vmem_limit_bytes=room + MARGIN),
        name=name,
    )(*[in_vmem(array) if memory == pltpu.VMEM else in_hbm(array) for array, memory in operands])


def row_copies(source, target, done, column=0):
    rows, width = source.shape[1] // COPIES, target.shape[2]
    return [
        pltpu.make_async_copy(
            source.at[:, pl.ds(i * rows, rows), pl.ds(column, width)], target.at[:, pl.ds(i * rows, rows)], done.at[i]
        )
        for i in range(COPIES)
    ]


def fill_kernel(source, target, done):
    copies = row_copies(source, target, done)
    for copy in copies:
        copy.start()
    for copy in copies:
        copy.wait()


def fetched(weights, width):
    operands = [(weights, pltpu.HBM)]
    outs = [((*weights.shape[:2], width), weights.dtype)]
    return call(fill_kernel, "fetched", operands, outs, [pltpu.SemaphoreType.DMA((COPIES,))], 0)[0]


def accumulate(chunks, products):
    size, width = chunks[0][0].shape
    depth = width if size * len(chunks[0]) <= 512 else TILE
    for c, blocks in enumerate(chunks):
        for at in range(0, width, depth):
            rows = jnp.concatenate([block[:, at:at + depth] for block in blocks], axis=0)
            above = c * width + at
            for weights, total in products:
                part = jnp.dot(rows, weights[0, above:above + depth, :], preferred_element_type=jnp.float32)
                total[...] = total[...] + part if above else part


def activated(gate, up):
    return (gate / (1.0 + jnp.exp(-gate)) * up).astype(jnp.bfloat16)


def gate_kernel(count, *refs):
    chunks, (weights, out) = (refs[:count], refs[count:2 * count]), refs[2 * count:]
    accumulate(chunks, [(weights, out)])


def add_down(hidden, down, outs):
    size, width = outs[0].shape
    depth = width if size * len(outs) <= 512 else TILE
    for at in range(0, width, depth):
        part = jnp.dot(hidden, down[0, :, at:at + depth], preferred_element_type=jnp.float32).astype(jnp.bfloat16)
        for b, out in enumerate(outs):
            out[:, at:at + depth] = part[b * size:(b + 1) * size]


def up_kernel(count, *refs):
    chunks, (weights, gate, out, total) = (refs[:count], refs[count:2 * count]), refs[2 * count:]
    accumulate(chunks, [(weights, total)])
    out[...] = activated(gate[...], total[...])


def rest_kernel(*refs):
    chunks, (w_gate, w_up, down_0, w_down), outs = (refs[:3], refs[3:6]), refs[6:10], refs[10:16]
    gate, up, down_1, done = refs[16:]
    copies = row_copies(w_down, down_1, done, down_1.shape[2])
    for copy in copies:
        copy.start()
    accumulate(chunks, [(w_gate, gate), (w_up, up)])
    hidden = activated(gate[...], up[...])
    add_down(hidden, down_0, outs[:3])
    for copy in copies:
        copy.wait()
    add_down(hidden, down_1, outs[3:])


def near_down_kernel(hidden, down_0, w_down, *refs):
    outs, (down_1, done) = refs[:-2], refs[-2:]
    count = len(outs) // 2
    copies = row_copies(w_down, down_1, done, down_1.shape[2])
    for copy in copies:
        copy.start()
    add_down(hidden[...], down_0, outs[:count])
    for copy in copies:
        copy.wait()
    add_down(hidden[...], down_1, outs[count:])


def routing(expert_ids, gate_probs, experts, slots):
    matches = expert_ids[:, :, None] == experts[None, None, :]
    member = jnp.any(matches, axis=1).astype(jnp.int32)
    weight = jnp.sum(jnp.where(matches, gate_probs[:, :, None], jnp.float32(0.0)), axis=1)
    slot_index = jnp.cumsum(member, axis=0) - member
    column = jnp.arange(slots)
    dispatch_map = (member[None, :, :] == 1) & (slot_index[None, :, :] == column[:, None, None])
    return (jnp.transpose(dispatch_map, (2, 0, 1)), weight)


def per_device(tokens, expert_ids, gate_probs, w_gate, w_up, w_down):
    n_tensor = lax.axis_size("tensor")
    half = n_tensor // 2
    size = 2 * CAP
    width = tokens.shape[1]
    mid_col = width // 2
    units = w_gate.shape[2]
    ring = ring_of(n_tensor)
    right = [(ring[i], ring[(i + 1) % n_tensor]) for i in range(n_tensor)]
    left = [(b, a) for a, b in right]
    swap = [(0, 1), (1, 0)]

    def step(to_right, to_left):
        pair = (lax.ppermute(to_right, "tensor", right), lax.ppermute(to_left, "tensor", left))
        return lax.optimization_barrier(pair)

    def across(rows, perm):
        pairs = [(e * n_tensor + source, (1 - e) * n_tensor + target) for e in range(2) for source, target in perm]
        return lax.ppermute(rows, ("expert", "tensor"), pairs)

    def tied(*values):
        return lax.optimization_barrier(values)

    me = lax.axis_index("expert")
    experts = jnp.stack([me, 1 - me])
    dispatch_map, weight = routing(expert_ids, gate_probs, experts, CAP)
    outgoing = jnp.dot(
        dispatch_map.astype(jnp.bfloat16).reshape(size, tokens.shape[0]),
        tokens,
        preferred_element_type=jnp.float32,
    ).astype(jnp.bfloat16)
    own = jnp.concatenate([outgoing[:CAP], lax.ppermute(outgoing[CAP:], "expert", swap)], axis=0)

    own, w_gate = tied(own, w_gate)
    halves = [own[:, :mid_col], own[:, mid_col:]]
    blocks = [[halves[0]], [halves[1]]]

    def arrived(a, b):
        blocks[0].extend([a[0], b[1]])
        blocks[1].extend([b[0], a[1]])

    a = step(halves[0], halves[1])
    b = step(halves[1], halves[0])
    gate_here = fetched(w_gate, units)
    a, gate_here = tied(a, gate_here)
    a, w_up = tied(a, w_up)
    up_here = fetched(w_up, units)
    b, up_here = tied(b, up_here)
    arrived(a, b)
    for _ in range(half - 3):
        a = step(*a)
        b = step(*b)
        arrived(a, b)
    near = [(block, pltpu.VMEM) for chunk in blocks for block in chunk]
    count = len(blocks[0])
    rows = count * size
    product = ((rows, units), jnp.float32)
    near_gate, = call(
        functools.partial(gate_kernel, count), "near_gate", near + [(gate_here, pltpu.VMEM)], [product], [],
        rows * units * 8,
    )
    b, near_gate = tied(b, near_gate)
    a = step(*a)
    b = step(*b)
    rest = [[a[0], b[1]], [b[0], a[1]]]
    a, near_gate = tied(a, near_gate)
    far = step(*a)
    near_hidden, = call(
        functools.partial(up_kernel, count), "near_up",
        near + [(up_here, pltpu.VMEM), (near_gate, pltpu.VMEM)], [((rows, units), jnp.bfloat16)],
        [pltpu.VMEM((rows, units), jnp.float32)], rows * units * 16,
    )
    near_hidden, w_down = tied(near_hidden, w_down)
    down_here = fetched(w_down, mid_col)
    rest = [rest[chunk] + [far[chunk]] for chunk in range(2)]
    rest, down_here = tied(rest, down_here)
    down_scratch = [pltpu.VMEM(down_here.shape, jnp.bfloat16), pltpu.SemaphoreType.DMA((COPIES,))]
    down_room = units * width
    rest_parts = call(
        rest_kernel, "rest",
        [(block, pltpu.VMEM) for chunk in rest for block in chunk]
        + [(gate_here, pltpu.VMEM), (up_here, pltpu.VMEM), (down_here, pltpu.VMEM), (w_down, pltpu.HBM)],
        [((size, mid_col), jnp.bfloat16)] * 6,
        [pltpu.VMEM((3 * size, units), jnp.float32)] * 2 + down_scratch,
        down_room + 3 * size * units * 16,
    )
    near_hidden, _, _ = tied(near_hidden, rest_parts[4], rest_parts[0])
    near_parts = call(
        near_down_kernel, "near_down", [(near_hidden, pltpu.VMEM), (down_here, pltpu.VMEM), (w_down, pltpu.HBM)],
        [((size, mid_col), jnp.bfloat16)] * (2 * count), down_scratch, down_room + rows * TILE * 12,
    )

    def part_of(chunk, distance, side):
        if distance == half - 1:
            return rest_parts[3 * chunk + side].astype(jnp.float32)
        index = 2 * distance - 1 + side if distance else 0
        return near_parts[count * chunk + index].astype(jnp.float32)

    def sends(stream, distance, got):
        to_right = part_of(stream, distance, 1) + got[0].astype(jnp.float32)
        to_left = part_of(1 - stream, distance, 0) + got[1].astype(jnp.float32)
        return to_right.astype(jnp.bfloat16), to_left.astype(jnp.bfloat16)

    a = step(rest_parts[2], rest_parts[5])
    b = step(rest_parts[4], rest_parts[0])
    a = step(*sends(0, half - 1, a))
    for distance in range(half - 2, 0, -1):
        b = step(*sends(1, distance, b))
        to_right, to_left = sends(0, distance, a)
        if distance > 1:
            a = step(to_right, to_left)
    kept = step(to_right[:CAP], to_left[:CAP])
    crossed = lax.optimization_barrier((across(to_right[CAP:], right), across(to_left[CAP:], left)))
    partial = jnp.concatenate(
        [part_of(0, 0, 0) + b[1].astype(jnp.float32), part_of(1, 0, 0) + b[0].astype(jnp.float32)], axis=1
    )
    exchanged = lax.ppermute(partial[CAP:].astype(jnp.bfloat16), "expert", swap)
    returned = [
        (base.astype(jnp.float32) + jnp.concatenate(last, axis=1).astype(jnp.float32)).astype(jnp.bfloat16)
        for base, last in ((partial[:CAP], kept), (exchanged, crossed))
    ]
    returned = jnp.stack(returned)
    combine = dispatch_map.astype(jnp.float32) * jnp.transpose(weight)[:, None, :]
    mixed = jnp.einsum("wcr,wcd->rd", combine, returned.astype(jnp.float32))
    return mixed.astype(jnp.bfloat16)


def solution(mesh):
    in_specs = (
        P(("groups", "expert", "tensor"), None),
        P(("groups", "expert", "tensor"), None),
        P(("groups", "expert", "tensor"), None),
        P("expert", None, "tensor"),
        P("expert", None, "tensor"),
        P("expert", "tensor", None),
    )
    out_specs = P(("groups", "expert", "tensor"), None)
    return jax.shard_map(
        per_device, mesh=mesh, in_specs=in_specs, out_specs=out_specs, check_vma=False
    )
```

```python
import functools
import jax
import jax.numpy as jnp
from jax import lax
from jax.experimental import pallas as pl
from jax.experimental.pallas import tpu as pltpu
from jax.sharding import PartitionSpec as P

CAP = 24
COPIES = 16
TILE = 512
MARGIN = 3 * 2**20
CHEAP = pl.CostEstimate(flops=1024, bytes_accessed=1024, transcendentals=0)


def ring_of(count):
    return list(range(0, count, 2)) + list(range(count - 1, 0, -2))


def in_vmem(array):
    return pltpu.with_memory_space_constraint(array, pltpu.VMEM)


def in_hbm(array):
    return pltpu.with_memory_space_constraint(array, pltpu.HBM)


def call(kernel, name, operands, outs, scratch, room):
    return pl.pallas_call(
        kernel,
        in_specs=[pl.BlockSpec(memory_space=memory) for _, memory in operands],
        out_specs=[pl.BlockSpec(memory_space=pltpu.VMEM)] * len(outs),
        out_shape=[pltpu.VMEM(*out) for out in outs],
        scratch_shapes=scratch,
        cost_estimate=CHEAP,
        compiler_params=pltpu.CompilerParams(vmem_limit_bytes=room + MARGIN),
        name=name,
    )(*[in_vmem(array) if memory == pltpu.VMEM else in_hbm(array) for array, memory in operands])


def row_copies(source, target, done, column=0):
    rows, width = source.shape[1] // COPIES, target.shape[2]
    return [
        pltpu.make_async_copy(
            source.at[:, pl.ds(i * rows, rows), pl.ds(column, width)], target.at[:, pl.ds(i * rows, rows)], done.at[i]
        )
        for i in range(COPIES)
    ]


def fill_kernel(source, target, done):
    copies = row_copies(source, target, done)
    for copy in copies:
        copy.start()
    for copy in copies:
        copy.wait()


def fetched(weights, width):
    operands = [(weights, pltpu.HBM)]
    outs = [((*weights.shape[:2], width), weights.dtype)]
    return call(fill_kernel, "fetched", operands, outs, [pltpu.SemaphoreType.DMA((COPIES,))], 0)[0]


def accumulate(chunks, products):
    size, width = chunks[0][0].shape
    depth = width if size * len(chunks[0]) <= 512 else TILE
    for c, blocks in enumerate(chunks):
        for at in range(0, width, depth):
            rows = jnp.concatenate([block[:, at:at + depth] for block in blocks], axis=0)
            above = c * width + at
            for weights, total in products:
                part = jnp.dot(rows, weights[0, above:above + depth, :], preferred_element_type=jnp.float32)
                total[...] = total[...] + part if above else part


def activated(gate, up):
    return (gate / (1.0 + jnp.exp(-gate)) * up).astype(jnp.bfloat16)


def gate_kernel(count, *refs):
    chunks, (weights, out) = (refs[:count], refs[count:2 * count]), refs[2 * count:]
    accumulate(chunks, [(weights, out)])


def add_down(hidden, down, outs):
    size, width = outs[0].shape
    depth = width if size * len(outs) <= 512 else TILE
    for at in range(0, width, depth):
        part = jnp.dot(hidden, down[0, :, at:at + depth], preferred_element_type=jnp.float32).astype(jnp.bfloat16)
        for b, out in enumerate(outs):
            out[:, at:at + depth] = part[b * size:(b + 1) * size]


def up_kernel(count, *refs):
    chunks, (weights, gate, out, total) = (refs[:count], refs[count:2 * count]), refs[2 * count:]
    accumulate(chunks, [(weights, total)])
    out[...] = activated(gate[...], total[...])


def rest_kernel(*refs):
    chunks, (w_gate, w_up, down), outs, hidden = (refs[:3], refs[3:6]), refs[6:9], refs[9:12], refs[12]
    gate, up = refs[13:]
    accumulate(chunks, [(w_gate, gate), (w_up, up)])
    hidden[...] = activated(gate[...], up[...])
    add_down(hidden[...], down, outs)


def rest_second_kernel(hidden, w_down, *refs):
    outs, down, done = refs[:3], refs[3], refs[4]
    copies = row_copies(w_down, down, done, down.shape[2])
    for copy in copies:
        copy.start()
    for copy in copies:
        copy.wait()
    add_down(hidden[...], down, outs)


def near_down_kernel(hidden, down, *outs):
    add_down(hidden[...], down, outs)


def routing(expert_ids, gate_probs, experts, slots):
    matches = expert_ids[:, :, None] == experts[None, None, :]
    member = jnp.any(matches, axis=1).astype(jnp.int32)
    weight = jnp.sum(jnp.where(matches, gate_probs[:, :, None], jnp.float32(0.0)), axis=1)
    slot_index = jnp.cumsum(member, axis=0) - member
    column = jnp.arange(slots)
    dispatch_map = (member[None, :, :] == 1) & (slot_index[None, :, :] == column[:, None, None])
    return (jnp.transpose(dispatch_map, (2, 0, 1)), weight)


def per_device(tokens, expert_ids, gate_probs, w_gate, w_up, w_down):
    n_tensor = lax.axis_size("tensor")
    half = n_tensor // 2
    size = 2 * CAP
    width = tokens.shape[1]
    mid_col = width // 2
    units = w_gate.shape[2]
    ring = ring_of(n_tensor)
    right = [(ring[i], ring[(i + 1) % n_tensor]) for i in range(n_tensor)]
    left = [(b, a) for a, b in right]
    swap = [(0, 1), (1, 0)]

    def step(to_right, to_left):
        pair = (lax.ppermute(to_right, "tensor", right), lax.ppermute(to_left, "tensor", left))
        return lax.optimization_barrier(pair)

    def tied(*values):
        return lax.optimization_barrier(values)

    me = lax.axis_index("expert")
    experts = jnp.stack([me, 1 - me])
    dispatch_map, weight = routing(expert_ids, gate_probs, experts, CAP)
    outgoing = jnp.dot(
        dispatch_map.astype(jnp.bfloat16).reshape(size, tokens.shape[0]),
        tokens,
        preferred_element_type=jnp.float32,
    ).astype(jnp.bfloat16)
    own = jnp.concatenate([outgoing[:CAP], lax.ppermute(outgoing[CAP:], "expert", swap)], axis=0)

    own, w_gate = tied(own, w_gate)
    halves = [own[:, :mid_col], own[:, mid_col:]]
    blocks = [[halves[0]], [halves[1]]]

    def arrived(a, b):
        blocks[0].extend([a[0], b[1]])
        blocks[1].extend([b[0], a[1]])

    a = step(halves[0], halves[1])
    b = step(halves[1], halves[0])
    gate_here = fetched(w_gate, units)
    a, gate_here = tied(a, gate_here)
    a, w_up = tied(a, w_up)
    up_here = fetched(w_up, units)
    b, up_here = tied(b, up_here)
    arrived(a, b)
    for _ in range(half - 3):
        a = step(*a)
        b = step(*b)
        arrived(a, b)
    near = [(block, pltpu.VMEM) for chunk in blocks for block in chunk]
    count = len(blocks[0])
    rows = count * size
    product = ((rows, units), jnp.float32)
    near_gate, = call(
        functools.partial(gate_kernel, count), "near_gate", near + [(gate_here, pltpu.VMEM)], [product], [],
        rows * units * 8,
    )
    b, near_gate = tied(b, near_gate)
    a = step(*a)
    b = step(*b)
    rest = [[a[0], b[1]], [b[0], a[1]]]
    a, near_gate = tied(a, near_gate)
    far = step(*a)
    near_hidden, = call(
        functools.partial(up_kernel, count), "near_up",
        near + [(up_here, pltpu.VMEM), (near_gate, pltpu.VMEM)], [((rows, units), jnp.bfloat16)],
        [pltpu.VMEM((rows, units), jnp.float32)], rows * units * 16,
    )
    near_hidden, w_down = tied(near_hidden, w_down)
    down_here = fetched(w_down, mid_col)
    rest = [rest[chunk] + [far[chunk]] for chunk in range(2)]
    rest, down_here = tied(rest, down_here)
    block = ((size, mid_col), jnp.bfloat16)
    *rest_0, rest_hidden = call(
        rest_kernel, "rest_first",
        [(part, pltpu.VMEM) for chunk in rest for part in chunk]
        + [(gate_here, pltpu.VMEM), (up_here, pltpu.VMEM), (down_here, pltpu.VMEM)],
        [block] * 3 + [((3 * size, units), jnp.bfloat16)],
        [pltpu.VMEM((3 * size, units), jnp.float32)] * 2,
        3 * size * units * 16,
    )
    *rest_1, down_rest = call(
        rest_second_kernel, "rest_second", [(rest_hidden, pltpu.VMEM), (w_down, pltpu.HBM)],
        [block] * 3 + [(down_here.shape, jnp.bfloat16)], [pltpu.SemaphoreType.DMA((COPIES,))], 3 * size * TILE * 12,
    )
    rest_parts = [rest_0, rest_1]

    def near_down(chunk, hidden):
        down = (down_here, down_rest)[chunk]
        return call(
            near_down_kernel, "near_down", [(hidden, pltpu.VMEM), (down, pltpu.VMEM)],
            [block] * count, [], rows * TILE * 12,
        )

    near_hidden, _, _ = tied(near_hidden, rest_1[1], rest_1[2])
    near_parts = [near_down(0, near_hidden), near_down(1, near_hidden)]

    def part_of(chunk, distance, side):
        if distance == half - 1:
            return rest_parts[chunk][side].astype(jnp.float32)
        return near_parts[chunk][2 * distance - 1 + side if distance else 0].astype(jnp.float32)

    def added(chunk, distance, side, got):
        return (part_of(chunk, distance, side) + got.astype(jnp.float32)).astype(jnp.bfloat16)

    flows = [step(rest_0[2], rest_0[0]), step(rest_1[1], rest_1[2])]
    for distance in range(half - 1, 1, -1):
        for chunk in range(2):
            to_right = added(chunk, distance - chunk, 1, flows[chunk][0])
            to_left = added(chunk, distance - 1 + chunk, 0, flows[chunk][1])
            flows[chunk] = step(to_right, to_left)
    last_right = lax.ppermute(added(0, 1, 1, flows[0][0]), "tensor", right)
    last_left = lax.ppermute(added(1, 1, 0, flows[1][1]), "tensor", left)
    totals = [
        part_of(0, 0, 0) + last_right.astype(jnp.float32) + flows[0][1].astype(jnp.float32),
        part_of(1, 0, 0) + flows[1][0].astype(jnp.float32) + last_left.astype(jnp.float32),
    ]
    total = jnp.concatenate(totals, axis=1).astype(jnp.bfloat16)
    returned = jnp.stack([total[:CAP], lax.ppermute(total[CAP:], "expert", swap)])
    combine = dispatch_map.astype(jnp.float32) * jnp.transpose(weight)[:, None, :]
    mixed = jnp.einsum("wcr,wcd->rd", combine, returned.astype(jnp.float32))
    return mixed.astype(jnp.bfloat16)


def solution(mesh):
    in_specs = (
        P(("groups", "expert", "tensor"), None),
        P(("groups", "expert", "tensor"), None),
        P(("groups", "expert", "tensor"), None),
        P("expert", None, "tensor"),
        P("expert", None, "tensor"),
        P("expert", "tensor", None),
    )
    out_specs = P(("groups", "expert", "tensor"), None)
    return jax.shard_map(
        per_device, mesh=mesh, in_specs=in_specs, out_specs=out_specs, check_vma=False
    )
```

```python
import functools
import jax
import jax.numpy as jnp
from jax import lax
from jax.experimental import pallas as pl
from jax.experimental.pallas import tpu as pltpu
from jax.sharding import PartitionSpec as P

CAP = 24
COPIES = 16
TILE = 512
MARGIN = 3 * 2**20
CHEAP = pl.CostEstimate(flops=1024, bytes_accessed=1024, transcendentals=0)


def ring_of(count):
    return list(range(0, count, 2)) + list(range(count - 1, 0, -2))


def placed(array, memory):
    return array if memory in (pltpu.SMEM, None) else pltpu.with_memory_space_constraint(array, memory)


def call(kernel, name, operands, outs, scratch, room):
    return pl.pallas_call(
        kernel,
        in_specs=[pl.BlockSpec(memory_space=memory or pltpu.VMEM) for _, memory in operands],
        out_specs=[pl.BlockSpec(memory_space=pltpu.VMEM)] * len(outs),
        out_shape=[pltpu.VMEM(*out) for out in outs],
        scratch_shapes=scratch,
        cost_estimate=CHEAP,
        compiler_params=pltpu.CompilerParams(vmem_limit_bytes=room + MARGIN),
        name=name,
    )(*[placed(array, memory) for array, memory in operands])


def row_copies(source, target, done, column=0):
    rows, width = source.shape[1] // COPIES, target.shape[2]
    return [
        pltpu.make_async_copy(
            source.at[:, pl.ds(i * rows, rows), pl.ds(column, width)], target.at[:, pl.ds(i * rows, rows)], done.at[i]
        )
        for i in range(COPIES)
    ]


def fill_kernel(source, target, done):
    copies = row_copies(source, target, done)
    for copy in copies:
        copy.start()
    for copy in copies:
        copy.wait()


def fetched(weights, width):
    operands = [(weights, pltpu.HBM)]
    outs = [((*weights.shape[:2], width), weights.dtype)]
    return call(fill_kernel, "fetched", operands, outs, [pltpu.SemaphoreType.DMA((COPIES,))], 0)[0]


def accumulate(chunks, products):
    size, width = chunks[0][0].shape
    depth = width if size * len(chunks[0]) <= 512 else TILE
    for c, blocks in enumerate(chunks):
        for at in range(0, width, depth):
            rows = jnp.concatenate([block[:, at:at + depth] for block in blocks], axis=0)
            above = c * width + at
            for weights, total in products:
                part = jnp.dot(rows, weights[0, above:above + depth, :], preferred_element_type=jnp.float32)
                total[...] = total[...] + part if above else part


def activated(gate, up):
    return (gate / (1.0 + jnp.exp(-gate)) * up).astype(jnp.bfloat16)


def gate_kernel(count, *refs):
    chunks, (weights, out) = (refs[:count], refs[count:2 * count]), refs[2 * count:]
    accumulate(chunks, [(weights, out)])


def add_down(hidden, down, outs):
    size, width = outs[0].shape
    depth = width if size * len(outs) <= 512 else TILE
    for at in range(0, width, depth):
        part = jnp.dot(hidden, down[0, :, at:at + depth], preferred_element_type=jnp.float32).astype(jnp.bfloat16)
        for b, out in enumerate(outs):
            out[:, at:at + depth] = part[b * size:(b + 1) * size]


def up_kernel(count, *refs):
    chunks, (weights, gate, out, total) = (refs[:count], refs[count:2 * count]), refs[2 * count:]
    accumulate(chunks, [(weights, total)])
    out[...] = activated(gate[...], total[...])


def rest_kernel(*refs):
    chunks, (w_gate, w_up, down), outs, hidden = (refs[:3], refs[3:6]), refs[6:9], refs[9:12], refs[12]
    gate, up = refs[13:]
    accumulate(chunks, [(w_gate, gate), (w_up, up)])
    hidden[...] = activated(gate[...], up[...])
    add_down(hidden[...], down, outs)


def rest_second_kernel(hidden, w_down, *refs):
    outs, down, done = refs[:3], refs[3], refs[4]
    copies = row_copies(w_down, down, done, down.shape[2])
    for copy in copies:
        copy.start()
    for copy in copies:
        copy.wait()
    add_down(hidden[...], down, outs)


def near_down_kernel(hidden, down, *outs):
    add_down(hidden[...], down, outs)


def dispatch_kernel(core, ids, probs, source, same, away, combine_0, combine_1, tokens, done):
    copy = pltpu.make_async_copy(source, tokens, done)
    copy.start()
    count = tokens.shape[0]
    slots = same.shape[0]
    earlier = lax.broadcasted_iota(jnp.int32, (count, count), 0) < lax.broadcasted_iota(jnp.int32, (count, count), 1)
    column = lax.broadcasted_iota(jnp.int32, (slots, count), 0)
    maps = []
    for expert, combine in ((core[0], combine_0), (1 - core[0], combine_1)):
        matches = (ids[...] == expert).astype(jnp.float32)
        member = jnp.max(matches, axis=0, keepdims=True)
        weight = jnp.sum(matches * probs[...], axis=0, keepdims=True)
        slot = jnp.dot(
            jnp.broadcast_to(member, (8, count)), earlier.astype(jnp.float32), preferred_element_type=jnp.float32
        )[:1].astype(jnp.int32)
        chosen = jnp.where(column == slot, member, 0.0)
        combine[...] = chosen * weight
        maps.append(chosen.astype(jnp.bfloat16))
    copy.wait()
    for chosen, rows in zip(maps, (same, away)):
        rows[...] = jnp.dot(chosen, tokens[...], preferred_element_type=jnp.float32).astype(jnp.bfloat16)


def per_device(tokens, expert_ids, gate_probs, w_gate, w_up, w_down):
    n_tensor = lax.axis_size("tensor")
    half = n_tensor // 2
    size = 2 * CAP
    width = tokens.shape[1]
    mid_col = width // 2
    units = w_gate.shape[2]
    ring = ring_of(n_tensor)
    right = [(ring[i], ring[(i + 1) % n_tensor]) for i in range(n_tensor)]
    left = [(b, a) for a, b in right]
    swap = [(0, 1), (1, 0)]

    def step(to_right, to_left):
        pair = (lax.ppermute(to_right, "tensor", right), lax.ppermute(to_left, "tensor", left))
        return lax.optimization_barrier(pair)

    def tied(*values):
        return lax.optimization_barrier(values)

    me = lax.axis_index("expert")
    core = jnp.reshape(me, (1,)).astype(jnp.int32)
    same, away, *combine = call(
        dispatch_kernel, "dispatch",
        [(core, pltpu.SMEM), (expert_ids.T, None), (gate_probs.T, None), (tokens, pltpu.HBM)],
        [((CAP, width), jnp.bfloat16)] * 2 + [((CAP, tokens.shape[0]), jnp.float32)] * 2,
        [pltpu.VMEM(tokens.shape, jnp.bfloat16), pltpu.SemaphoreType.DMA], 3 * 2**20,
    )
    own = jnp.concatenate([same, lax.ppermute(away, "expert", swap)], axis=0)

    own, w_gate = tied(own, w_gate)
    halves = [own[:, :mid_col], own[:, mid_col:]]
    blocks = [[halves[0]], [halves[1]]]

    def arrived(a, b):
        blocks[0].extend([a[0], b[1]])
        blocks[1].extend([b[0], a[1]])

    a = step(halves[0], halves[1])
    b = step(halves[1], halves[0])
    gate_here = fetched(w_gate, units)
    a, gate_here = tied(a, gate_here)
    a, w_up = tied(a, w_up)
    up_here = fetched(w_up, units)
    b, up_here = tied(b, up_here)
    arrived(a, b)
    for _ in range(half - 3):
        a = step(*a)
        b = step(*b)
        arrived(a, b)
    near = [(block, pltpu.VMEM) for chunk in blocks for block in chunk]
    count = len(blocks[0])
    rows = count * size
    product = ((rows, units), jnp.float32)
    near_gate, = call(
        functools.partial(gate_kernel, count), "near_gate", near + [(gate_here, pltpu.VMEM)], [product], [],
        rows * units * 8,
    )
    b, near_gate = tied(b, near_gate)
    a = step(*a)
    b = step(*b)
    rest = [[a[0], b[1]], [b[0], a[1]]]
    a, near_gate = tied(a, near_gate)
    far = step(*a)
    near_hidden, = call(
        functools.partial(up_kernel, count), "near_up",
        near + [(up_here, pltpu.VMEM), (near_gate, pltpu.VMEM)], [((rows, units), jnp.bfloat16)],
        [pltpu.VMEM((rows, units), jnp.float32)], rows * units * 16,
    )
    near_hidden, w_down = tied(near_hidden, w_down)
    down_here = fetched(w_down, mid_col)
    rest = [rest[chunk] + [far[chunk]] for chunk in range(2)]
    rest, down_here = tied(rest, down_here)
    block = ((size, mid_col), jnp.bfloat16)
    *rest_0, rest_hidden = call(
        rest_kernel, "rest_first",
        [(part, pltpu.VMEM) for chunk in rest for part in chunk]
        + [(gate_here, pltpu.VMEM), (up_here, pltpu.VMEM), (down_here, pltpu.VMEM)],
        [block] * 3 + [((3 * size, units), jnp.bfloat16)],
        [pltpu.VMEM((3 * size, units), jnp.float32)] * 2,
        3 * size * units * 16,
    )
    *rest_1, down_rest = call(
        rest_second_kernel, "rest_second", [(rest_hidden, pltpu.VMEM), (w_down, pltpu.HBM)],
        [block] * 3 + [(down_here.shape, jnp.bfloat16)], [pltpu.SemaphoreType.DMA((COPIES,))], 3 * size * TILE * 12,
    )
    rest_parts = [rest_0, rest_1]

    def near_down(chunk, hidden):
        down = (down_here, down_rest)[chunk]
        return call(
            near_down_kernel, "near_down", [(hidden, pltpu.VMEM), (down, pltpu.VMEM)],
            [block] * count, [], rows * TILE * 12,
        )

    near_hidden, _, _ = tied(near_hidden, rest_1[1], rest_1[2])
    near_parts = [near_down(0, near_hidden), near_down(1, near_hidden)]

    def part_of(chunk, distance, side):
        if distance == half - 1:
            return rest_parts[chunk][side].astype(jnp.float32)
        return near_parts[chunk][2 * distance - 1 + side if distance else 0].astype(jnp.float32)

    def added(chunk, distance, side, got):
        return (part_of(chunk, distance, side) + got.astype(jnp.float32)).astype(jnp.bfloat16)

    flows = [step(rest_0[2], rest_0[0]), step(rest_1[1], rest_1[2])]
    for distance in range(half - 1, 1, -1):
        for chunk in range(2):
            to_right = added(chunk, distance - chunk, 1, flows[chunk][0])
            to_left = added(chunk, distance - 1 + chunk, 0, flows[chunk][1])
            flows[chunk] = step(to_right, to_left)
    last_right = lax.ppermute(added(0, 1, 1, flows[0][0]), "tensor", right)
    last_left = lax.ppermute(added(1, 1, 0, flows[1][1]), "tensor", left)
    totals = [
        part_of(0, 0, 0) + last_right.astype(jnp.float32) + flows[0][1].astype(jnp.float32),
        part_of(1, 0, 0) + flows[1][0].astype(jnp.float32) + last_left.astype(jnp.float32),
    ]
    total = jnp.concatenate(totals, axis=1).astype(jnp.bfloat16)
    returned = jnp.stack([total[:CAP], lax.ppermute(total[CAP:], "expert", swap)])
    mixed = jnp.einsum("wcr,wcd->rd", jnp.stack(combine), returned.astype(jnp.float32))
    return mixed.astype(jnp.bfloat16)


def solution(mesh):
    in_specs = (
        P(("groups", "expert", "tensor"), None),
        P(("groups", "expert", "tensor"), None),
        P(("groups", "expert", "tensor"), None),
        P("expert", None, "tensor"),
        P("expert", None, "tensor"),
        P("expert", "tensor", None),
    )
    out_specs = P(("groups", "expert", "tensor"), None)
    return jax.shard_map(
        per_device, mesh=mesh, in_specs=in_specs, out_specs=out_specs, check_vma=False
    )
```

```python
import functools
import jax
import jax.numpy as jnp
from jax import lax
from jax.experimental import pallas as pl
from jax.experimental.pallas import tpu as pltpu
from jax.sharding import PartitionSpec as P

CAP = 24
COPIES = 16
TILE = 512
MARGIN = 3 * 2**20
CHEAP = pl.CostEstimate(flops=1024, bytes_accessed=1024, transcendentals=0)


def ring_of(count):
    return list(range(0, count, 2)) + list(range(count - 1, 0, -2))


def in_vmem(array):
    return pltpu.with_memory_space_constraint(array, pltpu.VMEM)


def in_hbm(array):
    return pltpu.with_memory_space_constraint(array, pltpu.HBM)


def call(kernel, name, operands, outs, scratch, room):
    return pl.pallas_call(
        kernel,
        in_specs=[pl.BlockSpec(memory_space=memory) for _, memory in operands],
        out_specs=[pl.BlockSpec(memory_space=pltpu.VMEM)] * len(outs),
        out_shape=[pltpu.VMEM(*out) for out in outs],
        scratch_shapes=scratch,
        cost_estimate=CHEAP,
        compiler_params=pltpu.CompilerParams(vmem_limit_bytes=room + MARGIN),
        name=name,
    )(*[in_vmem(array) if memory == pltpu.VMEM else in_hbm(array) for array, memory in operands])


def row_copies(source, target, done, column=0):
    rows, width = source.shape[1] // COPIES, target.shape[2]
    return [
        pltpu.make_async_copy(
            source.at[:, pl.ds(i * rows, rows), pl.ds(column, width)], target.at[:, pl.ds(i * rows, rows)], done.at[i]
        )
        for i in range(COPIES)
    ]


def fill_kernel(source, target, done):
    copies = row_copies(source, target, done)
    for copy in copies:
        copy.start()
    for copy in copies:
        copy.wait()


def fetched(weights, width):
    operands = [(weights, pltpu.HBM)]
    outs = [((*weights.shape[:2], width), weights.dtype)]
    return call(fill_kernel, "fetched", operands, outs, [pltpu.SemaphoreType.DMA((COPIES,))], 0)[0]


def accumulate(chunks, products):
    size, width = chunks[0][0].shape
    depth = width if size * len(chunks[0]) <= 512 else TILE
    for c, blocks in enumerate(chunks):
        for at in range(0, width, depth):
            rows = jnp.concatenate([block[:, at:at + depth] for block in blocks], axis=0)
            above = c * width + at
            for weights, total in products:
                part = jnp.dot(rows, weights[0, above:above + depth, :], preferred_element_type=jnp.float32)
                total[...] = total[...] + part if above else part


def activated(gate, up):
    return (gate / (1.0 + jnp.exp(-gate)) * up).astype(jnp.bfloat16)


def gate_kernel(count, *refs):
    chunks, (weights, out) = (refs[:count], refs[count:2 * count]), refs[2 * count:]
    accumulate(chunks, [(weights, out)])


def add_down(hidden, down, outs):
    size, width = outs[0].shape
    depth = width if size * len(outs) <= 512 else TILE
    for at in range(0, width, depth):
        part = jnp.dot(hidden, down[0, :, at:at + depth], preferred_element_type=jnp.float32).astype(jnp.bfloat16)
        for b, out in enumerate(outs):
            out[:, at:at + depth] = part[b * size:(b + 1) * size]


def up_kernel(count, *refs):
    chunks, (weights, gate, out, total) = (refs[:count], refs[count:2 * count]), refs[2 * count:]
    accumulate(chunks, [(weights, total)])
    out[...] = activated(gate[...], total[...])


def rest_kernel(*refs):
    chunks, (w_gate, w_up, down), outs, hidden = (refs[:3], refs[3:6]), refs[6:9], refs[9:12], refs[12]
    gate, up = refs[13:]
    accumulate(chunks, [(w_gate, gate), (w_up, up)])
    hidden[...] = activated(gate[...], up[...])
    add_down(hidden[...], down, outs)


def rest_second_kernel(hidden, w_down, *refs):
    outs, down, done = refs[:3], refs[3], refs[4]
    copies = row_copies(w_down, down, done, down.shape[2])
    for copy in copies:
        copy.start()
    for copy in copies:
        copy.wait()
    add_down(hidden[...], down, outs)


def near_down_kernel(hidden, down, *outs):
    add_down(hidden[...], down, outs)


def combine_kernel(weights, kept, swapped, *refs):
    out = refs[-1]
    part = jnp.dot(weights[0], kept[...], preferred_element_type=jnp.float32)
    part += jnp.dot(weights[1], swapped[...], preferred_element_type=jnp.float32)
    out[...] = part.astype(out.dtype)


def combined(chunk, width, weights, kept, swapped, result=None):
    rows, columns = weights.shape[1], kept.shape[1]
    operands = [weights, kept, swapped] + ([] if result is None else [result])
    in_specs = [pl.BlockSpec(memory_space=pltpu.VMEM)] * 3 + [pl.BlockSpec(memory_space=pl.ANY)] * (len(operands) - 3)
    return pl.pallas_call(
        combine_kernel,
        grid=(1,),
        in_specs=in_specs,
        out_specs=pl.BlockSpec((rows, columns), lambda i: (0, chunk)),
        out_shape=jax.ShapeDtypeStruct((rows, width), jnp.bfloat16),
        input_output_aliases={} if result is None else {3: 0},
        cost_estimate=CHEAP,
        compiler_params=pltpu.CompilerParams(vmem_limit_bytes=8 * 2**20),
        name="combined",
    )(*operands)


def routing(expert_ids, gate_probs, experts, slots):
    matches = expert_ids[:, :, None] == experts[None, None, :]
    member = jnp.any(matches, axis=1).astype(jnp.int32)
    weight = jnp.sum(jnp.where(matches, gate_probs[:, :, None], jnp.float32(0.0)), axis=1)
    slot_index = jnp.cumsum(member, axis=0) - member
    column = jnp.arange(slots)
    dispatch_map = (member[None, :, :] == 1) & (slot_index[None, :, :] == column[:, None, None])
    return (jnp.transpose(dispatch_map, (2, 0, 1)), weight)


def per_device(tokens, expert_ids, gate_probs, w_gate, w_up, w_down):
    n_tensor = lax.axis_size("tensor")
    half = n_tensor // 2
    size = 2 * CAP
    width = tokens.shape[1]
    mid_col = width // 2
    units = w_gate.shape[2]
    ring = ring_of(n_tensor)
    right = [(ring[i], ring[(i + 1) % n_tensor]) for i in range(n_tensor)]
    left = [(b, a) for a, b in right]
    swap = [(0, 1), (1, 0)]

    def step(to_right, to_left):
        pair = (lax.ppermute(to_right, "tensor", right), lax.ppermute(to_left, "tensor", left))
        return lax.optimization_barrier(pair)

    def tied(*values):
        return lax.optimization_barrier(values)

    me = lax.axis_index("expert")
    experts = jnp.stack([me, 1 - me])
    dispatch_map, weight = routing(expert_ids, gate_probs, experts, CAP)
    outgoing = jnp.dot(
        dispatch_map.astype(jnp.bfloat16).reshape(size, tokens.shape[0]),
        tokens,
        preferred_element_type=jnp.float32,
    ).astype(jnp.bfloat16)
    own = jnp.concatenate([outgoing[:CAP], lax.ppermute(outgoing[CAP:], "expert", swap)], axis=0)

    own, w_gate = tied(own, w_gate)
    halves = [own[:, :mid_col], own[:, mid_col:]]
    blocks = [[halves[0]], [halves[1]]]

    def arrived(a, b):
        blocks[0].extend([a[0], b[1]])
        blocks[1].extend([b[0], a[1]])

    a = step(halves[0], halves[1])
    b = step(halves[1], halves[0])
    gate_here = fetched(w_gate, units)
    a, gate_here = tied(a, gate_here)
    a, w_up = tied(a, w_up)
    up_here = fetched(w_up, units)
    b, up_here = tied(b, up_here)
    arrived(a, b)
    for _ in range(half - 3):
        a = step(*a)
        b = step(*b)
        arrived(a, b)
    near = [(block, pltpu.VMEM) for chunk in blocks for block in chunk]
    count = len(blocks[0])
    rows = count * size
    product = ((rows, units), jnp.float32)
    near_gate, = call(
        functools.partial(gate_kernel, count), "near_gate", near + [(gate_here, pltpu.VMEM)], [product], [],
        rows * units * 8,
    )
    b, near_gate = tied(b, near_gate)
    a = step(*a)
    b = step(*b)
    rest = [[a[0], b[1]], [b[0], a[1]]]
    a, near_gate = tied(a, near_gate)
    far = step(*a)
    near_hidden, = call(
        functools.partial(up_kernel, count), "near_up",
        near + [(up_here, pltpu.VMEM), (near_gate, pltpu.VMEM)], [((rows, units), jnp.bfloat16)],
        [pltpu.VMEM((rows, units), jnp.float32)], rows * units * 16,
    )
    near_hidden, w_down = tied(near_hidden, w_down)
    down_here = fetched(w_down, mid_col)
    rest = [rest[chunk] + [far[chunk]] for chunk in range(2)]
    rest, down_here = tied(rest, down_here)
    block = ((size, mid_col), jnp.bfloat16)
    *rest_0, rest_hidden = call(
        rest_kernel, "rest_first",
        [(part, pltpu.VMEM) for chunk in rest for part in chunk]
        + [(gate_here, pltpu.VMEM), (up_here, pltpu.VMEM), (down_here, pltpu.VMEM)],
        [block] * 3 + [((3 * size, units), jnp.bfloat16)],
        [pltpu.VMEM((3 * size, units), jnp.float32)] * 2,
        3 * size * units * 16,
    )
    *rest_1, down_rest = call(
        rest_second_kernel, "rest_second", [(rest_hidden, pltpu.VMEM), (w_down, pltpu.HBM)],
        [block] * 3 + [(down_here.shape, jnp.bfloat16)], [pltpu.SemaphoreType.DMA((COPIES,))], 3 * size * TILE * 12,
    )
    rest_parts = [rest_0, rest_1]

    def near_down(chunk, hidden):
        down = (down_here, down_rest)[chunk]
        return call(
            near_down_kernel, "near_down", [(hidden, pltpu.VMEM), (down, pltpu.VMEM)],
            [block] * count, [], rows * TILE * 12,
        )

    near_hidden, _, _ = tied(near_hidden, rest_1[1], rest_1[2])
    near_parts = [near_down(0, near_hidden), near_down(1, near_hidden)]

    def part_of(chunk, distance, side):
        if distance == half - 1:
            return rest_parts[chunk][side].astype(jnp.float32)
        return near_parts[chunk][2 * distance - 1 + side if distance else 0].astype(jnp.float32)

    def added(chunk, distance, side, got):
        return (part_of(chunk, distance, side) + got.astype(jnp.float32)).astype(jnp.bfloat16)

    flows = [step(rest_0[2], rest_0[0]), step(rest_1[1], rest_1[2])]
    for distance in range(half - 1, 1, -1):
        for chunk in range(2):
            to_right = added(chunk, distance - chunk, 1, flows[chunk][0])
            to_left = added(chunk, distance - 1 + chunk, 0, flows[chunk][1])
            flows[chunk] = step(to_right, to_left)
    last_right = lax.ppermute(added(0, 1, 1, flows[0][0]), "tensor", right)
    last_left = lax.ppermute(added(1, 1, 0, flows[1][1]), "tensor", left)
    combine = dispatch_map.astype(jnp.float32) * jnp.transpose(weight)[:, None, :]
    combine = jnp.transpose(combine, (0, 2, 1)).astype(jnp.bfloat16)
    pairs = [(last_right, flows[0][1]), (flows[1][0], last_left)]
    mixed = None
    for chunk, (from_left, from_right) in enumerate(pairs):
        if chunk:
            from_right, mixed = tied(from_right, mixed)
        total = part_of(chunk, 0, 0) + from_left.astype(jnp.float32) + from_right.astype(jnp.float32)
        total = total.astype(jnp.bfloat16)
        swapped = lax.ppermute(total[CAP:], "expert", swap)
        mixed = combined(chunk, width, combine, total[:CAP], swapped, mixed)
    return mixed


def solution(mesh):
    in_specs = (
        P(("groups", "expert", "tensor"), None),
        P(("groups", "expert", "tensor"), None),
        P(("groups", "expert", "tensor"), None),
        P("expert", None, "tensor"),
        P("expert", None, "tensor"),
        P("expert", "tensor", None),
    )
    out_specs = P(("groups", "expert", "tensor"), None)
    return jax.shard_map(
        per_device, mesh=mesh, in_specs=in_specs, out_specs=out_specs, check_vma=False
    )
```

```python
import functools
import jax
import jax.numpy as jnp
from jax import lax
from jax.experimental import pallas as pl
from jax.experimental.pallas import tpu as pltpu
from jax.sharding import PartitionSpec as P

CAP = 24
COPIES = 32
TILE = 512
MARGIN = 3 * 2**20
CHEAP = pl.CostEstimate(flops=1024, bytes_accessed=1024, transcendentals=0)


def ring_of(count):
    return list(range(0, count, 2)) + list(range(count - 1, 0, -2))


def in_vmem(array):
    return pltpu.with_memory_space_constraint(array, pltpu.VMEM)


def in_hbm(array):
    return pltpu.with_memory_space_constraint(array, pltpu.HBM)


def call(kernel, name, operands, outs, scratch, room):
    return pl.pallas_call(
        kernel,
        in_specs=[pl.BlockSpec(memory_space=memory) for _, memory in operands],
        out_specs=[pl.BlockSpec(memory_space=pltpu.VMEM)] * len(outs),
        out_shape=[pltpu.VMEM(*out) for out in outs],
        scratch_shapes=scratch,
        cost_estimate=CHEAP,
        compiler_params=pltpu.CompilerParams(vmem_limit_bytes=room + MARGIN),
        name=name,
    )(*[in_vmem(array) if memory == pltpu.VMEM else in_hbm(array) for array, memory in operands])


def row_copies(source, target, done, column=0):
    rows, width = max(16, source.shape[1] // COPIES), target.shape[2]
    return [
        pltpu.make_async_copy(
            source.at[:, pl.ds(i * rows, rows), pl.ds(column, width)], target.at[:, pl.ds(i * rows, rows)], done.at[i]
        )
        for i in range(source.shape[1] // rows)
    ]


def fill_kernel(source, target, done):
    copies = row_copies(source, target, done)
    for copy in copies:
        copy.start()
    for copy in copies:
        copy.wait()


def fetched(weights, width):
    operands = [(weights, pltpu.HBM)]
    outs = [((*weights.shape[:2], width), weights.dtype)]
    return call(fill_kernel, "fetched", operands, outs, [pltpu.SemaphoreType.DMA((COPIES,))], 0)[0]


def accumulate(chunks, products):
    size, width = chunks[0][0].shape
    depth = width if size * len(chunks[0]) <= 512 else TILE
    for c, blocks in enumerate(chunks):
        for at in range(0, width, depth):
            rows = jnp.concatenate([block[:, at:at + depth] for block in blocks], axis=0)
            above = c * width + at
            for weights, total in products:
                part = jnp.dot(rows, weights[0, above:above + depth, :], preferred_element_type=jnp.float32)
                total[...] = total[...] + part if above else part


def activated(gate, up):
    return (gate / (1.0 + jnp.exp(-gate)) * up).astype(jnp.bfloat16)


def gate_kernel(count, *refs):
    chunks, (weights, out) = (refs[:count], refs[count:2 * count]), refs[2 * count:]
    accumulate(chunks, [(weights, out)])


def add_down(hidden, down, outs):
    size, width = outs[0].shape
    depth = width if size * len(outs) <= 512 else TILE
    for at in range(0, width, depth):
        part = jnp.dot(hidden, down[0, :, at:at + depth], preferred_element_type=jnp.float32).astype(jnp.bfloat16)
        for b, out in enumerate(outs):
            out[:, at:at + depth] = part[b * size:(b + 1) * size]


def up_kernel(count, *refs):
    chunks, (weights, gate, out, total) = (refs[:count], refs[count:2 * count]), refs[2 * count:]
    accumulate(chunks, [(weights, total)])
    out[...] = activated(gate[...], total[...])


def rest_kernel(*refs):
    chunks, (w_gate, w_up, down), outs, hidden = (refs[:3], refs[3:6]), refs[6:9], refs[9:12], refs[12]
    gate, up = refs[13:]
    accumulate(chunks, [(w_gate, gate), (w_up, up)])
    hidden[...] = activated(gate[...], up[...])
    add_down(hidden[...], down, outs)


def rest_second_kernel(hidden, w_down, *refs):
    outs, down, done = refs[:3], refs[3], refs[4]
    copies = row_copies(w_down, down, done, down.shape[2])
    for copy in copies:
        copy.start()
    for copy in copies:
        copy.wait()
    add_down(hidden[...], down, outs)


def near_down_kernel(hidden, down, *outs):
    add_down(hidden[...], down, outs)


def combine_kernel(weights, kept, swapped, *refs):
    out = refs[-1]
    part = jnp.dot(weights[0], kept[...], preferred_element_type=jnp.float32)
    part += jnp.dot(weights[1], swapped[...], preferred_element_type=jnp.float32)
    out[...] = part.astype(out.dtype)


def combined(chunk, width, weights, kept, swapped, result=None):
    rows, columns = weights.shape[1], kept.shape[1]
    operands = [weights, kept, swapped] + ([] if result is None else [result])
    in_specs = [pl.BlockSpec(memory_space=pltpu.VMEM)] * 3 + [pl.BlockSpec(memory_space=pl.ANY)] * (len(operands) - 3)
    return pl.pallas_call(
        combine_kernel,
        grid=(1,),
        in_specs=in_specs,
        out_specs=pl.BlockSpec((rows, columns), lambda i: (0, chunk)),
        out_shape=jax.ShapeDtypeStruct((rows, width), jnp.bfloat16),
        input_output_aliases={} if result is None else {3: 0},
        cost_estimate=CHEAP,
        compiler_params=pltpu.CompilerParams(vmem_limit_bytes=8 * 2**20),
        name="combined",
    )(*operands)


def routing(expert_ids, gate_probs, experts, slots):
    matches = expert_ids[:, :, None] == experts[None, None, :]
    member = jnp.any(matches, axis=1).astype(jnp.int32)
    weight = jnp.sum(jnp.where(matches, gate_probs[:, :, None], jnp.float32(0.0)), axis=1)
    slot_index = jnp.cumsum(member, axis=0) - member
    column = jnp.arange(slots)
    dispatch_map = (member[None, :, :] == 1) & (slot_index[None, :, :] == column[:, None, None])
    return (jnp.transpose(dispatch_map, (2, 0, 1)), weight)


def per_device(tokens, expert_ids, gate_probs, w_gate, w_up, w_down):
    n_tensor = lax.axis_size("tensor")
    half = n_tensor // 2
    size = 2 * CAP
    width = tokens.shape[1]
    mid_col = width // 2
    units = w_gate.shape[2]
    ring = ring_of(n_tensor)
    right = [(ring[i], ring[(i + 1) % n_tensor]) for i in range(n_tensor)]
    left = [(b, a) for a, b in right]
    swap = [(0, 1), (1, 0)]

    def step(to_right, to_left):
        pair = (lax.ppermute(to_right, "tensor", right), lax.ppermute(to_left, "tensor", left))
        return lax.optimization_barrier(pair)

    def tied(*values):
        return lax.optimization_barrier(values)

    me = lax.axis_index("expert")
    experts = jnp.stack([me, 1 - me])
    dispatch_map, weight = routing(expert_ids, gate_probs, experts, CAP)
    outgoing = jnp.dot(
        dispatch_map.astype(jnp.bfloat16).reshape(size, tokens.shape[0]),
        tokens,
        preferred_element_type=jnp.float32,
    ).astype(jnp.bfloat16)
    own = jnp.concatenate([outgoing[:CAP], lax.ppermute(outgoing[CAP:], "expert", swap)], axis=0)

    own, w_gate = tied(own, w_gate)
    halves = [own[:, :mid_col], own[:, mid_col:]]
    blocks = [[halves[0]], [halves[1]]]

    def arrived(a, b):
        blocks[0].extend([a[0], b[1]])
        blocks[1].extend([b[0], a[1]])

    a = step(halves[0], halves[1])
    b = step(halves[1], halves[0])
    gate_here = fetched(w_gate, units)
    a, gate_here = tied(a, gate_here)
    a, w_up = tied(a, w_up)
    up_here = fetched(w_up, units)
    b, up_here = tied(b, up_here)
    arrived(a, b)
    for _ in range(half - 3):
        a = step(*a)
        b = step(*b)
        arrived(a, b)
    near = [(block, pltpu.VMEM) for chunk in blocks for block in chunk]
    count = len(blocks[0])
    rows = count * size
    product = ((rows, units), jnp.float32)
    near_gate, = call(
        functools.partial(gate_kernel, count), "near_gate", near + [(gate_here, pltpu.VMEM)], [product], [],
        rows * units * 8,
    )
    b, near_gate = tied(b, near_gate)
    a = step(*a)
    b = step(*b)
    rest = [[a[0], b[1]], [b[0], a[1]]]
    a, near_gate = tied(a, near_gate)
    far = step(*a)
    near_hidden, = call(
        functools.partial(up_kernel, count), "near_up",
        near + [(up_here, pltpu.VMEM), (near_gate, pltpu.VMEM)], [((rows, units), jnp.bfloat16)],
        [pltpu.VMEM((rows, units), jnp.float32)], rows * units * 16,
    )
    near_hidden, w_down = tied(near_hidden, w_down)
    down_here = fetched(w_down, mid_col)
    rest = [rest[chunk] + [far[chunk]] for chunk in range(2)]
    rest, down_here = tied(rest, down_here)
    block = ((size, mid_col), jnp.bfloat16)
    *rest_0, rest_hidden = call(
        rest_kernel, "rest_first",
        [(part, pltpu.VMEM) for chunk in rest for part in chunk]
        + [(gate_here, pltpu.VMEM), (up_here, pltpu.VMEM), (down_here, pltpu.VMEM)],
        [block] * 3 + [((3 * size, units), jnp.bfloat16)],
        [pltpu.VMEM((3 * size, units), jnp.float32)] * 2,
        3 * size * units * 16,
    )
    *rest_1, down_rest = call(
        rest_second_kernel, "rest_second", [(rest_hidden, pltpu.VMEM), (w_down, pltpu.HBM)],
        [block] * 3 + [(down_here.shape, jnp.bfloat16)], [pltpu.SemaphoreType.DMA((COPIES,))], 3 * size * TILE * 12,
    )
    rest_parts = [rest_0, rest_1]

    def near_down(chunk, hidden):
        down = (down_here, down_rest)[chunk]
        return call(
            near_down_kernel, "near_down", [(hidden, pltpu.VMEM), (down, pltpu.VMEM)],
            [block] * count, [], rows * TILE * 12,
        )

    near_hidden, _, _ = tied(near_hidden, rest_1[1], rest_1[2])
    near_parts = [near_down(0, near_hidden), near_down(1, near_hidden)]

    def part_of(chunk, distance, side):
        if distance == half - 1:
            return rest_parts[chunk][side].astype(jnp.float32)
        return near_parts[chunk][2 * distance - 1 + side if distance else 0].astype(jnp.float32)

    def added(chunk, distance, side, got):
        return (part_of(chunk, distance, side) + got.astype(jnp.float32)).astype(jnp.bfloat16)

    flows = [step(rest_0[2], rest_0[0]), step(rest_1[1], rest_1[2])]
    for distance in range(half - 1, 1, -1):
        for chunk in range(2):
            to_right = added(chunk, distance - chunk, 1, flows[chunk][0])
            to_left = added(chunk, distance - 1 + chunk, 0, flows[chunk][1])
            flows[chunk] = step(to_right, to_left)
    last_right = lax.ppermute(added(0, 1, 1, flows[0][0]), "tensor", right)
    last_left = lax.ppermute(added(1, 1, 0, flows[1][1]), "tensor", left)
    combine = dispatch_map.astype(jnp.float32) * jnp.transpose(weight)[:, None, :]
    combine = jnp.transpose(combine, (0, 2, 1)).astype(jnp.bfloat16)
    pairs = [(last_right, flows[0][1]), (flows[1][0], last_left)]
    mixed = None
    for chunk, (from_left, from_right) in enumerate(pairs):
        if chunk:
            from_right, mixed = tied(from_right, mixed)
        total = part_of(chunk, 0, 0) + from_left.astype(jnp.float32) + from_right.astype(jnp.float32)
        total = total.astype(jnp.bfloat16)
        swapped = lax.ppermute(total[CAP:], "expert", swap)
        mixed = combined(chunk, width, combine, total[:CAP], swapped, mixed)
    return mixed


def solution(mesh):
    in_specs = (
        P(("groups", "expert", "tensor"), None),
        P(("groups", "expert", "tensor"), None),
        P(("groups", "expert", "tensor"), None),
        P("expert", None, "tensor"),
        P("expert", None, "tensor"),
        P("expert", "tensor", None),
    )
    out_specs = P(("groups", "expert", "tensor"), None)
    return jax.shard_map(
        per_device, mesh=mesh, in_specs=in_specs, out_specs=out_specs, check_vma=False
    )
```

```python
import functools
import jax
import jax.numpy as jnp
from jax import lax
from jax.experimental import pallas as pl
from jax.experimental.pallas import tpu as pltpu
from jax.sharding import PartitionSpec as P

CAP = 24
COPIES = 16
TILE = 512
MARGIN = 3 * 2**20
CHEAP = pl.CostEstimate(flops=1024, bytes_accessed=1024, transcendentals=0)


def ring_of(count):
    return list(range(0, count, 2)) + list(range(count - 1, 0, -2))


def in_vmem(array):
    return pltpu.with_memory_space_constraint(array, pltpu.VMEM)


def in_hbm(array):
    return pltpu.with_memory_space_constraint(array, pltpu.HBM)


def call(kernel, name, operands, outs, scratch, room):
    return pl.pallas_call(
        kernel,
        in_specs=[pl.BlockSpec(memory_space=memory) for _, memory in operands],
        out_specs=[pl.BlockSpec(memory_space=pltpu.VMEM)] * len(outs),
        out_shape=[pltpu.VMEM(*out) for out in outs],
        scratch_shapes=scratch,
        cost_estimate=CHEAP,
        compiler_params=pltpu.CompilerParams(vmem_limit_bytes=room + MARGIN),
        name=name,
    )(*[in_vmem(array) if memory == pltpu.VMEM else in_hbm(array) for array, memory in operands])


def row_copies(source, target, done, column=0):
    rows, width = source.shape[1] // COPIES, target.shape[2]
    return [
        pltpu.make_async_copy(
            source.at[:, pl.ds(i * rows, rows), pl.ds(column, width)], target.at[:, pl.ds(i * rows, rows)], done.at[i]
        )
        for i in range(COPIES)
    ]


def fill_kernel(source, target, done):
    copies = row_copies(source, target, done)
    for copy in copies:
        copy.start()
    for copy in copies:
        copy.wait()


def fetched(weights, width):
    operands = [(weights, pltpu.HBM)]
    outs = [((*weights.shape[:2], width), weights.dtype)]
    return call(fill_kernel, "fetched", operands, outs, [pltpu.SemaphoreType.DMA((COPIES,))], 0)[0]


def accumulate(chunks, products):
    size, width = chunks[0][0].shape
    depth = width if size * len(chunks[0]) <= 512 else TILE
    for c, blocks in enumerate(chunks):
        for at in range(0, width, depth):
            rows = jnp.concatenate([block[:, at:at + depth] for block in blocks], axis=0)
            above = c * width + at
            for weights, total in products:
                part = jnp.dot(rows, weights[0, above:above + depth, :], preferred_element_type=jnp.float32)
                total[...] = total[...] + part if above else part


def activated(gate, up):
    return (gate / (1.0 + jnp.exp(-gate)) * up).astype(jnp.bfloat16)


def gate_kernel(count, *refs):
    chunks, (weights, out) = (refs[:count], refs[count:2 * count]), refs[2 * count:]
    accumulate(chunks, [(weights, out)])


def add_down(hidden, down, outs):
    size, width = outs[0].shape
    depth = width if size * len(outs) <= 512 else TILE
    for at in range(0, width, depth):
        part = jnp.dot(hidden, down[0, :, at:at + depth], preferred_element_type=jnp.float32).astype(jnp.bfloat16)
        for b, out in enumerate(outs):
            out[:, at:at + depth] = part[b * size:(b + 1) * size]


def up_kernel(count, *refs):
    chunks, (weights, gate, out, total) = (refs[:count], refs[count:2 * count]), refs[2 * count:]
    accumulate(chunks, [(weights, total)])
    out[...] = activated(gate[...], total[...])


def rest_kernel(*refs):
    chunks, (w_gate, w_up, down), outs, hidden = (refs[:3], refs[3:6]), refs[6:9], refs[9:12], refs[12]
    gate, up = refs[13:]
    accumulate(chunks, [(w_gate, gate), (w_up, up)])
    hidden[...] = activated(gate[...], up[...])
    add_down(hidden[...], down, outs)


def rest_second_kernel(hidden, w_down, *refs):
    outs, down, done = refs[:3], refs[3], refs[4]
    copies = row_copies(w_down, down, done, down.shape[2])
    for copy in copies:
        copy.start()
    for copy in copies:
        copy.wait()
    add_down(hidden[...], down, outs)


def near_down_kernel(hidden, down, *outs):
    add_down(hidden[...], down, outs)


def combine_kernel(weights, kept, swapped, *refs):
    out = refs[-1]
    part = jnp.dot(weights[0], kept[...], preferred_element_type=jnp.float32)
    part += jnp.dot(weights[1], swapped[...], preferred_element_type=jnp.float32)
    out[...] = part.astype(out.dtype)


def combined(chunk, width, weights, kept, swapped, result=None):
    rows, columns = weights.shape[1], kept.shape[1]
    operands = [weights, kept, swapped] + ([] if result is None else [result])
    in_specs = [pl.BlockSpec(memory_space=pltpu.VMEM)] * 3 + [pl.BlockSpec(memory_space=pl.ANY)] * (len(operands) - 3)
    return pl.pallas_call(
        combine_kernel,
        grid=(1,),
        in_specs=in_specs,
        out_specs=pl.BlockSpec((rows, columns), lambda i: (0, chunk)),
        out_shape=jax.ShapeDtypeStruct((rows, width), jnp.bfloat16),
        input_output_aliases={} if result is None else {3: 0},
        cost_estimate=CHEAP,
        compiler_params=pltpu.CompilerParams(vmem_limit_bytes=8 * 2**20),
        name="combined",
    )(*operands)


def routing(expert_ids, gate_probs, experts, slots):
    matches = expert_ids[:, :, None] == experts[None, None, :]
    member = jnp.any(matches, axis=1).astype(jnp.int32)
    weight = jnp.sum(jnp.where(matches, gate_probs[:, :, None], jnp.float32(0.0)), axis=1)
    slot_index = jnp.cumsum(member, axis=0) - member
    column = jnp.arange(slots)
    dispatch_map = (member[None, :, :] == 1) & (slot_index[None, :, :] == column[:, None, None])
    return (jnp.transpose(dispatch_map, (2, 0, 1)), weight)


def per_device(tokens, expert_ids, gate_probs, w_gate, w_up, w_down):
    n_tensor = lax.axis_size("tensor")
    half = n_tensor // 2
    size = 2 * CAP
    width = tokens.shape[1]
    mid_col = width // 2
    units = w_gate.shape[2]
    ring = ring_of(n_tensor)
    right = [(ring[i], ring[(i + 1) % n_tensor]) for i in range(n_tensor)]
    left = [(b, a) for a, b in right]
    swap = [(0, 1), (1, 0)]

    def step(to_right, to_left):
        pair = (lax.ppermute(to_right, "tensor", right), lax.ppermute(to_left, "tensor", left))
        return lax.optimization_barrier(pair)

    def tied(*values):
        return lax.optimization_barrier(values)

    me = lax.axis_index("expert")
    experts = jnp.stack([me, 1 - me])
    dispatch_map, weight = routing(expert_ids, gate_probs, experts, CAP)
    outgoing = jnp.dot(
        dispatch_map.astype(jnp.bfloat16).reshape(size, tokens.shape[0]),
        tokens,
        preferred_element_type=jnp.float32,
    ).astype(jnp.bfloat16)
    own = jnp.concatenate([outgoing[:CAP], lax.ppermute(outgoing[CAP:], "expert", swap)], axis=0)

    own, w_gate = tied(own, w_gate)
    halves = [own[:, :mid_col], own[:, mid_col:]]
    blocks = [[halves[0]], [halves[1]]]

    def arrived(a, b):
        blocks[0].extend([a[0], b[1]])
        blocks[1].extend([b[0], a[1]])

    a = step(halves[0], halves[1])
    b = step(halves[1], halves[0])
    gate_here = fetched(w_gate, units)
    a, gate_here = tied(a, gate_here)
    a, w_up = tied(a, w_up)
    up_here = fetched(w_up, units)
    b, up_here = tied(b, up_here)
    arrived(a, b)
    for _ in range(half - 3):
        a = step(*a)
        b = step(*b)
        arrived(a, b)
    near = [(block, pltpu.VMEM) for chunk in blocks for block in chunk]
    count = len(blocks[0])
    rows = count * size
    product = ((rows, units), jnp.float32)
    near_gate, = call(
        functools.partial(gate_kernel, count), "near_gate", near + [(gate_here, pltpu.VMEM)], [product], [],
        rows * units * 8,
    )
    b, near_gate = tied(b, near_gate)
    a = step(*a)
    b = step(*b)
    rest = [[a[0], b[1]], [b[0], a[1]]]
    a, near_gate = tied(a, near_gate)
    far = step(*a)
    near_hidden, = call(
        functools.partial(up_kernel, count), "near_up",
        near + [(up_here, pltpu.VMEM), (near_gate, pltpu.VMEM)], [((rows, units), jnp.bfloat16)],
        [pltpu.VMEM((rows, units), jnp.float32)], rows * units * 16,
    )
    near_hidden, w_down = tied(near_hidden, w_down)
    down_here = fetched(w_down, mid_col)
    rest = [rest[chunk] + [far[chunk]] for chunk in range(2)]
    rest, down_here = tied(rest, down_here)
    block = ((size, mid_col), jnp.bfloat16)
    *rest_0, rest_hidden = call(
        rest_kernel, "rest_first",
        [(part, pltpu.VMEM) for chunk in rest for part in chunk]
        + [(gate_here, pltpu.VMEM), (up_here, pltpu.VMEM), (down_here, pltpu.VMEM)],
        [block] * 3 + [((3 * size, units), jnp.bfloat16)],
        [pltpu.VMEM((3 * size, units), jnp.float32)] * 2,
        3 * size * units * 16,
    )
    *rest_1, down_rest = call(
        rest_second_kernel, "rest_second", [(rest_hidden, pltpu.VMEM), (w_down, pltpu.HBM)],
        [block] * 3 + [(down_here.shape, jnp.bfloat16)], [pltpu.SemaphoreType.DMA((COPIES,))], 3 * size * TILE * 12,
    )
    rest_parts = [rest_0, rest_1]

    def near_down(chunk, hidden):
        down = (down_here, down_rest)[chunk]
        return call(
            near_down_kernel, "near_down", [(hidden, pltpu.VMEM), (down, pltpu.VMEM)],
            [block] * count, [], rows * TILE * 12,
        )

    near_hidden, _, _ = tied(near_hidden, rest_1[1], rest_1[2])
    near_parts = [near_down(0, near_hidden), near_down(1, near_hidden)]

    def part_of(chunk, distance, side):
        if distance == half - 1:
            return rest_parts[chunk][side].astype(jnp.float32)
        return near_parts[chunk][2 * distance - 1 + side if distance else 0].astype(jnp.float32)

    def added(chunk, distance, side, got):
        return (part_of(chunk, distance, side) + got.astype(jnp.float32)).astype(jnp.bfloat16)

    second_left = lax.optimization_barrier(lax.ppermute(rest_1[2], "tensor", left))
    second_right = lax.optimization_barrier(lax.ppermute(rest_1[1], "tensor", right))
    flows = [step(rest_0[2], rest_0[0]), (second_right, second_left)]
    for distance in range(half - 1, 1, -1):
        for chunk in range(2):
            to_right = added(chunk, distance - chunk, 1, flows[chunk][0])
            to_left = added(chunk, distance - 1 + chunk, 0, flows[chunk][1])
            flows[chunk] = step(to_right, to_left)
    last_right = lax.ppermute(added(0, 1, 1, flows[0][0]), "tensor", right)
    last_left = lax.ppermute(added(1, 1, 0, flows[1][1]), "tensor", left)
    combine = dispatch_map.astype(jnp.float32) * jnp.transpose(weight)[:, None, :]
    combine = jnp.transpose(combine, (0, 2, 1)).astype(jnp.bfloat16)
    pairs = [(last_right, flows[0][1]), (flows[1][0], last_left)]
    mixed = None
    for chunk, (from_left, from_right) in enumerate(pairs):
        if chunk:
            from_right, mixed = tied(from_right, mixed)
        total = part_of(chunk, 0, 0) + from_left.astype(jnp.float32) + from_right.astype(jnp.float32)
        total = total.astype(jnp.bfloat16)
        swapped = lax.ppermute(total[CAP:], "expert", swap)
        mixed = combined(chunk, width, combine, total[:CAP], swapped, mixed)
    return mixed


def solution(mesh):
    in_specs = (
        P(("groups", "expert", "tensor"), None),
        P(("groups", "expert", "tensor"), None),
        P(("groups", "expert", "tensor"), None),
        P("expert", None, "tensor"),
        P("expert", None, "tensor"),
        P("expert", "tensor", None),
    )
    out_specs = P(("groups", "expert", "tensor"), None)
    return jax.shard_map(
        per_device, mesh=mesh, in_specs=in_specs, out_specs=out_specs, check_vma=False
    )
```

```python
import functools
import jax
import jax.numpy as jnp
from jax import lax
from jax.experimental import pallas as pl
from jax.experimental.pallas import tpu as pltpu
from jax.sharding import PartitionSpec as P

CAP = 24
COPIES = 16
TILE = 512
MARGIN = 3 * 2**20
CHEAP = pl.CostEstimate(flops=1024, bytes_accessed=1024, transcendentals=0)


def ring_of(count):
    return list(range(0, count, 2)) + list(range(count - 1, 0, -2))


def in_vmem(array):
    return pltpu.with_memory_space_constraint(array, pltpu.VMEM)


def in_hbm(array):
    return pltpu.with_memory_space_constraint(array, pltpu.HBM)


def call(kernel, name, operands, outs, scratch, room):
    return pl.pallas_call(
        kernel,
        in_specs=[pl.BlockSpec(memory_space=memory) for _, memory in operands],
        out_specs=[pl.BlockSpec(memory_space=pltpu.VMEM)] * len(outs),
        out_shape=[pltpu.VMEM(*out) for out in outs],
        scratch_shapes=scratch,
        cost_estimate=CHEAP,
        compiler_params=pltpu.CompilerParams(vmem_limit_bytes=room + MARGIN),
        name=name,
    )(*[in_vmem(array) if memory == pltpu.VMEM else in_hbm(array) for array, memory in operands])


def row_copies(source, target, done, column=0):
    rows, width = source.shape[1] // COPIES, target.shape[2]
    return [
        pltpu.make_async_copy(
            source.at[:, pl.ds(i * rows, rows), pl.ds(column, width)], target.at[:, pl.ds(i * rows, rows)], done.at[i]
        )
        for i in range(COPIES)
    ]


def fill_kernel(source, target, done):
    copies = row_copies(source, target, done)
    for copy in copies:
        copy.start()
    for copy in copies:
        copy.wait()


def fetched(weights, width):
    operands = [(weights, pltpu.HBM)]
    outs = [((*weights.shape[:2], width), weights.dtype)]
    return call(fill_kernel, "fetched", operands, outs, [pltpu.SemaphoreType.DMA((COPIES,))], 0)[0]


def accumulate(chunks, products):
    size, width = chunks[0][0].shape
    depth = width if size * len(chunks[0]) <= 512 else TILE
    for c, blocks in enumerate(chunks):
        for at in range(0, width, depth):
            rows = jnp.concatenate([block[:, at:at + depth] for block in blocks], axis=0)
            above = c * width + at
            for weights, total in products:
                part = jnp.dot(rows, weights[0, above:above + depth, :], preferred_element_type=jnp.float32)
                total[...] = total[...] + part if above else part


def activated(gate, up):
    return (gate / (1.0 + jnp.exp(-gate)) * up).astype(jnp.bfloat16)


def gate_kernel(count, *refs):
    chunks, (weights, out) = (refs[:count], refs[count:2 * count]), refs[2 * count:]
    accumulate(chunks, [(weights, out)])


def add_down(hidden, down, outs):
    size, width = outs[0].shape
    depth = width if size * len(outs) <= 512 else TILE
    for at in range(0, width, depth):
        part = jnp.dot(hidden, down[0, :, at:at + depth], preferred_element_type=jnp.float32).astype(jnp.bfloat16)
        for b, out in enumerate(outs):
            out[:, at:at + depth] = part[b * size:(b + 1) * size]


def up_kernel(count, *refs):
    chunks, (weights, gate, out, total) = (refs[:count], refs[count:2 * count]), refs[2 * count:]
    accumulate(chunks, [(weights, total)])
    out[...] = activated(gate[...], total[...])


def rest_kernel(*refs):
    chunks, (w_gate, w_up, down), outs, hidden = (refs[:3], refs[3:6]), refs[6:9], refs[9:12], refs[12]
    gate, up = refs[13:]
    accumulate(chunks, [(w_gate, gate), (w_up, up)])
    hidden[...] = activated(gate[...], up[...])
    add_down(hidden[...], down, outs)


def rest_second_kernel(hidden, w_down, *refs):
    outs, down, done = refs[:3], refs[3], refs[4]
    copies = row_copies(w_down, down, done, down.shape[2])
    for copy in copies:
        copy.start()
    for copy in copies:
        copy.wait()
    add_down(hidden[...], down, outs)


def near_down_kernel(hidden, down, *outs):
    add_down(hidden[...], down, outs)


def combine_kernel(weights, kept, swapped, *refs):
    out = refs[-1]
    part = jnp.dot(weights[0], kept[...], preferred_element_type=jnp.float32)
    part += jnp.dot(weights[1], swapped[...], preferred_element_type=jnp.float32)
    out[...] = part.astype(out.dtype)


def combined(chunk, width, weights, kept, swapped, result=None):
    rows, columns = weights.shape[1], kept.shape[1]
    operands = [weights, kept, swapped] + ([] if result is None else [result])
    in_specs = [pl.BlockSpec(memory_space=pltpu.VMEM)] * 3 + [pl.BlockSpec(memory_space=pl.ANY)] * (len(operands) - 3)
    return pl.pallas_call(
        combine_kernel,
        grid=(1,),
        in_specs=in_specs,
        out_specs=pl.BlockSpec((rows, columns), lambda i: (0, chunk)),
        out_shape=jax.ShapeDtypeStruct((rows, width), jnp.bfloat16),
        input_output_aliases={} if result is None else {3: 0},
        cost_estimate=CHEAP,
        compiler_params=pltpu.CompilerParams(vmem_limit_bytes=8 * 2**20),
        name="combined",
    )(*operands)


def routing(expert_ids, gate_probs, experts, slots):
    matches = expert_ids[:, :, None] == experts[None, None, :]
    member = jnp.any(matches, axis=1).astype(jnp.int32)
    weight = jnp.sum(jnp.where(matches, gate_probs[:, :, None], jnp.float32(0.0)), axis=1)
    slot_index = jnp.cumsum(member, axis=0) - member
    column = jnp.arange(slots)
    dispatch_map = (member[None, :, :] == 1) & (slot_index[None, :, :] == column[:, None, None])
    return (jnp.transpose(dispatch_map, (2, 0, 1)), weight)


def per_device(tokens, expert_ids, gate_probs, w_gate, w_up, w_down):
    n_tensor = lax.axis_size("tensor")
    half = n_tensor // 2
    size = 2 * CAP
    width = tokens.shape[1]
    mid_col = width // 2
    units = w_gate.shape[2]
    ring = ring_of(n_tensor)
    right = [(ring[i], ring[(i + 1) % n_tensor]) for i in range(n_tensor)]
    left = [(b, a) for a, b in right]
    swap = [(0, 1), (1, 0)]

    def step(to_right, to_left):
        pair = (lax.ppermute(to_right, "tensor", right), lax.ppermute(to_left, "tensor", left))
        return lax.optimization_barrier(pair)

    def tied(*values):
        return lax.optimization_barrier(values)

    me = lax.axis_index("expert")
    experts = jnp.stack([me, 1 - me])
    dispatch_map, weight = routing(expert_ids, gate_probs, experts, CAP)
    outgoing = jnp.dot(
        dispatch_map.astype(jnp.bfloat16).reshape(size, tokens.shape[0]),
        tokens,
        preferred_element_type=jnp.float32,
    ).astype(jnp.bfloat16)
    own = jnp.concatenate([outgoing[:CAP], lax.ppermute(outgoing[CAP:], "expert", swap)], axis=0)

    own, w_gate = tied(own, w_gate)
    halves = [own[:, :mid_col], own[:, mid_col:]]
    blocks = [[halves[0]], [halves[1]]]

    def arrived(a, b):
        blocks[0].extend([a[0], b[1]])
        blocks[1].extend([b[0], a[1]])

    a = step(halves[0], halves[1])
    b = step(halves[1], halves[0])
    gate_here = fetched(w_gate, units)
    a, gate_here = tied(a, gate_here)
    a, w_up = tied(a, w_up)
    up_here = fetched(w_up, units)
    b, up_here = tied(b, up_here)
    arrived(a, b)
    for _ in range(half - 3):
        a = step(*a)
        b = step(*b)
        arrived(a, b)
    near = [(block, pltpu.VMEM) for chunk in blocks for block in chunk]
    count = len(blocks[0])
    rows = count * size
    product = ((rows, units), jnp.float32)
    near_gate, = call(
        functools.partial(gate_kernel, count), "near_gate", near + [(gate_here, pltpu.VMEM)], [product], [],
        rows * units * 8,
    )
    b, near_gate = tied(b, near_gate)
    a = step(*a)
    b = step(*b)
    rest = [[a[0], b[1]], [b[0], a[1]]]
    a, near_gate = tied(a, near_gate)
    far = step(*a)
    near_hidden, = call(
        functools.partial(up_kernel, count), "near_up",
        near + [(up_here, pltpu.VMEM), (near_gate, pltpu.VMEM)], [((rows, units), jnp.bfloat16)],
        [pltpu.VMEM((rows, units), jnp.float32)], rows * units * 16,
    )
    near_hidden, w_down = tied(near_hidden, w_down)
    down_here = fetched(w_down, mid_col)
    rest = [rest[chunk] + [far[chunk]] for chunk in range(2)]
    rest, down_here = tied(rest, down_here)
    block = ((size, mid_col), jnp.bfloat16)
    *rest_0, rest_hidden = call(
        rest_kernel, "rest_first",
        [(part, pltpu.VMEM) for chunk in rest for part in chunk]
        + [(gate_here, pltpu.VMEM), (up_here, pltpu.VMEM), (down_here, pltpu.VMEM)],
        [block] * 3 + [((3 * size, units), jnp.bfloat16)],
        [pltpu.VMEM((3 * size, units), jnp.float32)] * 2,
        3 * size * units * 16,
    )
    *rest_1, down_rest = call(
        rest_second_kernel, "rest_second", [(rest_hidden, pltpu.VMEM), (w_down, pltpu.HBM)],
        [block] * 3 + [(down_here.shape, jnp.bfloat16)], [pltpu.SemaphoreType.DMA((COPIES,))], 3 * size * TILE * 12,
    )
    rest_parts = [rest_0, rest_1]

    def near_down(chunk, hidden):
        down = (down_here, down_rest)[chunk]
        return call(
            near_down_kernel, "near_down", [(hidden, pltpu.VMEM), (down, pltpu.VMEM)],
            [block] * count, [], rows * TILE * 12,
        )

    near_hidden, _, _ = tied(near_hidden, rest_1[1], rest_1[2])
    near_parts = [near_down(0, near_hidden)]

    def part_of(chunk, distance, side):
        if distance == half - 1:
            return rest_parts[chunk][side].astype(jnp.float32)
        return near_parts[chunk][2 * distance - 1 + side if distance else 0].astype(jnp.float32)

    def added(chunk, distance, side, got):
        return (part_of(chunk, distance, side) + got.astype(jnp.float32)).astype(jnp.bfloat16)

    second_left = lax.optimization_barrier(lax.ppermute(rest_1[2], "tensor", left))
    second_right = lax.optimization_barrier(lax.ppermute(rest_1[1], "tensor", right))
    flows = [step(rest_0[2], rest_0[0]), (second_right, second_left)]
    for distance in range(half - 1, 1, -1):
        for chunk in range(2):
            to_right = added(chunk, distance - chunk, 1, flows[chunk][0])
            to_left = added(chunk, distance - 1 + chunk, 0, flows[chunk][1])
            if len(near_parts) == 1:
                near_hidden, _, _ = tied(near_hidden, to_right, to_left)
                near_parts.append(near_down(1, near_hidden))
            flows[chunk] = step(to_right, to_left)
    last_right = lax.ppermute(added(0, 1, 1, flows[0][0]), "tensor", right)
    last_left = lax.ppermute(added(1, 1, 0, flows[1][1]), "tensor", left)
    combine = dispatch_map.astype(jnp.float32) * jnp.transpose(weight)[:, None, :]
    combine = jnp.transpose(combine, (0, 2, 1)).astype(jnp.bfloat16)
    pairs = [(last_right, flows[0][1]), (flows[1][0], last_left)]
    mixed = None
    for chunk, (from_left, from_right) in enumerate(pairs):
        if chunk:
            from_right, mixed = tied(from_right, mixed)
        total = part_of(chunk, 0, 0) + from_left.astype(jnp.float32) + from_right.astype(jnp.float32)
        total = total.astype(jnp.bfloat16)
        swapped = lax.ppermute(total[CAP:], "expert", swap)
        mixed = combined(chunk, width, combine, total[:CAP], swapped, mixed)
    return mixed


def solution(mesh):
    in_specs = (
        P(("groups", "expert", "tensor"), None),
        P(("groups", "expert", "tensor"), None),
        P(("groups", "expert", "tensor"), None),
        P("expert", None, "tensor"),
        P("expert", None, "tensor"),
        P("expert", "tensor", None),
    )
    out_specs = P(("groups", "expert", "tensor"), None)
    return jax.shard_map(
        per_device, mesh=mesh, in_specs=in_specs, out_specs=out_specs, check_vma=False
    )
```
